32 devices in a mesh: gx: 8 (over z, x), gy: 4 (over y, core).
Axes of the slice: x: 2, y: 2, z: 4, core: 2. Of those that a mesh axis runs over, the one named last changes fastest.
Arguments:
- velocity: float32 [3, 8, 256, 512], P(None, None, 'gx', 'gy'), may hold values from -6 to 6
- stress: float32 [6, 8, 256, 512], P(None, None, 'gx', 'gy'), may hold values from -6 to 6
- zones: int32 [8, 256, 512], P(None, 'gx', 'gy'), may hold values from 0 to 15
- zone_table: float32 [3, 16], replicated, may hold values from 0.5 to 2
- regional: float32 [8, 2, 3, 8, 1024], P('gx', None, None, None, 'gy'), may hold values from -6 to 6
- owner: int32 [4], replicated, may hold values from 0 to 7
- footprint_building: int32 [8, 4, 64], P('gx', 'gy'), may hold values from 0 to 1023
- footprint_block: int32 [8, 4, 64], P('gx', 'gy'), may hold values from 0 to 63
Outputs:
- velocity_out: float32 [3, 8, 256, 512], P(None, None, 'gx', 'gy')
- stress_out: float32 [6, 8, 256, 512], P(None, None, 'gx', 'gy')
- base_shear: float32 [2, 1024], replicated
The draws below stay inside these ranges and needn't reach their ends.
All inputs are finite; a program needn't handle non-finite values.
Results may differ from the reference program's by a relative error of at most 0.000084.
Values sent between devices are 32-bit elements; how exact they have to be, the bound alone decides.
No kernel may reach another device: no remote copies, remote signals or barrier semaphores. Data moves between devices by JAX's collectives and lax.ppermute only.
A program may use at most 64 MiB of HBM per device.

```python
import jax
import jax.numpy as jnp

CX = 32
CY = 128
NZ = 8
STEPS = 2
COARSE = 4
BLOCK = 8
ZONES = 16
BUILDINGS = 1024
FP_DEV = 64
NX = 256
NY = 512
CXC = 8
CYC = 32
BLOCKS_DEV = 64
N_GX = 8
N_GY = 4


def draw_owner(key, part):
    first = jax.random.fold_in(key, 11)
    second = jax.random.fold_in(key, 23)
    values = jax.random.randint(first, (N_GY,), 0, N_GX)
    where = jax.random.randint(second, (), 0, N_GY)
    return values.at[where].set(N_GX - 1).astype(jnp.int32)


def set_ends(entries, stream_key, least, high):
    longest = entries.shape.index(max(entries.shape))
    spots = []
    for shift in (0, 1):
        where = [jax.random.randint(jax.random.fold_in(stream_key, axis), (), 0, length) for axis, length in enumerate(entries.shape)]
        where[longest] = (where[longest] + shift) % entries.shape[longest]
        spots.append(tuple(where))
    return entries.at[spots[0]].set(least).at[spots[1]].set(high)


def block_levels(key, extent, split, least, high):
    loudness = 1.0
    for dim, parts in split:
        steps = jax.random.uniform(jax.random.fold_in(jax.random.fold_in(key, 6), dim), (parts,), jnp.float32, least / len(split), high / len(split))
        loudness = loudness * jnp.repeat(jnp.exp(steps), extent[dim] // parts).reshape((-1,) + (1,) * (len(extent) - 1 - dim))
    return loudness


def bell_draw(rng, dims, width, limit, cuts=(), held_as=jnp.bfloat16):
    gain = block_levels(rng, dims, cuts, -0.22, 0.18) if cuts else 1.0
    array = jax.random.normal(rng, dims, jnp.float32) * width * gain
    return jnp.minimum(jnp.maximum(array, -limit), limit).astype(held_as)


def setup_inputs(seed: int = 0) -> dict:
    splits = jax.random.split(jax.random.key(seed), 9)
    return {
        "velocity": bell_draw(splits[0], (3, NZ, NX, NY), 1.0, 6.0, ((2, 8), (3, 4)), jnp.float32),
        "stress": bell_draw(splits[1], (6, NZ, NX, NY), 1.0, 6.0, ((2, 8), (3, 4)), jnp.float32),
        "zones": set_ends(jax.random.randint(splits[2], (NZ, NX, NY), 0, ZONES), jax.random.fold_in(splits[2], 1), 0, ZONES - 1).astype(jnp.int32),
        "zone_table": jnp.clip(jax.random.uniform(splits[3], (3, ZONES), jnp.float32, 0.5, 2.0), 0.5, 2.0),
        "regional": bell_draw(splits[4], (N_GX, STEPS, 3, N_GX, N_GY * CXC * CYC), 1.0, 6.0, ((0, 8), (4, 4)), jnp.float32),
        "owner": draw_owner(jax.random.fold_in(splits[8], 71), 0),
        "footprint_building": set_ends(jax.random.randint(splits[6], (N_GX, N_GY, FP_DEV), 0, BUILDINGS), jax.random.fold_in(splits[6], 1), 0, BUILDINGS - 1).astype(jnp.int32),
        "footprint_block": set_ends(jax.random.randint(splits[7], (N_GX, N_GY, FP_DEV), 0, BLOCKS_DEV), jax.random.fold_in(splits[7], 1), 0, BLOCKS_DEV - 1).astype(jnp.int32),
    }


def diff_x(field):
    return (jnp.roll(field, -1, axis=1) - jnp.roll(field, 1, axis=1)) * 0.5


def diff_y(field):
    return (jnp.roll(field, -1, axis=2) - jnp.roll(field, 1, axis=2)) * 0.5


def diff_z(field):
    padded = jnp.pad(field, ((1, 1), (0, 0), (0, 0)))
    return (padded[2:] - padded[:-2]) * 0.5


def reference(velocity, stress, zones, zone_table, regional, owner, footprint_building, footprint_block):
    lam = zone_table[0][zones]
    shear_mod = zone_table[1][zones]
    buoy = zone_table[2][zones]
    shaped = regional.reshape(N_GX, STEPS, 3, N_GX, N_GY, CXC, CYC)
    shaped = jnp.moveaxis(shaped, 4, 0)
    picked = shaped[jnp.arange(N_GY), owner.astype(jnp.int32)]
    picked = jnp.transpose(picked, (1, 2, 3, 4, 0, 5)).reshape(STEPS, 3, N_GX * CXC, N_GY * CYC)
    drm = jnp.repeat(jnp.repeat(picked, COARSE, axis=2), COARSE, axis=3)
    for step in range(STEPS):
        sxx, sxz, sxy, syy, syz, szz = stress[0], stress[1], stress[2], stress[3], stress[4], stress[5]
        force_x = diff_x(sxx) + diff_y(sxy) + diff_z(sxz)
        force_y = diff_x(sxy) + diff_y(syy) + diff_z(syz)
        force_z = diff_x(sxz) + diff_y(syz) + diff_z(szz)
        force = jnp.stack([force_x, force_y, force_z])
        force = force.at[:, NZ - 1].add(shear_mod[NZ - 1][None] * drm[step])
        velocity = velocity + 0.2 * buoy[None] * force
        vx, vy, vz = velocity[0], velocity[1], velocity[2]
        dvx_dx = diff_x(vx)
        dvy_dy = diff_y(vy)
        dvz_dz = diff_z(vz)
        theta = dvx_dx + dvy_dy + dvz_dz
        new_xx = sxx + 0.2 * (lam * theta + 2.0 * shear_mod * dvx_dx)
        new_xz = sxz + 0.2 * shear_mod * (diff_z(vx) + diff_x(vz))
        new_xy = sxy + 0.2 * shear_mod * (diff_y(vx) + diff_x(vy))
        new_yy = syy + 0.2 * (lam * theta + 2.0 * shear_mod * dvy_dy)
        new_yz = syz + 0.2 * shear_mod * (diff_z(vy) + diff_y(vz))
        new_zz = szz + 0.2 * (lam * theta + 2.0 * shear_mod * dvz_dz)
        stress = jnp.stack([new_xx, new_xz, new_xy, new_yy, new_yz, new_zz])
    plane = jnp.stack([stress[1, 1], stress[4, 1]])
    plane = plane.reshape(2, N_GX, CX // BLOCK, BLOCK, N_GY, CY // BLOCK, BLOCK)
    means = jnp.sum(plane, axis=(3, 6)) * (1.0 / (BLOCK * BLOCK))
    means = jnp.transpose(means, (0, 1, 3, 2, 4)).reshape(2, N_GX, N_GY, BLOCKS_DEV)
    rows = jnp.arange(N_GX)[:, None, None]
    cols = jnp.arange(N_GY)[None, :, None]
    values = means[:, rows, cols, footprint_block.astype(jnp.int32)]
    shear = jnp.zeros((2, BUILDINGS), jnp.float32)
    shear = shear.at[:, footprint_building.reshape(-1)].add(values.reshape(2, -1))
    return velocity, stress, shear
```

```python
import functools

import jax
import jax.numpy as jnp
from jax import lax
from jax.experimental import pallas as pl
from jax.experimental.pallas import tpu as pltpu
from jax.sharding import PartitionSpec as P

CX = 32
CY = 128
NZ = 8
STEPS = 2
COARSE = 4
BLOCK = 8
ZONES = 16
BUILDINGS = 1024
FP_DEV = 64
HALO = 4
RING = CX + 2 * HALO
FIELDS = 10
PACKS = 3
CHUNK = 16
CXC = CX // COARSE
CYC = CY // COARSE
F32 = jnp.float32
VMEM_LIMIT = 32 * 1024 * 1024


def iota(shape, dim):
    return lax.broadcasted_iota(jnp.int32, shape, dim)


def take(x, idx):
    idx = jnp.broadcast_to(idx, x.shape)
    return jnp.take_along_axis(x, idx, axis=1, mode="promise_in_bounds")


def roll(x, shift, axis):
    size = x.shape[axis]
    shift = shift % size
    return x if shift == 0 else pltpu.roll(x, shift, axis)


def pack_kernel(n_gx, n_gy, vel, stress, zones, regional, gxa, gxb, gya, gyb, mesh_out):
    gx = lax.axis_index("gx")
    gy = lax.axis_index("gy")
    even_x = (gx & 1) == 0
    even_y = (gy & 1) == 0
    slot = iota((CX, CY), 1) // HALO
    low = iota((8, CY), 0) < 4
    lane8 = iota((8, CY), 1)

    def plane(f, z, a, b):
        if f < 6:
            return stress[f, z, a:b, :]
        if f < 9:
            return vel[f - 6, z, a:b, :]
        return zones[z, a:b, :].astype(F32)

    last_cols, first_cols = [], []
    for p in range(PACKS):
        lasts = jnp.zeros((CX, CY), F32)
        firsts = jnp.zeros((CX, CY), F32)
        for s in range(4):
            f = 4 * p + s
            if f >= FIELDS:
                continue
            for z in range(NZ):
                turned = roll(plane(f, z, 0, CX), 16 * z + 4 * s + 4, 1)
                at = 4 * z + s
                lasts = jnp.where(slot == at, turned, lasts)
                firsts = jnp.where(slot == (at + 1) % 32, turned, firsts)
        last_cols.append(lasts)
        first_cols.append(firsts)
        gya[p] = jnp.where(even_y, lasts, firsts)
        gyb[p] = jnp.where(even_y, firsts, lasts)

    for f in range(FIELDS):
        for q in range(NZ // 2):
            first = jnp.where(low, plane(f, 2 * q, 0, 8), roll(plane(f, 2 * q + 1, 0, 8), 4, 0))
            last = jnp.where(low, roll(plane(f, 2 * q + 1, CX - 8, CX), 4, 0), plane(f, 2 * q, CX - 8, CX))
            gxa[f * 4 + q] = jnp.where(even_x, last, first)
            gxb[f * 4 + q] = jnp.where(even_x, first, last)

    lane_g = iota((n_gx, CY), 1)
    part = lane_g // CYC
    digit = lane_g % 10
    group = lane_g // 10
    e_last = jnp.zeros((n_gx, CY), F32)
    e_first = jnp.zeros((n_gx, CY), F32)
    for s in range(STEPS):
        halves = [[regional[0, s, c, :, t * CY:(t + 1) * CY] for t in range(2)] for c in range(3)]
        nexts = [roll(halves[c][0], n_gx - 1, 0) for c in range(3)]
        befores = [roll(halves[c][1], 1, 0) for c in range(3)]
        for r in range(CXC):
            row = jnp.zeros((n_gx, CY), F32)
            for c in range(3):
                row = jnp.where(part == c, roll(halves[c][r // 4], CYC * (c - r % 4), 1), row)
            if r < 3:
                row = jnp.where(part == 3, roll(nexts[r], 96, 1), row)
            elif r < 6:
                row = jnp.where(part == 3, befores[r - 3], row)
            mesh_out[pl.ds(gy * CHUNK + s * CXC + r, n_gx, stride=n_gy * CHUNK), :] = row
        for c in range(3):
            here = group == s * 3 + c
            for is_last in (True, False):
                col = CYC - 1 if is_last else 0
                idx_low = jnp.where(digit < 4, digit * CYC + col, 0)
                idx_high = jnp.where((digit >= 4) & (digit < 8), (digit - 4) * CYC + col, 0)
                edge = jnp.where(digit < 4, take(halves[c][0], idx_low), take(halves[c][1], idx_high))
                edge = jnp.where(digit == 8, take(nexts[c], jnp.full_like(digit, col)), edge)
                edge = jnp.where(digit == 9, take(befores[c], jnp.full_like(digit, 3 * CYC + col)), edge)
                if is_last:
                    e_last = jnp.where(here, edge, e_last)
                else:
                    e_first = jnp.where(here, edge, e_first)
    right = (gy + 1) % n_gy
    left = (gy + n_gy - 1) % n_gy
    for i in range(n_gx):
        for edges, to in ((e_last, right), (e_first, left)):
            at = pl.multiple_of((i * n_gy + to) * CHUNK + 8, 8)
            mesh_out[pl.ds(at, 8), :] = jnp.broadcast_to(edges[i:i + 1, :], (8, CY))

    for step_x, rows, natural in ((1, slice(CX - 8, CX), ~low), (n_gx - 1, slice(0, 8), low)):
        to_x = (gx + step_x) % n_gx
        for cols, to_y in ((last_cols, right), (first_cols, left)):
            at = pl.multiple_of((to_x * n_gy + to_y) * CHUNK, CHUNK)
            mesh_out[pl.ds(at, 8), :] = jnp.where(natural, cols[0][rows, :], roll(cols[1][rows, :], 4, 0))
            at = pl.multiple_of(at + 8, 8)
            mesh_out[pl.ds(at, 8), :] = jnp.where(natural, cols[2][rows, :], mesh_out[pl.ds(at, 8), :])


def step_kernel(
    n_gx, n_gy,
    vel, stress, zones, table, own_a, own_b, ra, rb, ca, cb, mesh_in, owner, building, block,
    vel_out, stress_out, shares,
    S, V, Z, LAM, MU, BUOY, BF, BM, DRM, sems, out_sems,
):
    gx = lax.axis_index("gx")
    gy = lax.axis_index("gy")
    even_x = (gx & 1) == 0
    even_y = (gy & 1) == 0
    loads = [
        pltpu.make_async_copy(stress, S.at[:, :, pl.ds(0, CX), :], sems.at[0]),
        pltpu.make_async_copy(vel, V.at[:, :, pl.ds(0, CX), :], sems.at[1]),
        pltpu.make_async_copy(zones, Z.at[:, pl.ds(0, CX), :], sems.at[2]),
    ]
    for copy in loads:
        copy.start()
    low = iota((8, CY), 0) < 4
    lane8 = iota((8, CY), 1)
    sub8 = iota((8, CY), 0)
    lane = iota((RING, CY), 1)
    quarter8 = (lane8 // 4) % 4
    quarter = (lane // 4) % 4
    tail = slice(CX, RING)

    for f in range(FIELDS):
        for q in range(NZ // 2):
            k = f * 4 + q
            after = jnp.where(even_x, ra[k], rb[k])
            before = jnp.where(even_x, rb[k], ra[k])
            one = jnp.where(low, after, before)
            two = roll(jnp.where(low, before, after), 4, 0)
            if f < 6:
                S[f, 2 * q, tail, :] = one
                S[f, 2 * q + 1, tail, :] = two
            elif f < 9:
                V[f - 6, 2 * q, tail, :] = one
                V[f - 6, 2 * q + 1, tail, :] = two
            else:
                Z[2 * q, tail, :] = one.astype(jnp.int32)
                Z[2 * q + 1, tail, :] = two.astype(jnp.int32)

    up_x = (gx + 1) % n_gx
    down_x = (gx + n_gx - 1) % n_gx
    left_y = (gy + n_gy - 1) % n_gy
    right_y = (gy + 1) % n_gy

    def tile_of(x, y, t):
        at = pl.multiple_of((x * n_gy + y) * CHUNK + 8 * t, 8)
        return mesh_in[pl.ds(at, 8), :]

    def corner_rows(y):
        a0, a1 = tile_of(up_x, y, 0), tile_of(up_x, y, 1)
        b0, b1 = tile_of(down_x, y, 0), tile_of(down_x, y, 1)
        return [
            jnp.where(low, a0, b0),
            roll(jnp.where(low, b0, a0), 4, 0),
            jnp.where(low, a1, b1),
        ]

    left_tail = corner_rows(left_y)
    right_tail = corner_rows(right_y)
    own_idx = jnp.where(quarter8 == 1, lane8 % 16 - 4, jnp.where(quarter8 == 2, lane8 % 16 - 8 + CY - 4, 0))
    for f in range(FIELDS):
        p, s = f // 4, f % 4
        own_first = jnp.where(even_y, own_b[p], own_a[p])
        own_last = jnp.where(even_y, own_a[p], own_b[p])
        from_left = jnp.where(even_y, cb[p], ca[p])
        from_right = jnp.where(even_y, ca[p], cb[p])
        part = jnp.where(
            quarter[:CX] == 0, roll(from_left, -4 * s, 1),
            jnp.where(quarter[:CX] == 1, roll(own_first, -4 * s, 1),
                      jnp.where(quarter[:CX] == 2, roll(own_last, 8 - 4 * s, 1), roll(from_right, 8 - 4 * s, 1))),
        )
        BF[f, 0:CX, :] = part
        own = jnp.zeros((8, CY), F32)
        for z in range(NZ):
            if f < 6:
                src = S[f, z, tail, :]
            elif f < 9:
                src = V[f - 6, z, tail, :]
            else:
                src = Z[z, tail, :].astype(F32)
            own = jnp.where(lane8 // 16 == z, take(src, own_idx), own)
        end = jnp.where(
            quarter8 == 0, roll(left_tail[p], -4 * s, 1),
            jnp.where(quarter8 == 3, roll(right_tail[p], 8 - 4 * s, 1), own),
        )
        BF[f, tail, :] = end

    my_owner = owner[gy]
    left_owner = owner[left_y]
    right_owner = owner[right_y]
    main_at = (my_owner * n_gy + gy) * CHUNK
    left_at = (left_owner * n_gy + left_y) * CHUNK + 8 + jnp.where(left_owner == up_x, 7, 0)
    right_at = (right_owner * n_gy + right_y) * CHUNK + 8 + jnp.where(right_owner == up_x, 7, 0)
    left_edge = jnp.broadcast_to(mesh_in[pl.ds(left_at, 1), :], (8, CY))
    right_edge = jnp.broadcast_to(mesh_in[pl.ds(right_at, 1), :], (8, CY))
    deepest = lane8 >= 16 * (NZ - 1)
    for s in range(STEPS):
        for c in range(3):
            for q in range(RING // 8):
                if q < 4:
                    row_a = mesh_in[pl.ds(main_at + s * CXC + 2 * q, 1), :]
                    row_b = mesh_in[pl.ds(main_at + s * CXC + 2 * q + 1, 1), :]
                    base = c * CYC
                else:
                    row_a = mesh_in[pl.ds(main_at + s * CXC + c, 1), :]
                    row_b = mesh_in[pl.ds(main_at + s * CXC + 3 + c, 1), :]
                    base = 3 * CYC
                rows = jnp.where(low, jnp.broadcast_to(row_a, (8, CY)), jnp.broadcast_to(row_b, (8, CY)))
                DRM[s, c, 0, 8 * q:8 * q + 8, :] = take(rows, base + lane8 // COARSE)
                inner = take(rows, base + jnp.where(quarter8 == 2, CYC - 1, 0))
                at = (s * 3 + c) * 10 + 2 * q
                edge_idx = jnp.where(low, at, at + 1)
                value = jnp.where(
                    quarter8 == 0, take(left_edge, edge_idx),
                    jnp.where(quarter8 == 3, take(right_edge, edge_idx), inner),
                )
                DRM[s, c, 1, 8 * q:8 * q + 8, :] = jnp.where(deepest, value, 0.0)

    for copy in loads:
        copy.wait()

    scaled = table[...] * 0.1
    spread = jnp.concatenate([scaled] * (CY // ZONES), axis=1)
    columns = [jnp.broadcast_to(spread[k:k + 1, :], (RING, CY)) for k in range(3)]
    for z in range(NZ):
        ids = Z[z]
        LAM[z] = take(columns[0], ids)
        MU[z] = take(columns[1], ids)
        BUOY[z] = take(columns[2], ids)
    ids = BF[9].astype(jnp.int32)
    for k in range(3):
        BM[k] = take(columns[k], ids)

    def dx(x):
        return roll(x, RING - 1, 0) - roll(x, 1, 0)

    def dy(x, band, z):
        idx = jnp.where(lane == 0, 16 * z + 3, 16 * z + 12)
        seam = take(band, idx)
        return jnp.where(lane == CY - 1, seam, roll(x, CY - 1, 1)) - jnp.where(lane == 0, seam, roll(x, 1, 1))

    def dz(ref, f, z):
        if z == 0:
            return ref[f, 1]
        if z == NZ - 1:
            return -ref[f, NZ - 2]
        return ref[f, z + 1] - ref[f, z - 1]

    def band_dy(x):
        return roll(x, CY - 1, 1) - roll(x, 1, 1)

    def band_dz(x):
        return jnp.where(lane < CY - 16, roll(x, CY - 16, 1), 0.0) - jnp.where(lane >= 16, roll(x, 16, 1), 0.0)

    XX, XZ, XY, YY, YZ, ZZ = range(6)
    saves = []
    for step in range(STEPS):
        for z in range(NZ):
            sxy, sxz, syz = S[XY, z], S[XZ, z], S[YZ, z]
            fx = dx(S[XX, z]) + dy(sxy, BF[XY], z) + dz(S, XZ, z)
            fy = dx(sxy) + dy(S[YY, z], BF[YY], z) + dz(S, YZ, z)
            fz = dx(sxz) + dy(syz, BF[YZ], z) + dz(S, ZZ, z)
            force = [fx, fy, fz]
            if z == NZ - 1:
                force = [force[c] + (20.0 * MU[z]) * DRM[step, c, 0] for c in range(3)]
            for c in range(3):
                V[c, z] = V[c, z] + BUOY[z] * force[c]
        sxy, sxz, syz = BF[XY], BF[XZ], BF[YZ]
        force = [
            dx(BF[XX]) + band_dy(sxy) + band_dz(sxz),
            dx(sxy) + band_dy(BF[YY]) + band_dz(syz),
            dx(sxz) + band_dy(syz) + band_dz(BF[ZZ]),
        ]
        for c in range(3):
            BF[6 + c] = BF[6 + c] + BM[2] * (force[c] + (20.0 * BM[1]) * DRM[step, c, 1])
        if step == STEPS - 1:
            save = pltpu.make_async_copy(V.at[:, :, pl.ds(0, CX), :], vel_out, out_sems.at[NZ])
            save.start()
            saves.append(save)
        for z in range(NZ):
            vx, vy, vz = V[0, z], V[1, z], V[2, z]
            lam, mu = LAM[z], MU[z]
            xx, yy, zz = dx(vx), dy(vy, BF[7], z), dz(V, 2, z)
            theta = lam * (xx + yy + zz)
            two = mu + mu
            S[XX, z] = S[XX, z] + (theta + two * xx)
            S[YY, z] = S[YY, z] + (theta + two * yy)
            S[ZZ, z] = S[ZZ, z] + (theta + two * zz)
            S[XZ, z] = S[XZ, z] + mu * (dz(V, 0, z) + dx(vz))
            S[XY, z] = S[XY, z] + mu * (dy(vx, BF[6], z) + dx(vy))
            S[YZ, z] = S[YZ, z] + mu * (dz(V, 1, z) + dy(vz, BF[8], z))
            if step == STEPS - 1:
                save = pltpu.make_async_copy(S.at[:, z, pl.ds(0, CX), :], stress_out.at[:, z], out_sems.at[z])
                save.start()
                saves.append(save)
        if step < STEPS - 1:
            vx, vy, vz = BF[6], BF[7], BF[8]
            lam, mu = BM[0], BM[1]
            xx, yy, zz = dx(vx), band_dy(vy), band_dz(vz)
            theta = lam * (xx + yy + zz)
            two = mu + mu
            BF[XX] = BF[XX] + (theta + two * xx)
            BF[YY] = BF[YY] + (theta + two * yy)
            BF[ZZ] = BF[ZZ] + (theta + two * zz)
            BF[XZ] = BF[XZ] + mu * (band_dz(vx) + dx(vz))
            BF[XY] = BF[XY] + mu * (band_dy(vx) + dx(vy))
            BF[YZ] = BF[YZ] + mu * (band_dz(vy) + band_dy(vz))

    total = jnp.zeros((8, CY), F32)
    for c, f in enumerate((XZ, YZ)):
        for r in range(CX // BLOCK):
            row = jnp.sum(S[f, 1, 8 * r:8 * r + 8, :], axis=0, keepdims=True)
            total = jnp.where(sub8 == 4 * c + r, jnp.broadcast_to(row, (8, CY)), total)
    for shift in (1, 2, 4):
        total = total + roll(total, CY - shift, 1)
    total = total * (1.0 / (BLOCK * BLOCK))
    ids = jnp.broadcast_to(jnp.concatenate([block[0], block[0]], axis=1), (8, CY))
    cells = CY // BLOCK
    picked = take(total, (ids % cells) * BLOCK)
    mine = (sub8 % 4 == ids // cells) & (sub8 // 4 == lane8 // FP_DEV)
    values = jnp.sum(jnp.where(mine, picked, 0.0), axis=0, keepdims=True)
    names = jnp.concatenate([building[0], building[0]], axis=1).astype(F32)
    message = jnp.concatenate([values, names], axis=0)
    shares[...] = jnp.broadcast_to(message[None], shares.shape)
    for save in saves:
        save.wait()


def sum_kernel(n, shares, out):
    half = n // 2
    low = iota((half, CY), 1) < FP_DEV
    values = shares[:, 0, :]
    names = shares[:, 1, :].astype(jnp.int32)
    entry = [
        jnp.where(low, values[:half], roll(values[half:], FP_DEV, 1)),
        jnp.where(low, roll(values[:half], FP_DEV, 1), values[half:]),
    ]
    names = jnp.where(low, names[:half], names[half:])
    high = names // CY
    names = names % CY
    n_high = BUILDINGS // CY
    rows = iota((n_high, CY), 0)
    wanted = iota((CY, CY), 0)
    acc = jnp.zeros((6 * n_high, CY), F32)
    for k in range(half):
        hot = (jnp.broadcast_to(names[k:k + 1], (CY, CY)) == wanted).astype(F32).astype(jnp.bfloat16)
        here = jnp.broadcast_to(high[k:k + 1], (n_high, CY)) == rows
        left = []
        for c in range(2):
            rest = jnp.where(here, jnp.broadcast_to(entry[c][k:k + 1], (n_high, CY)), 0.0)
            for _ in range(3):
                piece = rest.astype(jnp.bfloat16)
                rest = rest - piece.astype(F32)
                left.append(piece.astype(F32))
        left = jnp.concatenate(left, axis=0).astype(jnp.bfloat16)
        acc = acc + lax.dot_general(left, hot, (((1,), (1,)), ((), ())), preferred_element_type=F32)
    for c in range(2):
        base = 3 * c * n_high
        out[c] = acc[base:base + n_high] + acc[base + n_high:base + 2 * n_high] + acc[base + 2 * n_high:base + 3 * n_high]


def pairs_near(n):
    return [(i, i ^ 1) for i in range(n)]


def pairs_far(n):
    return [(i, (i + 1) % n if i % 2 else (i - 1) % n) for i in range(n)]


def body(n_gx, n_gy, velocity, stress, zones, zone_table, regional, owner, building, block):
    n = n_gx * n_gy
    vmem = pl.BlockSpec(memory_space=pltpu.VMEM)
    smem = pl.BlockSpec(memory_space=pltpu.SMEM)
    anywhere = pl.BlockSpec(memory_space=pl.ANY)
    params = pltpu.CompilerParams(vmem_limit_bytes=VMEM_LIMIT)
    rows = jax.ShapeDtypeStruct((FIELDS * 4, 8, CY), F32)
    cols = jax.ShapeDtypeStruct((PACKS, CX, CY), F32)
    gxa, gxb, gya, gyb, slices = pl.pallas_call(
        functools.partial(pack_kernel, n_gx, n_gy),
        out_shape=(rows, rows, cols, cols, jax.ShapeDtypeStruct((n * CHUNK, CY), F32)),
        in_specs=[vmem] * 4,
        out_specs=(vmem,) * 5,
        compiler_params=params,
        name="pack",
    )(velocity, stress, zones, regional)
    rb = lax.ppermute(gxb, "gx", pairs_far(n_gx))
    ra = lax.ppermute(gxa, "gx", pairs_near(n_gx))
    ca = lax.ppermute(gya, "gy", pairs_near(n_gy))
    cb = lax.ppermute(gyb, "gy", pairs_far(n_gy))
    got = lax.all_to_all(slices.reshape(n, CHUNK, CY), ("gx", "gy"), 0, 0).reshape(n * CHUNK, CY)
    full = (NZ, RING, CY)
    vel_out, stress_out, shares = pl.pallas_call(
        functools.partial(step_kernel, n_gx, n_gy),
        out_shape=(
            jax.ShapeDtypeStruct(velocity.shape, F32),
            jax.ShapeDtypeStruct(stress.shape, F32),
            jax.ShapeDtypeStruct((n, 2, CY), F32),
        ),
        in_specs=[anywhere] * 3 + [vmem] * 8 + [smem] + [vmem] * 2,
        out_specs=(anywhere, anywhere, vmem),
        scratch_shapes=[
            pltpu.VMEM((6,) + full, F32),
            pltpu.VMEM((3,) + full, F32),
            pltpu.VMEM(full, jnp.int32),
            pltpu.VMEM(full, F32),
            pltpu.VMEM(full, F32),
            pltpu.VMEM(full, F32),
            pltpu.VMEM((FIELDS, RING, CY), F32),
            pltpu.VMEM((3, RING, CY), F32),
            pltpu.VMEM((STEPS, 3, 2, RING, CY), F32),
            pltpu.SemaphoreType.DMA((3,)),
            pltpu.SemaphoreType.DMA((NZ + 1,)),
        ],
        compiler_params=params,
        name="steps",
    )(velocity, stress, zones, zone_table, gya, gyb, ra, rb, ca, cb, got, owner, building, block)
    every = lax.all_to_all(shares, ("gx", "gy"), 0, 0)
    shear = pl.pallas_call(
        functools.partial(sum_kernel, n),
        out_shape=jax.ShapeDtypeStruct((2, BUILDINGS // CY, CY), F32),
        in_specs=[vmem],
        out_specs=vmem,
        compiler_params=params,
        name="sum_by_building",
    )(every)
    return vel_out, stress_out, shear.reshape(2, BUILDINGS)


def solution(mesh):
    n_gx, n_gy = mesh.shape["gx"], mesh.shape["gy"]
    return jax.shard_map(
        functools.partial(body, n_gx, n_gy),
        mesh=mesh,
        in_specs=(
            P(None, None, "gx", "gy"),
            P(None, None, "gx", "gy"),
            P(None, "gx", "gy"),
            P(),
            P("gx", None, None, None, "gy"),
            P(),
            P("gx", "gy", None),
            P("gx", "gy", None),
        ),
        out_specs=(P(None, None, "gx", "gy"), P(None, None, "gx", "gy"), P()),
        check_vma=False,
    )
```

```python
import functools

import jax
import jax.numpy as jnp
from jax import lax
from jax.experimental import pallas as pl
from jax.experimental.pallas import tpu as pltpu
from jax.sharding import PartitionSpec as P

CX = 32
CY = 128
NZ = 8
STEPS = 2
COARSE = 4
BLOCK = 8
ZONES = 16
BUILDINGS = 1024
FP_DEV = 64
HALO = 4
RING = CX + 2 * HALO
FIELDS = 10
PACKS = 3
CHUNK = 16
COLS = PACKS * CX
CXC = CX // COARSE
CYC = CY // COARSE
F32 = jnp.float32
VMEM_LIMIT = 32 * 1024 * 1024


def iota(shape, dim):
    return lax.broadcasted_iota(jnp.int32, shape, dim)


def take(x, idx):
    idx = jnp.broadcast_to(idx, x.shape)
    return jnp.take_along_axis(x, idx, axis=1, mode="promise_in_bounds")


def roll(x, shift, axis):
    size = x.shape[axis]
    shift = shift % size
    return x if shift == 0 else pltpu.roll(x, shift, axis)


def pack_kernel(
    n_gx, n_gy, vel, stress, zones, regional, table_in, building_in, block_in, owner,
    S, V, gxa, gxb, gya, gyb, slices, source, table, building, block, Z, R, sems,
):
    gx = lax.axis_index("gx")
    gy = lax.axis_index("gy")
    even_x = (gx & 1) == 0
    even_y = (gy & 1) == 0
    inner = pl.ds(0, CX)
    loads = [pltpu.make_async_copy(stress.at[f], S.at[f, :, inner, :], sems.at[f]) for f in range(6)]
    loads += [pltpu.make_async_copy(vel.at[f], V.at[f, :, inner, :], sems.at[6 + f]) for f in range(3)]
    loads.append(pltpu.make_async_copy(zones, Z, sems.at[9]))
    loads.append(pltpu.make_async_copy(regional, R, sems.at[10]))
    loads.append(pltpu.make_async_copy(table_in, table, sems.at[11]))
    loads.append(pltpu.make_async_copy(building_in, building, sems.at[12]))
    loads.append(pltpu.make_async_copy(block_in, block, sems.at[13]))
    for copy in loads:
        copy.start()
    row = iota((CHUNK, CY), 0)
    edge = (iota((CHUNK, CY), 1) >= 96) & ((row & 7) >= 6)
    sides = jnp.where(row < CXC, owner[(gy + n_gy - 1) % n_gy], owner[(gy + 1) % n_gy])
    source[...] = jnp.where(edge, sides, owner[gy])
    slot = iota((CX, CY), 1) // HALO
    low = iota((8, CY), 0) < 4

    def plane(f, z, a, b):
        if f < 6:
            return S[f, z, a:b, :]
        if f < 9:
            return V[f - 6, z, a:b, :]
        return Z[z, a:b, :].astype(F32)

    for p in range(PACKS):
        lasts = jnp.zeros((CX, CY), F32)
        firsts = jnp.zeros((CX, CY), F32)
        for s in range(4):
            f = 4 * p + s
            if f >= FIELDS:
                continue
            loads[f].wait()
            for z in range(NZ):
                turned = roll(plane(f, z, 0, CX), 16 * z + 4 * s + 4, 1)
                at = 4 * z + s
                lasts = jnp.where(slot == at, turned, lasts)
                firsts = jnp.where(slot == (at + 1) % 32, turned, firsts)
            for q in range(NZ // 2):
                first = jnp.where(low, plane(f, 2 * q, 0, 8), roll(plane(f, 2 * q + 1, 0, 8), 4, 0))
                last = jnp.where(low, roll(plane(f, 2 * q + 1, CX - 8, CX), 4, 0), plane(f, 2 * q, CX - 8, CX))
                gxa[f * 4 + q] = jnp.where(even_x, last, first)
                gxb[f * 4 + q] = jnp.where(even_x, first, last)
        gya[p * CX:(p + 1) * CX, :] = jnp.where(even_y, lasts, firsts)
        gyb[p * CX:(p + 1) * CX, :] = jnp.where(even_y, firsts, lasts)

    loads[10].wait()
    lane = iota((n_gx, CY), 1)
    part = lane // CYC
    digit = (lane - 96) % 10
    group = (lane - 96) // 10
    for s in range(STEPS):
        halves = [[R[0, s, c, :, t * CY:(t + 1) * CY] for t in range(2)] for c in range(3)]
        nexts = [roll(halves[c][0], n_gx - 1, 0) for c in range(3)]
        befores = [roll(halves[c][1], 1, 0) for c in range(3)]
        for r in range(CXC):
            row = jnp.zeros((n_gx, CY), F32)
            for c in range(3):
                row = jnp.where(part == c, roll(halves[c][r // 4], CYC * (c - r % 4), 1), row)
            if r < 3:
                row = jnp.where(part == 3, roll(nexts[r], 96, 1), row)
            elif r < 6:
                row = jnp.where(part == 3, befores[r - 3], row)
            slices[pl.ds(s * CXC + r, n_gx, stride=CHUNK), :] = row
        ends = []
        for col in (CYC - 1, 0):
            ends.append(jnp.zeros((n_gx, CY), F32))
            idx_low = jnp.where(digit < 4, digit * CYC + col, 0)
            idx_high = jnp.where((digit >= 4) & (digit < 8), (digit - 4) * CYC + col, 0)
            for c in range(3):
                edge = jnp.where(digit < 4, take(halves[c][0], idx_low), take(halves[c][1], idx_high))
                edge = jnp.where(digit == 8, take(nexts[c], jnp.full_like(digit, col)), edge)
                edge = jnp.where(digit == 9, take(befores[c], jnp.full_like(digit, 3 * CYC + col)), edge)
                ends[-1] = jnp.where((lane >= 96) & (group == c), edge, ends[-1])
        at = COLS + s * n_gx
        gya[at:at + n_gx, :] = jnp.where(even_y, ends[0], ends[1])
        gyb[at:at + n_gx, :] = jnp.where(even_y, ends[1], ends[0])
    for copy in loads[11:]:
        copy.wait()


def relay_kernel(n_gx, ca, cb, slices, ea, eb, sent, kept):
    gx = lax.axis_index("gx")
    even_x = (gx & 1) == 0
    even_y = (lax.axis_index("gy") & 1) == 0
    low = iota((8, CY), 0) < 4

    for p in range(PACKS):
        top, end = slice(p * CX, p * CX + 8), slice((p + 1) * CX - 8, (p + 1) * CX)
        left_top, right_top = jnp.where(even_y, cb[top], ca[top]), jnp.where(even_y, ca[top], cb[top])
        left_end, right_end = jnp.where(even_y, cb[end], ca[end]), jnp.where(even_y, ca[end], cb[end])
        first = jnp.where(low, left_top, roll(right_top, 4, 0))
        last = jnp.where(low, roll(left_end, 4, 0), right_end)
        ea[p] = jnp.where(even_x, last, first)
        eb[p] = jnp.where(even_x, first, last)

    half = n_gx // 2
    bit = (gx >= half).astype(jnp.int32)
    lane = iota((CHUNK, CY), 1)
    row = iota((CHUNK, CY), 0)
    for out, side in ((sent, 1 - bit), (kept, bit)):
        for i in range(half):
            at = side * half + i
            value = slices[pl.ds(pl.multiple_of(at * CHUNK, CHUNK), CHUNK), :]
            for s in range(STEPS):
                a, b = ca[pl.ds(COLS + s * n_gx + at, 1), :], cb[pl.ds(COLS + s * n_gx + at, 1), :]
                ends = (jnp.where(even_y, b, a), jnp.where(even_y, a, b))
                for k in range(2):
                    here = (lane >= 96) & (row == k * CXC + 6 + s)
                    value = jnp.where(here, jnp.broadcast_to(ends[k], (CHUNK, CY)), value)
            out[i] = value


def spread_table(table):
    scaled = table[...] * 0.1
    spread = jnp.concatenate([scaled] * (CY // ZONES), axis=1)
    return [spread[k:k + 1, :] for k in range(3)]


def material_kernel(zones, table, LAM, MU, BUOY):
    columns = [jnp.broadcast_to(row, (CX, CY)) for row in spread_table(table)]
    for z in range(NZ):
        ids = zones[z]
        for k, ref in enumerate((LAM, MU, BUOY)):
            ref[z, 0:CX, :] = take(columns[k], ids)


XX, XZ, XY, YY, YZ, ZZ = range(6)


def dx(x):
    return roll(x, RING - 1, 0) - roll(x, 1, 0)


def dy(x, seam, z):
    lane = iota((RING, CY), 1)
    seam = roll(seam, -(16 * z + 3), 1)
    return jnp.where(lane == CY - 1, seam, roll(x, CY - 1, 1)) - jnp.where(lane == 0, seam, roll(x, 1, 1))


def dz(ref, f, z):
    if z == 0:
        return ref[f, 1]
    if z == NZ - 1:
        return -ref[f, NZ - 2]
    return ref[f, z + 1] - ref[f, z - 1]


def band_dy(x):
    return roll(x, CY - 1, 1) - roll(x, 1, 1)


def band_dz(x):
    lane = iota((RING, CY), 1)
    return jnp.where(lane < CY - 16, roll(x, CY - 16, 1), 0.0) - jnp.where(lane >= 16, roll(x, 16, 1), 0.0)


def seams(band, fields):
    lane = iota((RING, CY), 1)
    return {f: jnp.where(lane % 16 == 2, roll(band[f], -10, 1), band[f]) for f in fields}


def velocity_planes(planes, S, V, MU, BUOY, band, drm):
    seam = seams(band, (XY, YY, YZ))
    for z in planes:
        sxy, sxz, syz = S[XY, z], S[XZ, z], S[YZ, z]
        force = [
            dx(S[XX, z]) + dy(sxy, seam[XY], z) + dz(S, XZ, z),
            dx(sxy) + dy(S[YY, z], seam[YY], z) + dz(S, YZ, z),
            dx(sxz) + dy(syz, seam[YZ], z) + dz(S, ZZ, z),
        ]
        if z == NZ - 1:
            force = [force[c] + (20.0 * MU[z]) * drm(c, 0) for c in range(3)]
        for c in range(3):
            V[c, z] = V[c, z] + BUOY[z] * force[c]


def velocity_band(band, new, BM, drm):
    sxy, sxz, syz = band[XY], band[XZ], band[YZ]
    force = [
        dx(band[XX]) + band_dy(sxy) + band_dz(sxz),
        dx(sxy) + band_dy(band[YY]) + band_dz(syz),
        dx(sxz) + band_dy(syz) + band_dz(band[ZZ]),
    ]
    for c in range(3):
        if drm is not None:
            force[c] = force[c] + (20.0 * BM[1]) * drm(c, 1)
        new[6 + c] = band[6 + c] + BM[2] * force[c]


def stress_plane(z, seam, S, V, LAM, MU, fields):
    vx, vy, vz = V[0, z], V[1, z], V[2, z]
    mu = MU[z]
    if XX in fields:
        lam = LAM[z]
        xx, yy, zz = dx(vx), dy(vy, seam[7], z), dz(V, 2, z)
        theta = lam * (xx + yy + zz)
        two = mu + mu
        S[XX, z] = S[XX, z] + (theta + two * xx)
        S[YY, z] = S[YY, z] + (theta + two * yy)
        S[ZZ, z] = S[ZZ, z] + (theta + two * zz)
    if XZ in fields:
        S[XZ, z] = S[XZ, z] + mu * (dz(V, 0, z) + dx(vz))
    if XY in fields:
        S[XY, z] = S[XY, z] + mu * (dy(vx, seam[6], z) + dx(vy))
    if YZ in fields:
        S[YZ, z] = S[YZ, z] + mu * (dz(V, 1, z) + dy(vz, seam[8], z))


def stress_band(band, new, BM):
    vx, vy, vz = new[6], new[7], new[8]
    lam, mu = BM[0], BM[1]
    xx, yy, zz = dx(vx), band_dy(vy), band_dz(vz)
    theta = lam * (xx + yy + zz)
    two = mu + mu
    new[XX] = band[XX] + (theta + two * xx)
    new[YY] = band[YY] + (theta + two * yy)
    new[ZZ] = band[ZZ] + (theta + two * zz)
    new[XZ] = band[XZ] + mu * (band_dz(vx) + dx(vz))
    new[XY] = band[XY] + mu * (band_dy(vx) + dx(vy))
    new[YZ] = band[YZ] + mu * (band_dz(vy) + band_dy(vz))


ALL = (XX, XZ, XY, YY, YZ, ZZ)


def cone_kernel(
    S_in, V_in, LAM_in, MU_in, BUOY_in, table, own_a, own_b, ra, rb, ca, cb, ea, eb, building, block,
    S, V, LAM, MU, BUOY, BF, BM, shares, BW,
):
    even_x = (lax.axis_index("gx") & 1) == 0
    even_y = (lax.axis_index("gy") & 1) == 0
    low = iota((8, CY), 0) < 4
    lane8 = iota((8, CY), 1)
    sub8 = iota((8, CY), 0)
    quarter8 = (lane8 // 4) % 4
    quarter = (iota((CX, CY), 1) // 4) % 4
    tail = slice(CX, RING)
    columns = spread_table(table)
    columns8 = [jnp.broadcast_to(row, (8, CY)) for row in columns]

    own_idx = jnp.where(quarter8 == 1, lane8 % 16 - 4, jnp.where(quarter8 == 2, lane8 % 16 - 8 + CY - 4, 0))
    own_tail = []
    for f in range(FIELDS):
        own = jnp.zeros((8, CY), F32)
        for q in range(NZ // 2):
            k = f * 4 + q
            after = jnp.where(even_x, ra[k], rb[k])
            before = jnp.where(even_x, rb[k], ra[k])
            both = (jnp.where(low, after, before), roll(jnp.where(low, before, after), 4, 0))
            for z in (2 * q, 2 * q + 1):
                rows = both[z % 2]
                own = jnp.where(lane8 // 16 == z, take(rows, own_idx), own)
                if f < 6:
                    S[f, z, tail, :] = rows
                elif f < 9:
                    V[f - 6, z, tail, :] = rows
                else:
                    ids = rows.astype(jnp.int32)
                    for column, ref in zip(columns8, (LAM, MU, BUOY)):
                        ref[z, tail, :] = take(column, ids)
        own_tail.append(own)

    for p in range(PACKS):
        at = slice(p * CX, (p + 1) * CX)
        own_first = jnp.where(even_y, own_b[at], own_a[at])
        own_last = jnp.where(even_y, own_a[at], own_b[at])
        from_left = jnp.where(even_y, cb[at], ca[at])
        from_right = jnp.where(even_y, ca[at], cb[at])
        after = jnp.where(even_x, ea[p], eb[p])
        before = jnp.where(even_x, eb[p], ea[p])
        left_tail = jnp.where(low, after, roll(before, 4, 0))
        right_tail = jnp.where(low, roll(after, 4, 0), before)
        for s in range(4):
            f = 4 * p + s
            if f >= FIELDS:
                continue
            BF[f, 0:CX, :] = jnp.where(
                quarter == 0, roll(from_left, -4 * s, 1),
                jnp.where(quarter == 1, roll(own_first, -4 * s, 1),
                          jnp.where(quarter == 2, roll(own_last, 8 - 4 * s, 1), roll(from_right, 8 - 4 * s, 1))),
            )
            BF[f, tail, :] = jnp.where(
                quarter8 == 0, roll(left_tail, -4 * s, 1),
                jnp.where(quarter8 == 3, roll(right_tail, 8 - 4 * s, 1), own_tail[f]),
            )
    ids = BF[9].astype(jnp.int32)
    for k in range(3):
        BM[k] = take(jnp.broadcast_to(columns[k], (RING, CY)), ids)

    velocity_planes(range(0, 5), S, V, MU, BUOY, BF, None)
    velocity_band(BF, BW, BM, None)
    seam = seams(BW, (6, 7, 8))
    for z in range(0, 4):
        stress_plane(z, seam, S, V, LAM, MU, ALL)
    stress_band(BF, BW, BM)
    velocity_planes(range(0, 3), S, V, MU, BUOY, BW, None)
    velocity_band(BW, BW, BM, None)
    stress_plane(1, seams(BW, (8,)), S, V, LAM, MU, (XZ, YZ))

    total = jnp.zeros((8, CY), F32)
    for c, f in enumerate((XZ, YZ)):
        for r in range(CX // BLOCK):
            row = jnp.sum(S[f, 1, 8 * r:8 * r + 8, :], axis=0, keepdims=True)
            total = jnp.where(sub8 == 4 * c + r, jnp.broadcast_to(row, (8, CY)), total)
    for shift in (1, 2, 4):
        total = total + roll(total, CY - shift, 1)
    total = total * (1.0 / (BLOCK * BLOCK))
    ids = jnp.broadcast_to(jnp.concatenate([block[0], block[0]], axis=1), (8, CY))
    cells = CY // BLOCK
    picked = take(total, (ids % cells) * BLOCK)
    mine = (sub8 % 4 == ids // cells) & (sub8 // 4 == lane8 // FP_DEV)
    values = jnp.sum(jnp.where(mine, picked, 0.0), axis=0, keepdims=True)
    names = jnp.concatenate([building[0], building[0]], axis=1).astype(F32)
    message = jnp.concatenate([values, names], axis=0)
    shares[...] = jnp.broadcast_to(message[None], shares.shape)


def rest_kernel(
    S_in, V_in, LAM, MU, BUOY, BF_in, BM, drm_in,
    S, V, BF, vel_out, stress_out, DRM, sems,
):
    low = iota((8, CY), 0) < 4
    lane8 = iota((8, CY), 1)
    quarter8 = (lane8 // 4) % 4
    deepest = lane8 >= 16 * (NZ - 1)

    def wide(row):
        return jnp.broadcast_to(drm_in[row:row + 1, :], (8, CY))

    for s in range(STEPS):
        left_edge, right_edge = wide(6 + s), wide(CXC + 6 + s)
        for c in range(3):
            for q in range(RING // 8):
                if q < 4:
                    rows = jnp.where(low, wide(s * CXC + 2 * q), wide(s * CXC + 2 * q + 1))
                    base = c * CYC
                else:
                    rows = jnp.where(low, wide(s * CXC + c), wide(s * CXC + 3 + c))
                    base = 3 * CYC
                DRM[s, c, 0, 8 * q:8 * q + 8, :] = take(rows, base + lane8 // COARSE)
                inner = take(rows, base + jnp.where(quarter8 == 2, CYC - 1, 0))
                at = 96 + c * 10 + 2 * q
                edge_idx = jnp.where(low, at, at + 1)
                value = jnp.where(
                    quarter8 == 0, take(left_edge, edge_idx),
                    jnp.where(quarter8 == 3, take(right_edge, edge_idx), inner),
                )
                DRM[s, c, 1, 8 * q:8 * q + 8, :] = jnp.where(deepest, value, 0.0)

    def drm(step):
        return lambda c, k: DRM[step, c, k]

    saves = []
    velocity_planes(range(5, NZ), S, V, MU, BUOY, BF, drm(0))
    velocity_band(BF, BF, BM, drm(0))
    seam = seams(BF, (6, 7, 8))
    for z in range(4, NZ):
        stress_plane(z, seam, S, V, LAM, MU, ALL)
    stress_band(BF, BF, BM)
    velocity_planes(range(3, NZ), S, V, MU, BUOY, BF, drm(1))
    velocity_band(BF, BF, BM, drm(1))
    inner = pl.ds(0, CX)
    saves.append(pltpu.make_async_copy(V.at[:, :, inner, :], vel_out, sems.at[NZ]))
    saves[-1].start()
    seam = seams(BF, (6, 7, 8))
    for z in range(NZ):
        stress_plane(z, seam, S, V, LAM, MU, (XX, XY) if z == 1 else ALL)
        saves.append(pltpu.make_async_copy(S.at[:, z, inner, :], stress_out.at[:, z], sems.at[z]))
        saves[-1].start()
    for save in saves:
        save.wait()


def sum_kernel(n, shares, out):
    half = n // 2
    low = iota((half, CY), 1) < FP_DEV
    values = shares[:, 0, :]
    names = shares[:, 1, :].astype(jnp.int32)
    entry = [
        jnp.where(low, values[:half], roll(values[half:], FP_DEV, 1)),
        jnp.where(low, roll(values[:half], FP_DEV, 1), values[half:]),
    ]
    names = jnp.where(low, names[:half], names[half:])
    high = names // CY
    names = names % CY
    n_high = BUILDINGS // CY
    rows = iota((n_high, CY), 0)
    wanted = iota((CY, CY), 0)
    acc = jnp.zeros((6 * n_high, CY), F32)
    for k in range(half):
        hot = (jnp.broadcast_to(names[k:k + 1], (CY, CY)) == wanted).astype(F32).astype(jnp.bfloat16)
        here = jnp.broadcast_to(high[k:k + 1], (n_high, CY)) == rows
        left = []
        for c in range(2):
            rest = jnp.where(here, jnp.broadcast_to(entry[c][k:k + 1], (n_high, CY)), 0.0)
            for _ in range(3):
                piece = rest.astype(jnp.bfloat16)
                rest = rest - piece.astype(F32)
                left.append(piece.astype(F32))
        left = jnp.concatenate(left, axis=0).astype(jnp.bfloat16)
        acc = acc + lax.dot_general(left, hot, (((1,), (1,)), ((), ())), preferred_element_type=F32)
    sums = []
    for c in range(2):
        base = 3 * c * n_high
        sums.append(acc[base:base + n_high] + acc[base + n_high:base + 2 * n_high] + acc[base + 2 * n_high:base + 3 * n_high])
    for h in range(n_high):
        out[:, h * CY:(h + 1) * CY] = jnp.concatenate([sums[0][h:h + 1], sums[1][h:h + 1]], axis=0)


def pairs_near(n):
    return [(i, i ^ 1) for i in range(n)]


def pairs_far(n):
    return [(i, (i + 1) % n if i % 2 else (i - 1) % n) for i in range(n)]


def body(n_gx, n_gy, velocity, stress, zones, zone_table, regional, owner, building, block):
    n = n_gx * n_gy
    gx = lax.axis_index("gx")
    vmem = pl.BlockSpec(memory_space=pltpu.VMEM)
    hbm = pl.BlockSpec(memory_space=pltpu.HBM)
    params = pltpu.CompilerParams(vmem_limit_bytes=VMEM_LIMIT)

    def shaped(*shape):
        return jax.ShapeDtypeStruct(shape, F32)

    def whole(shape, dtype):
        return jax.ShapeDtypeStruct(shape, dtype)

    s_ring = shaped(6, NZ, RING, CY)
    v_ring = shaped(3, NZ, RING, CY)
    m_ring = shaped(NZ, RING, CY)
    rows = shaped(FIELDS * 4, 8, CY)
    cols = shaped(COLS + STEPS * n_gx, CY)
    from_hbm = [
        pltpu.with_memory_space_constraint(x, pltpu.HBM)
        for x in (velocity, stress, zones, regional, zone_table, building, block)
    ]
    S, V, gxa, gxb, gya, gyb, slices, source, zone_table, building, block = pl.pallas_call(
        functools.partial(pack_kernel, n_gx, n_gy),
        out_shape=(
            s_ring, v_ring, rows, rows, cols, cols, shaped(n_gx * CHUNK, CY), whole((CHUNK, CY), jnp.int32),
            whole(zone_table.shape, F32), whole(building.shape, jnp.int32), whole(block.shape, jnp.int32),
        ),
        in_specs=[hbm] * 7 + [pl.BlockSpec(memory_space=pltpu.SMEM)],
        out_specs=(vmem,) * 11,
        scratch_shapes=[
            pltpu.VMEM(zones.shape, jnp.int32),
            pltpu.VMEM(regional.shape, F32),
            pltpu.SemaphoreType.DMA((14,)),
        ],
        compiler_params=params,
        name="pack",
    )(*from_hbm, owner)
    near_x, far_x = pairs_near(n_gx), pairs_far(n_gx)
    ca = lax.ppermute(gya, "gy", pairs_near(n_gy))
    cb = lax.ppermute(gyb, "gy", pairs_far(n_gy))
    rb = lax.ppermute(gxb, "gx", far_x)
    ra = lax.ppermute(gxa, "gx", near_x)
    half = n_gx // 2
    corner = shaped(PACKS, 8, CY)
    part = shaped(half, CHUNK, CY)
    msg_a, msg_b, sent, kept = pl.pallas_call(
        functools.partial(relay_kernel, n_gx),
        out_shape=(corner, corner, part, part),
        in_specs=[vmem] * 3,
        out_specs=(vmem,) * 4,
        compiler_params=params,
        name="relay",
    )(ca, cb, slices)
    eb = lax.ppermute(msg_b, "gx", far_x)
    ea = lax.ppermute(msg_a, "gx", near_x)

    def trade(sent, kept, width):
        got = lax.ppermute(sent, "gx", [(i, i ^ width) for i in range(n_gx)])
        held = jnp.where(((source ^ gx) & width) == 0, kept, got)
        if width == 1:
            return held, None
        width //= 2
        halves = held.reshape(2, width, CHUNK, CY)
        upper = (gx & width) != 0
        return jnp.where(upper, halves[0], halves[1]), jnp.where(upper, halves[1], halves[0])

    sent, kept = trade(sent, kept, half)
    LAM, MU, BUOY = pl.pallas_call(
        material_kernel,
        out_shape=(m_ring,) * 3,
        in_specs=[vmem] * 2,
        out_specs=(vmem,) * 3,
        compiler_params=params,
        name="materials",
    )(zones, zone_table)
    S, V, LAM, MU, BUOY, BF, BM, shares = pl.pallas_call(
        cone_kernel,
        out_shape=(s_ring, v_ring, m_ring, m_ring, m_ring, shaped(FIELDS, RING, CY), shaped(3, RING, CY), shaped(n, 2, CY)),
        in_specs=[vmem] * 16,
        out_specs=(vmem,) * 8,
        scratch_shapes=[pltpu.VMEM((9, RING, CY), F32)],
        input_output_aliases={k: k for k in range(5)},
        compiler_params=params,
        name="cone",
    )(S, V, LAM, MU, BUOY, zone_table, gya, gyb, ra, rb, ca, cb, ea, eb, building, block)
    sent, BM = lax.optimization_barrier((sent, BM))
    width = half // 2
    while width > 1:
        sent, kept = trade(sent, kept, width)
        width //= 2
    drm = trade(sent, kept, 1)[0].reshape(CHUNK, CY)
    every = lax.all_to_all(shares, ("gx", "gy"), 0, 0)
    _, _, _, vel_out, stress_out = pl.pallas_call(
        rest_kernel,
        out_shape=(s_ring, v_ring, shaped(FIELDS, RING, CY), shaped(*velocity.shape), shaped(*stress.shape)),
        in_specs=[vmem] * 8,
        out_specs=(vmem, vmem, vmem, hbm, hbm),
        scratch_shapes=[
            pltpu.VMEM((STEPS, 3, 2, RING, CY), F32),
            pltpu.SemaphoreType.DMA((NZ + 1,)),
        ],
        input_output_aliases={0: 0, 1: 1, 5: 2},
        compiler_params=params,
        name="rest",
    )(S, V, LAM, MU, BUOY, BF, BM, drm)
    shear = pl.pallas_call(
        functools.partial(sum_kernel, n),
        out_shape=shaped(2, BUILDINGS),
        in_specs=[vmem],
        out_specs=vmem,
        compiler_params=params,
        name="sum_by_building",
    )(every)
    return vel_out, stress_out, shear


def solution(mesh):
    n_gx, n_gy = mesh.shape["gx"], mesh.shape["gy"]
    return jax.shard_map(
        functools.partial(body, n_gx, n_gy),
        mesh=mesh,
        in_specs=(
            P(None, None, "gx", "gy"),
            P(None, None, "gx", "gy"),
            P(None, "gx", "gy"),
            P(),
            P("gx", None, None, None, "gy"),
            P(),
            P("gx", "gy", None),
            P("gx", "gy", None),
        ),
        out_specs=(P(None, None, "gx", "gy"), P(None, None, "gx", "gy"), P()),
        check_vma=False,
    )
```

```python
import functools

import jax
import jax.numpy as jnp
from jax import lax
from jax.experimental import pallas as pl
from jax.experimental.pallas import tpu as pltpu
from jax.sharding import PartitionSpec as P

CX = 32
CY = 128
NZ = 8
STEPS = 2
COARSE = 4
BLOCK = 8
ZONES = 16
BUILDINGS = 1024
FP_DEV = 64
HALO = 4
RING = CX + 2 * HALO
FIELDS = 10
PACKS = 3
CHUNK = 16
COLS = PACKS * CX
CXC = CX // COARSE
CYC = CY // COARSE
F32 = jnp.float32
VMEM_LIMIT = 32 * 1024 * 1024


def iota(shape, dim):
    return lax.broadcasted_iota(jnp.int32, shape, dim)


def take(x, idx):
    idx = jnp.broadcast_to(idx, x.shape)
    return jnp.take_along_axis(x, idx, axis=1, mode="promise_in_bounds")


def roll(x, shift, axis):
    size = x.shape[axis]
    shift = shift % size
    return x if shift == 0 else pltpu.roll(x, shift, axis)


def rows_kernel(
    vel, stress, zones, regional_in, table_in, building_in, block_in,
    gxa, gxb, regional, table, building, block, F, Z, sems,
):
    even_x = (lax.axis_index("gx") & 1) == 0
    low = iota((8, CY), 0) < 4
    loads = []
    for end, at in enumerate((0, CX - 8)):
        rows = pl.ds(at, 8)
        loads.append(pltpu.make_async_copy(stress.at[:, :, rows, :], F.at[end, pl.ds(0, 6)], sems.at[3 * end]))
        loads.append(pltpu.make_async_copy(vel.at[:, :, rows, :], F.at[end, pl.ds(6, 3)], sems.at[3 * end + 1]))
        loads.append(pltpu.make_async_copy(zones.at[:, rows, :], Z.at[end], sems.at[3 * end + 2]))
    small = ((regional_in, regional), (table_in, table), (building_in, building), (block_in, block))
    loads += [pltpu.make_async_copy(src, dst, sems.at[6 + k]) for k, (src, dst) in enumerate(small)]
    for copy in loads:
        copy.start()
    for copy in loads:
        copy.wait()

    for f in range(FIELDS):
        for q in range(NZ // 2):
            tiles = [F[end, f, z] if f < 9 else Z[end, z].astype(F32) for end in range(2) for z in (2 * q, 2 * q + 1)]
            first = jnp.where(low, tiles[0], roll(tiles[1], 4, 0))
            last = jnp.where(low, roll(tiles[3], 4, 0), tiles[2])
            gxa[f * 4 + q] = jnp.where(even_x, last, first)
            gxb[f * 4 + q] = jnp.where(even_x, first, last)


def cols_kernel(vel, stress, zones, S, V, gya, gyb, sems):
    even_y = (lax.axis_index("gy") & 1) == 0
    inner = pl.ds(0, CX)
    loads = [
        pltpu.make_async_copy(stress, S.at[:, :, inner, :], sems.at[0]),
        pltpu.make_async_copy(vel, V.at[:, :, inner, :], sems.at[1]),
    ]
    for copy in loads:
        copy.start()
    slot = iota((CX, CY), 1) // HALO

    def plane(f, z):
        if f < 6:
            return stress[f, z]
        if f < 9:
            return vel[f - 6, z]
        return zones[z].astype(F32)

    for p in range(PACKS):
        lasts = jnp.zeros((CX, CY), F32)
        firsts = jnp.zeros((CX, CY), F32)
        for s in range(4):
            f = 4 * p + s
            if f >= FIELDS:
                continue
            for z in range(NZ):
                turned = roll(plane(f, z), 16 * z + 4 * s + 4, 1)
                at = 4 * z + s
                lasts = jnp.where(slot == at, turned, lasts)
                firsts = jnp.where(slot == (at + 1) % 32, turned, firsts)
        gya[p * CX:(p + 1) * CX, :] = jnp.where(even_y, lasts, firsts)
        gyb[p * CX:(p + 1) * CX, :] = jnp.where(even_y, firsts, lasts)

    for copy in loads:
        copy.wait()


def split(count):
    return [(4 * (k // 2) + k % 2, 2) for k in range(count // 2)]


def slices_kernel(n_gx, n_gy, R, owner, source, sent, kept, slices):
    gy = lax.axis_index("gy")
    row = iota((CHUNK, CY), 0)
    edge = (iota((CHUNK, CY), 1) >= 96) & ((row & 7) >= 6)
    sides = jnp.where(row < CXC, owner[(gy + n_gy - 1) % n_gy], owner[(gy + 1) % n_gy])
    source[...] = jnp.where(edge, sides, owner[gy])
    part = iota((n_gx, CY), 1) // CYC
    for s in range(STEPS):
        halves = [[R[0, s, c, :, t * CY:(t + 1) * CY] for t in range(2)] for c in range(3)]
        for r in range(CXC):
            turned = jnp.zeros((n_gx, CY), F32)
            for c in range(3):
                turned = jnp.where(part == c, roll(halves[c][r // 4], CYC * (c - r % 4), 1), turned)
            if r < 3:
                turned = jnp.where(part == 3, roll(roll(halves[r][0], n_gx - 1, 0), 96, 1), turned)
            elif r < 6:
                turned = jnp.where(part == 3, roll(halves[r - 3][1], 1, 0), turned)
            slices[pl.ds(s * CXC + r, n_gx, stride=CHUNK), :] = turned
    bit = (lax.axis_index("gx") >> 1) & 1
    for k, (at, step) in enumerate(split(n_gx)):
        for out, side in ((sent, 1 - bit), (kept, bit)):
            out[k] = slices[pl.ds(pl.multiple_of((at + step * side) * CHUNK, CHUNK), CHUNK), :]


def trade_kernel(width, got, kept, source, sent, kept_out, held):
    gx = lax.axis_index("gx")
    mine = ((source[...] ^ gx) & width) == 0
    count = got.shape[0]
    for i in range(count):
        held[i] = jnp.where(mine, kept[i], got[i])
    bit = (gx & (2 * width)) // (2 * width)
    for k, (at, step) in enumerate(split(count)):
        sent[k] = held[at + step * (1 - bit)]
        kept_out[k] = held[at + step * bit]


def ends_kernel(width, got, kept, source, pair, ta, tb):
    even_y = (lax.axis_index("gy") & 1) == 0
    mine = ((source[...] ^ lax.axis_index("gx")) & width) == 0
    lane = iota((8, CY), 1)
    sub = iota((8, CY), 0)
    digit, group = (lane - 96) % 10, (lane - 96) // 10
    row = jnp.where(digit < 8, digit, jnp.where(digit == 8, group, 3 + group))
    here = (lane >= 96) & (group < 3) & (sub == row)
    tiles = [jnp.zeros((8, CY), F32), jnp.zeros((8, CY), F32)]
    for i in range(4):
        pair[i] = jnp.where(mine, kept[i], got[i])
        for s in range(STEPS):
            tile = pair[i, s * CXC:(s + 1) * CXC, :]
            for k, col in enumerate((CYC - 1, 0)):
                idx = jnp.where(here, jnp.where(digit < 8, group * CYC, 96) + col, 0)
                ends = jnp.sum(jnp.where(here, take(tile, idx), 0.0), axis=0, keepdims=True)
                tiles[k] = jnp.where(sub == 2 * i + s, jnp.broadcast_to(ends, (8, CY)), tiles[k])
    ta[...] = jnp.where(even_y, tiles[0], tiles[1])
    tb[...] = jnp.where(even_y, tiles[1], tiles[0])


def edges_kernel(width, quad, tca, tcb, own, sent, kept):
    even_y = (lax.axis_index("gy") & 1) == 0
    bit = (lax.axis_index("gx") & width) // width
    beside = iota((1, CY), 1) >= 96
    for k, (first, step) in enumerate(split(4)):
        for out, side in ((sent, 1 - bit), (kept, bit)):
            at = first + step * side
            out[k] = quad[at]
            for s in range(STEPS):
                a, b = tca[PACKS, pl.ds(2 * at + s, 1), :], tcb[PACKS, pl.ds(2 * at + s, 1), :]
                for j, ends in enumerate((jnp.where(even_y, b, a), jnp.where(even_y, a, b))):
                    put = j * CXC + 6 + s
                    out[k, put:put + 1, :] = jnp.where(beside, ends, out[k, put:put + 1, :])


def spread_table(table):
    scaled = table[...] * 0.1
    spread = jnp.concatenate([scaled] * (CY // ZONES), axis=1)
    return [spread[k:k + 1, :] for k in range(3)]


def material_kernel(zones, zone_tail, table, LAM, MU, BUOY):
    columns = [jnp.broadcast_to(row, (RING, CY)) for row in spread_table(table)]
    for z in range(NZ):
        ids = jnp.concatenate([zones[z], zone_tail[z].astype(jnp.int32)], axis=0)
        for k, ref in enumerate((LAM, MU, BUOY)):
            ref[z] = take(columns[k], ids)


XX, XZ, XY, YY, YZ, ZZ = range(6)


def dx(x):
    return roll(x, RING - 1, 0) - roll(x, 1, 0)


def dy(x, seam, z):
    lane = iota((RING, CY), 1)
    if seam is None:
        return jnp.where(lane == CY - 1, 0.0, roll(x, CY - 1, 1)) - jnp.where(lane == 0, 0.0, roll(x, 1, 1))
    seam = roll(seam, -(16 * z + 3), 1)
    return jnp.where(lane == CY - 1, seam, roll(x, CY - 1, 1)) - jnp.where(lane == 0, seam, roll(x, 1, 1))


def dz(ref, f, z):
    if z == 0:
        return ref[f, 1]
    if z == NZ - 1:
        return -ref[f, NZ - 2]
    return ref[f, z + 1] - ref[f, z - 1]


def band_dy(x):
    return roll(x, CY - 1, 1) - roll(x, 1, 1)


def band_dz(x):
    lane = iota((RING, CY), 1)
    return jnp.where(lane < CY - 16, roll(x, CY - 16, 1), 0.0) - jnp.where(lane >= 16, roll(x, 16, 1), 0.0)


def seams(band, fields):
    lane = iota((RING, CY), 1)
    return {f: jnp.where(lane % 16 == 2, roll(band[f], -10, 1), band[f]) for f in fields}


def velocity_planes(planes, S, V, MU, BUOY, band, drm):
    seam = {XY: None, YY: None, YZ: None} if band is None else seams(band, (XY, YY, YZ))
    for z in planes:
        sxy, sxz, syz = S[XY, z], S[XZ, z], S[YZ, z]
        force = [
            dx(S[XX, z]) + dy(sxy, seam[XY], z) + dz(S, XZ, z),
            dx(sxy) + dy(S[YY, z], seam[YY], z) + dz(S, YZ, z),
            dx(sxz) + dy(syz, seam[YZ], z) + dz(S, ZZ, z),
        ]
        if z == NZ - 1:
            force = [force[c] + (20.0 * MU[z]) * drm(c, 0) for c in range(3)]
        for c in range(3):
            V[c, z] = V[c, z] + BUOY[z] * force[c]


def velocity_seams(planes, V, BUOY, band):
    lane = iota((RING, CY), 1)
    sign = jnp.where(lane == 0, -1.0, jnp.where(lane == CY - 1, 1.0, 0.0))
    seam = seams(band, (XY, YY, YZ))
    for z in planes:
        scale = BUOY[z] * sign
        for c, f in enumerate((XY, YY, YZ)):
            V[c, z] = V[c, z] + scale * roll(seam[f], -(16 * z + 3), 1)


def velocity_band(band, new, BM, drm):
    sxy, sxz, syz = band[XY], band[XZ], band[YZ]
    force = [
        dx(band[XX]) + band_dy(sxy) + band_dz(sxz),
        dx(sxy) + band_dy(band[YY]) + band_dz(syz),
        dx(sxz) + band_dy(syz) + band_dz(band[ZZ]),
    ]
    for c in range(3):
        if drm is not None:
            force[c] = force[c] + (20.0 * BM[1]) * drm(c, 1)
        new[6 + c] = band[6 + c] + BM[2] * force[c]


def stress_plane(z, seam, S, V, LAM, MU, fields):
    vx, vy, vz = V[0, z], V[1, z], V[2, z]
    mu = MU[z]
    if XX in fields:
        lam = LAM[z]
        xx, yy, zz = dx(vx), dy(vy, seam[7], z), dz(V, 2, z)
        theta = lam * (xx + yy + zz)
        two = mu + mu
        S[XX, z] = S[XX, z] + (theta + two * xx)
        S[YY, z] = S[YY, z] + (theta + two * yy)
        S[ZZ, z] = S[ZZ, z] + (theta + two * zz)
    if XZ in fields:
        S[XZ, z] = S[XZ, z] + mu * (dz(V, 0, z) + dx(vz))
    if XY in fields:
        S[XY, z] = S[XY, z] + mu * (dy(vx, seam[6], z) + dx(vy))
    if YZ in fields:
        S[YZ, z] = S[YZ, z] + mu * (dz(V, 1, z) + dy(vz, seam[8], z))


def stress_band(band, new, BM):
    vx, vy, vz = new[6], new[7], new[8]
    lam, mu = BM[0], BM[1]
    xx, yy, zz = dx(vx), band_dy(vy), band_dz(vz)
    theta = lam * (xx + yy + zz)
    two = mu + mu
    new[XX] = band[XX] + (theta + two * xx)
    new[YY] = band[YY] + (theta + two * yy)
    new[ZZ] = band[ZZ] + (theta + two * zz)
    new[XZ] = band[XZ] + mu * (band_dz(vx) + dx(vz))
    new[XY] = band[XY] + mu * (band_dy(vx) + dx(vy))
    new[YZ] = band[YZ] + mu * (band_dz(vy) + band_dy(vz))


ALL = (XX, XZ, XY, YY, YZ, ZZ)


def unpack_kernel(
    S_in, V_in, ra, rb, ends_a, ends_b, ca, cb,
    S, V, zone_tail, ta, tb,
):
    even_x = (lax.axis_index("gx") & 1) == 0
    even_y = (lax.axis_index("gy") & 1) == 0
    low = iota((8, CY), 0) < 4
    slot = iota((8, CY), 1) // HALO
    tail = slice(CX, RING)
    for p in range(PACKS):
        lasts = jnp.zeros((8, CY), F32)
        firsts = jnp.zeros((8, CY), F32)
        for s in range(4):
            f = 4 * p + s
            if f >= FIELDS:
                continue
            for q in range(NZ // 2):
                k = f * 4 + q
                after = jnp.where(even_x, ra[k], rb[k])
                before = jnp.where(even_x, rb[k], ra[k])
                both = (jnp.where(low, after, before), roll(jnp.where(low, before, after), 4, 0))
                for z in (2 * q, 2 * q + 1):
                    rows = both[z % 2]
                    turned = roll(rows, 16 * z + 4 * s + 4, 1)
                    at = 4 * z + s
                    lasts = jnp.where(slot == at, turned, lasts)
                    firsts = jnp.where(slot == (at + 1) % 32, turned, firsts)
                    if f < 6:
                        S[f, z, tail, :] = rows
                    elif f < 9:
                        V[f - 6, z, tail, :] = rows
                    else:
                        zone_tail[z] = rows
        ta[p] = jnp.where(even_y, lasts, firsts)
        tb[p] = jnp.where(even_y, firsts, lasts)
    ta[PACKS] = ends_a[...]
    tb[PACKS] = ends_b[...]


def inner_kernel(S, V_in, MU, BUOY, own_a, own_b, ta, tb, V, own):
    even_y = (lax.axis_index("gy") & 1) == 0
    quarter = (iota((RING, CY), 1) // 4) % 4
    for p in range(PACKS):
        at = slice(p * CX, (p + 1) * CX)
        one, two = jnp.concatenate([own_a[at], ta[p]], axis=0), jnp.concatenate([own_b[at], tb[p]], axis=0)
        last, first = jnp.where(even_y, one, two), jnp.where(even_y, two, one)
        for s in range(4):
            if 4 * p + s < FIELDS:
                own[4 * p + s] = jnp.where(quarter == 1, roll(first, -4 * s, 1), roll(last, 8 - 4 * s, 1))
    velocity_planes(range(0, 5), S, V, MU, BUOY, None, None)


def cone_kernel(
    S_in, V_in, LAM, MU, BUOY, table, own, ca, cb, tca, tcb, building, block,
    S, V, BF, BM, BV, BW, shares,
):
    even_y = (lax.axis_index("gy") & 1) == 0
    lane8 = iota((8, CY), 1)
    sub8 = iota((8, CY), 0)
    quarter = (iota((RING, CY), 1) // 4) % 4
    columns = spread_table(table)

    for p in range(PACKS):
        at = slice(p * CX, (p + 1) * CX)
        one, two = jnp.concatenate([ca[at], tca[p]], axis=0), jnp.concatenate([cb[at], tcb[p]], axis=0)
        from_right, from_left = jnp.where(even_y, one, two), jnp.where(even_y, two, one)
        for s in range(4):
            f = 4 * p + s
            if f < FIELDS:
                BF[f] = jnp.where(
                    quarter == 0, roll(from_left, -4 * s, 1),
                    jnp.where(quarter == 3, roll(from_right, 8 - 4 * s, 1), own[f]),
                )
    ids = BF[9].astype(jnp.int32)
    for k in range(3):
        BM[k] = take(jnp.broadcast_to(columns[k], (RING, CY)), ids)

    velocity_seams(range(0, 5), V, BUOY, BF)
    velocity_band(BF, BW, BM, None)
    for c in range(3):
        BV[c] = BW[6 + c]
    seam = seams(BW, (6, 7, 8))
    for z in range(0, 4):
        stress_plane(z, seam, S, V, LAM, MU, ALL)
    stress_band(BF, BW, BM)
    velocity_planes(range(0, 3), S, V, MU, BUOY, BW, None)
    velocity_band(BW, BW, BM, None)
    stress_plane(1, seams(BW, (8,)), S, V, LAM, MU, (XZ, YZ))

    total = jnp.zeros((8, CY), F32)
    for c, f in enumerate((XZ, YZ)):
        for r in range(CX // BLOCK):
            row = jnp.sum(S[f, 1, 8 * r:8 * r + 8, :], axis=0, keepdims=True)
            total = jnp.where(sub8 == 4 * c + r, jnp.broadcast_to(row, (8, CY)), total)
    for shift in (1, 2, 4):
        total = total + roll(total, CY - shift, 1)
    total = total * (1.0 / (BLOCK * BLOCK))
    ids = jnp.broadcast_to(jnp.concatenate([block[0], block[0]], axis=1), (8, CY))
    cells = CY // BLOCK
    picked = take(total, (ids % cells) * BLOCK)
    mine = (sub8 % 4 == ids // cells) & (sub8 // 4 == lane8 // FP_DEV)
    values = jnp.sum(jnp.where(mine, picked, 0.0), axis=0, keepdims=True)
    names = jnp.concatenate([building[0], building[0]], axis=1).astype(F32)
    message = jnp.concatenate([values, names], axis=0)
    shares[...] = jnp.broadcast_to(message[None], shares.shape)


def upper_kernel(S_in, V_in, LAM, MU, BUOY, BF, BV, BW, S, V):
    velocity_planes(range(5, 7), S, V, MU, BUOY, BF, None)
    seam = {6 + c: value for c, value in seams(BV, range(3)).items()}
    for z in range(4, 6):
        stress_plane(z, seam, S, V, LAM, MU, ALL)
    velocity_planes(range(3, 5), S, V, MU, BUOY, BW, None)
    seam = seams(BW, (6, 7, 8))
    for z in range(0, 4):
        stress_plane(z, seam, S, V, LAM, MU, (XX, XY) if z == 1 else ALL)


def lower_kernel(
    S_in, V_in, LAM, MU, BUOY, BF_in, BM, source, got, kept,
    S, V, BF, vel_out, stress_out, DRM, drm_in, sems,
):
    saves = []

    def save(ref, out, first, count):
        at = pl.ds(first, count)
        copy = pltpu.make_async_copy(ref.at[:, at, pl.ds(0, CX), :], out.at[:, at], sems.at[len(saves)])
        copy.start()
        saves.append(copy)

    save(V, vel_out, 0, 5)
    save(S, stress_out, 0, 4)
    low = iota((8, CY), 0) < 4
    lane8 = iota((8, CY), 1)
    quarter8 = (lane8 // 4) % 4
    deepest = lane8 >= 16 * (NZ - 1)

    mine = ((source[...] ^ lax.axis_index("gx")) & 1) == 0
    drm_in[...] = jnp.where(mine, kept[0], got[0])

    def wide(row):
        return jnp.broadcast_to(drm_in[row:row + 1, :], (8, CY))

    for s in range(STEPS):
        both = jnp.where(lane8 >= 96, wide(6 + s), roll(wide(CXC + 6 + s), 32, 1))
        for c in range(3):
            for q in range(RING // 8):
                if q < 4:
                    rows = jnp.where(low, wide(s * CXC + 2 * q), wide(s * CXC + 2 * q + 1))
                    base = c * CYC
                else:
                    rows = jnp.where(low, wide(s * CXC + c), wide(s * CXC + 3 + c))
                    base = 3 * CYC
                DRM[s, c, 0, 8 * q:8 * q + 8, :] = take(rows, base + lane8 // COARSE)
                inner = take(rows, base + jnp.where(quarter8 == 2, CYC - 1, 0))
                at = c * 10 + 2 * q + jnp.where(low, 0, 1) + jnp.where(quarter8 == 0, 96, 0)
                value = jnp.where((quarter8 & 1) == (quarter8 >> 1), take(both, at), inner)
                DRM[s, c, 1, 8 * q:8 * q + 8, :] = jnp.where(deepest, value, 0.0)

    def drm(step):
        return lambda c, k: DRM[step, c, k]

    velocity_planes(range(7, NZ), S, V, MU, BUOY, BF, drm(0))
    velocity_band(BF, BF, BM, drm(0))
    seam = seams(BF, (6, 7, 8))
    for z in range(6, NZ):
        stress_plane(z, seam, S, V, LAM, MU, ALL)
    stress_band(BF, BF, BM)
    velocity_planes(range(5, NZ), S, V, MU, BUOY, BF, drm(1))
    velocity_band(BF, BF, BM, drm(1))
    save(V, vel_out, 5, NZ - 5)
    seam = seams(BF, (6, 7, 8))
    for z in range(4, NZ):
        stress_plane(z, seam, S, V, LAM, MU, ALL)
        save(S, stress_out, z, 1)
    for copy in saves:
        copy.wait()


def sum_kernel(n, shares, out):
    half = n // 2
    low = iota((half, CY), 1) < FP_DEV
    values = shares[:, 0, :]
    names = shares[:, 1, :].astype(jnp.int32)
    entry = [
        jnp.where(low, values[:half], roll(values[half:], FP_DEV, 1)),
        jnp.where(low, roll(values[:half], FP_DEV, 1), values[half:]),
    ]
    names = jnp.where(low, names[:half], names[half:])
    high = names // CY
    names = names % CY
    n_high = BUILDINGS // CY
    rows = iota((n_high, CY), 0)
    wanted = iota((CY, CY), 0)
    acc = jnp.zeros((6 * n_high, CY), F32)
    for k in range(half):
        hot = (jnp.broadcast_to(names[k:k + 1], (CY, CY)) == wanted).astype(F32).astype(jnp.bfloat16)
        here = jnp.broadcast_to(high[k:k + 1], (n_high, CY)) == rows
        left = []
        for c in range(2):
            rest = jnp.where(here, jnp.broadcast_to(entry[c][k:k + 1], (n_high, CY)), 0.0)
            for _ in range(3):
                piece = rest.astype(jnp.bfloat16)
                rest = rest - piece.astype(F32)
                left.append(piece.astype(F32))
        left = jnp.concatenate(left, axis=0).astype(jnp.bfloat16)
        acc = acc + lax.dot_general(left, hot, (((1,), (1,)), ((), ())), preferred_element_type=F32)
    sums = []
    for c in range(2):
        base = 3 * c * n_high
        sums.append(acc[base:base + n_high] + acc[base + n_high:base + 2 * n_high] + acc[base + 2 * n_high:base + 3 * n_high])
    for h in range(n_high):
        out[:, h * CY:(h + 1) * CY] = jnp.concatenate([sums[0][h:h + 1], sums[1][h:h + 1]], axis=0)


def pairs_near(n):
    return [(i, i ^ 1) for i in range(n)]


def pairs_far(n):
    return [(i, (i + 1) % n if i % 2 else (i - 1) % n) for i in range(n)]


def after(x, *done):
    return lax.optimization_barrier((x,) + done)[0]


def body(n_gx, n_gy, velocity, stress, zones, zone_table, regional, owner, building, block):
    n = n_gx * n_gy
    gx = lax.axis_index("gx")
    vmem = pl.BlockSpec(memory_space=pltpu.VMEM)
    hbm = pl.BlockSpec(memory_space=pltpu.HBM)
    anywhere = pl.BlockSpec(memory_space=pl.ANY)
    params = pltpu.CompilerParams(vmem_limit_bytes=VMEM_LIMIT)

    def shaped(*shape):
        return jax.ShapeDtypeStruct(shape, F32)

    def whole(shape, dtype):
        return jax.ShapeDtypeStruct(shape, dtype)

    s_ring = shaped(6, NZ, RING, CY)
    v_ring = shaped(3, NZ, RING, CY)
    m_ring = shaped(NZ, RING, CY)
    rows = shaped(FIELDS * 4, 8, CY)
    cols = shaped(COLS, CY)
    from_hbm = [
        pltpu.with_memory_space_constraint(x, pltpu.HBM)
        for x in (velocity, stress, zones, regional, zone_table, building, block)
    ]
    gxa, gxb, regional, zone_table, building, block = pl.pallas_call(
        rows_kernel,
        out_shape=(
            rows, rows, whole(regional.shape, F32), whole(zone_table.shape, F32),
            whole(building.shape, jnp.int32), whole(block.shape, jnp.int32),
        ),
        in_specs=[hbm] * 7,
        out_specs=(vmem,) * 6,
        scratch_shapes=[
            pltpu.VMEM((2, 9, NZ, 8, CY), F32),
            pltpu.VMEM((2, NZ, 8, CY), jnp.int32),
            pltpu.SemaphoreType.DMA((10,)),
        ],
        compiler_params=params,
        name="pack_rows",
    )(*from_hbm)
    rb = lax.ppermute(gxb, "gx", pairs_far(n_gx))
    ra = lax.ppermute(gxa, "gx", pairs_near(n_gx))
    S, V, gya, gyb = pl.pallas_call(
        cols_kernel,
        out_shape=(s_ring, v_ring, cols, cols),
        in_specs=[vmem] * 3,
        out_specs=(vmem,) * 4,
        scratch_shapes=[pltpu.SemaphoreType.DMA((2,))],
        compiler_params=params,
        name="pack_columns",
    )(velocity, stress, zones)
    cb = lax.ppermute(gyb, "gy", pairs_far(n_gy))
    ca = lax.ppermute(gya, "gy", pairs_near(n_gy))

    def across(x, width):
        return lax.ppermute(x, "gx", [(i, i ^ width) for i in range(n_gx)])

    half = shaped(n_gx // 2, CHUNK, CY)
    source, sent, kept = pl.pallas_call(
        functools.partial(slices_kernel, n_gx, n_gy),
        out_shape=(whole((CHUNK, CY), jnp.int32), half, half),
        in_specs=[vmem, pl.BlockSpec(memory_space=pltpu.SMEM)],
        out_specs=(vmem,) * 3,
        scratch_shapes=[pltpu.VMEM((n_gx * CHUNK, CY), F32)],
        compiler_params=params,
        name="slices",
    )(regional, owner)
    width = 2
    while 4 * width < n_gx:
        count = sent.shape[0]
        part = shaped(count // 2, CHUNK, CY)
        sent, kept = pl.pallas_call(
            functools.partial(trade_kernel, width),
            out_shape=(part, part),
            in_specs=[vmem] * 3,
            out_specs=(vmem,) * 2,
            scratch_shapes=[pltpu.VMEM((count, CHUNK, CY), F32)],
            compiler_params=params,
            name="trade",
        )(across(sent, width), kept, source)
        width *= 2
    tile = shaped(8, CY)
    quad, ends_a, ends_b = pl.pallas_call(
        functools.partial(ends_kernel, width),
        out_shape=(shaped(4, CHUNK, CY), tile, tile),
        in_specs=[vmem] * 3,
        out_specs=(vmem,) * 3,
        compiler_params=params,
        name="ends",
    )(across(sent, width), kept, source)
    ends = shaped(PACKS + 1, 8, CY)
    S, V, zone_tail, ta, tb = pl.pallas_call(
        unpack_kernel,
        out_shape=(s_ring, v_ring, shaped(NZ, 8, CY), ends, ends),
        in_specs=[vmem] * 6 + [anywhere] * 2,
        out_specs=(vmem,) * 5,
        input_output_aliases={0: 0, 1: 1},
        compiler_params=params,
        name="unpack",
    )(S, V, ra, rb, ends_a, ends_b, ca, cb)
    tcb = lax.ppermute(tb, "gy", pairs_far(n_gy))
    tca = lax.ppermute(ta, "gy", pairs_near(n_gy))
    LAM, MU, BUOY = pl.pallas_call(
        material_kernel,
        out_shape=(m_ring,) * 3,
        in_specs=[vmem] * 3,
        out_specs=(vmem,) * 3,
        compiler_params=params,
        name="materials",
    )(zones, zone_tail, zone_table)
    V, own = pl.pallas_call(
        inner_kernel,
        out_shape=(v_ring, shaped(FIELDS, RING, CY)),
        in_specs=[vmem] * 8,
        out_specs=(vmem,) * 2,
        input_output_aliases={1: 0},
        compiler_params=params,
        name="inner",
    )(S, V, MU, BUOY, gya, gyb, ta, tb)
    two = shaped(2, CHUNK, CY)
    width *= 2
    sent, kept = pl.pallas_call(
        functools.partial(edges_kernel, width),
        out_shape=(two, two),
        in_specs=[vmem] * 3 + [anywhere],
        out_specs=(vmem,) * 2,
        compiler_params=params,
        name="edges",
    )(quad, tca, tcb, own)
    band = shaped(3, RING, CY)
    S, V, BF, BM, BV, BW, shares = pl.pallas_call(
        cone_kernel,
        out_shape=(s_ring, v_ring, shaped(FIELDS, RING, CY), band, band, shaped(9, RING, CY), shaped(n, 2, CY)),
        in_specs=[vmem] * 13,
        out_specs=(vmem,) * 7,
        input_output_aliases={0: 0, 1: 1},
        compiler_params=params,
        name="cone",
    )(S, V, LAM, MU, BUOY, zone_table, own, ca, cb, tca, tcb, building, block)
    held = jnp.where(((source ^ gx) & width) == 0, kept, across(sent, width))
    odd = (gx & 1) != 0
    sent, kept = jnp.where(odd, held[0], held[1])[None], jnp.where(odd, held[1], held[0])[None]
    got = across(sent, 1)
    every = lax.all_to_all(shares, ("gx", "gy"), 0, 0)
    S, V = pl.pallas_call(
        upper_kernel,
        out_shape=(s_ring, v_ring),
        in_specs=[vmem] * 8,
        out_specs=(vmem,) * 2,
        input_output_aliases={0: 0, 1: 1},
        compiler_params=params,
        name="upper",
    )(S, V, LAM, MU, BUOY, BF, BV, BW)
    shear = pl.pallas_call(
        functools.partial(sum_kernel, n),
        out_shape=shaped(2, BUILDINGS),
        in_specs=[vmem],
        out_specs=vmem,
        compiler_params=params,
        name="sum_by_building",
    )(every)
    _, _, _, vel_out, stress_out = pl.pallas_call(
        lower_kernel,
        out_shape=(s_ring, v_ring, shaped(FIELDS, RING, CY), shaped(*velocity.shape), shaped(*stress.shape)),
        in_specs=[vmem] * 10,
        out_specs=(vmem, vmem, vmem, hbm, hbm),
        scratch_shapes=[
            pltpu.VMEM((STEPS, 3, 2, RING, CY), F32),
            pltpu.VMEM((CHUNK, CY), F32),
            pltpu.SemaphoreType.DMA((NZ,)),
        ],
        input_output_aliases={0: 0, 1: 1, 5: 2},
        compiler_params=params,
        name="lower",
    )(S, V, LAM, MU, BUOY, BF, BM, source, got, kept)
    return vel_out, stress_out, shear


def solution(mesh):
    n_gx, n_gy = mesh.shape["gx"], mesh.shape["gy"]
    return jax.shard_map(
        functools.partial(body, n_gx, n_gy),
        mesh=mesh,
        in_specs=(
            P(None, None, "gx", "gy"),
            P(None, None, "gx", "gy"),
            P(None, "gx", "gy"),
            P(),
            P("gx", None, None, None, "gy"),
            P(),
            P("gx", "gy", None),
            P("gx", "gy", None),
        ),
        out_specs=(P(None, None, "gx", "gy"), P(None, None, "gx", "gy"), P()),
        check_vma=False,
    )
```

```python
import functools

import jax
import jax.numpy as jnp
from jax import lax
from jax.experimental import pallas as pl
from jax.experimental.pallas import tpu as pltpu
from jax.sharding import PartitionSpec as P

CX = 32
CY = 128
NZ = 8
STEPS = 2
COARSE = 4
BLOCK = 8
ZONES = 16
BUILDINGS = 1024
FP_DEV = 64
HALO = 4
RING = CX + 2 * HALO
FIELDS = 10
WIDE = 3
ROWS_AT = WIDE * 4 * 8
ROWS = ROWS_AT + (FIELDS - WIDE) * 3 * 8
PACKS = 3
CHUNK = 16
COLS = PACKS * CX
CXC = CX // COARSE
CYC = CY // COARSE
F32 = jnp.float32
VMEM_LIMIT = 32 * 1024 * 1024


def iota(shape, dim):
    return lax.broadcasted_iota(jnp.int32, shape, dim)


def take(x, idx):
    idx = jnp.broadcast_to(idx, x.shape)
    return jnp.take_along_axis(x, idx, axis=1, mode="promise_in_bounds")


def roll(x, shift, axis):
    size = x.shape[axis]
    shift = shift % size
    return x if shift == 0 else pltpu.roll(x, shift, axis)


def rows_kernel(
    vel, stress, zones, regional_in, table_in, building_in, block_in,
    gxa, gxb, regional, table, building, block, F, Z, sems,
):
    even_x = (lax.axis_index("gx") & 1) == 0
    low = iota((8, CY), 0) < 4
    loads = []
    for end, at in enumerate((0, CX - 8)):
        rows = pl.ds(at, 8)
        loads.append(pltpu.make_async_copy(stress.at[:, :, rows, :], F.at[end, pl.ds(0, 6)], sems.at[3 * end]))
        loads.append(pltpu.make_async_copy(vel.at[:, :, rows, :], F.at[end, pl.ds(6, 3)], sems.at[3 * end + 1]))
        loads.append(pltpu.make_async_copy(zones.at[:, rows, :], Z.at[end], sems.at[3 * end + 2]))
    small = ((regional_in, regional), (table_in, table), (building_in, building), (block_in, block))
    loads += [pltpu.make_async_copy(src, dst, sems.at[6 + k]) for k, (src, dst) in enumerate(small)]
    for copy in loads:
        copy.start()
    for copy in loads:
        copy.wait()

    def tile(f, z, end):
        return F[end, f, z] if f < 9 else Z[end, z].astype(F32)

    for f in range(WIDE):
        for q in range(NZ // 2):
            first = jnp.where(low, tile(f, 2 * q, 0), roll(tile(f, 2 * q + 1, 0), 4, 0))
            last = jnp.where(low, roll(tile(f, 2 * q + 1, 1), 4, 0), tile(f, 2 * q, 1))
            at = 8 * (f * 4 + q)
            gxa[at:at + 8, :] = jnp.where(even_x, last, first)
            gxb[at:at + 8, :] = jnp.where(even_x, first, last)
    for f in range(WIDE, FIELDS):
        for z in range(NZ):
            first, last = tile(f, z, 0), roll(tile(f, z, 1), 3, 0)
            at = pl.ds(ROWS_AT + (f - WIDE) * 24 + z, 3, stride=8)
            gxa[at, :] = jnp.where(even_x, last, first)[0:3]
            gxb[at, :] = jnp.where(even_x, first, last)[0:3]


def own_band(own, p, at, lasts, firsts):
    inner = (iota(lasts.shape, 1) // 4) % 4 == 1
    for s in range(4):
        if 4 * p + s < FIELDS:
            own[4 * p + s, at, :] = jnp.where(inner, roll(firsts, -4 * s, 1), roll(lasts, 8 - 4 * s, 1))


def cols_kernel(vel, stress, zones, S, V, gya, gyb, own, sems):
    even_y = (lax.axis_index("gy") & 1) == 0
    inner = pl.ds(0, CX)
    loads = [
        pltpu.make_async_copy(stress, S.at[:, :, inner, :], sems.at[0]),
        pltpu.make_async_copy(vel, V.at[:, :, inner, :], sems.at[1]),
    ]
    for copy in loads:
        copy.start()
    slot = iota((CX, CY), 1) // HALO

    def plane(f, z):
        if f < 6:
            return stress[f, z]
        if f < 9:
            return vel[f - 6, z]
        return zones[z].astype(F32)

    for p in range(PACKS):
        lasts = jnp.zeros((CX, CY), F32)
        firsts = jnp.zeros((CX, CY), F32)
        for s in range(4):
            f = 4 * p + s
            if f >= FIELDS:
                continue
            for z in range(NZ):
                turned = roll(plane(f, z), 16 * z + 4 * s + 4, 1)
                at = 4 * z + s
                lasts = jnp.where(slot == at, turned, lasts)
                firsts = jnp.where(slot == (at + 1) % 32, turned, firsts)
        own_band(own, p, slice(0, CX), lasts, firsts)
        gya[p * CX:(p + 1) * CX, :] = jnp.where(even_y, lasts, firsts)
        gyb[p * CX:(p + 1) * CX, :] = jnp.where(even_y, firsts, lasts)

    for copy in loads:
        copy.wait()


def split(count):
    return [(4 * (k // 2) + k % 2, 2) for k in range(count // 2)]


def slices_kernel(n_gx, n_gy, R, owner, source, sent, kept, slices):
    gy = lax.axis_index("gy")
    row = iota((CHUNK, CY), 0)
    edge = (iota((CHUNK, CY), 1) >= 96) & ((row & 7) >= 6)
    sides = jnp.where(row < CXC, owner[(gy + n_gy - 1) % n_gy], owner[(gy + 1) % n_gy])
    source[...] = jnp.where(edge, sides, owner[gy])
    part = iota((n_gx, CY), 1) // CYC
    for s in range(STEPS):
        halves = [[R[0, s, c, :, t * CY:(t + 1) * CY] for t in range(2)] for c in range(3)]
        for r in range(CXC):
            turned = jnp.zeros((n_gx, CY), F32)
            for c in range(3):
                turned = jnp.where(part == c, roll(halves[c][r // 4], CYC * (c - r % 4), 1), turned)
            if r < 3:
                turned = jnp.where(part == 3, roll(roll(halves[r][0], n_gx - 1, 0), 96, 1), turned)
            elif r < 6:
                turned = jnp.where(part == 3, roll(halves[r - 3][1], 1, 0), turned)
            slices[pl.ds(s * CXC + r, n_gx, stride=CHUNK), :] = turned
    bit = (lax.axis_index("gx") >> 1) & 1
    for k, (at, step) in enumerate(split(n_gx)):
        for out, side in ((sent, 1 - bit), (kept, bit)):
            out[k] = slices[pl.ds(pl.multiple_of((at + step * side) * CHUNK, CHUNK), CHUNK), :]


def trade_kernel(width, got, kept, source, sent, kept_out, held):
    gx = lax.axis_index("gx")
    mine = ((source[...] ^ gx) & width) == 0
    count = got.shape[0]
    for i in range(count):
        held[i] = jnp.where(mine, kept[i], got[i])
    bit = (gx & (2 * width)) // (2 * width)
    for k, (at, step) in enumerate(split(count)):
        sent[k] = held[at + step * (1 - bit)]
        kept_out[k] = held[at + step * bit]


def ends_kernel(width, got, kept, source, gya, gyb, made, pair, ta, tb):
    ta[0:COLS] = gya[...]
    tb[0:COLS] = gyb[...]
    even_y = (lax.axis_index("gy") & 1) == 0
    mine = ((source[...] ^ lax.axis_index("gx")) & width) == 0
    lane = iota((8, CY), 1)
    sub = iota((8, CY), 0)
    digit, group = (lane - 96) % 10, (lane - 96) // 10
    row = jnp.where(digit < 8, digit, jnp.where(digit == 8, group, 3 + group))
    here = (lane >= 96) & (group < 3) & (sub == row)
    tiles = [jnp.zeros((8, CY), F32), jnp.zeros((8, CY), F32)]
    for i in range(4):
        pair[i] = jnp.where(mine, kept[i], got[i])
        for s in range(STEPS):
            tile = pair[i, s * CXC:(s + 1) * CXC, :]
            for k, col in enumerate((CYC - 1, 0)):
                idx = jnp.where(here, jnp.where(digit < 8, group * CYC, 96) + col, 0)
                ends = jnp.sum(jnp.where(here, take(tile, idx), 0.0), axis=0, keepdims=True)
                tiles[k] = jnp.where(sub == 2 * i + s, jnp.broadcast_to(ends, (8, CY)), tiles[k])
    ta[COLS:COLS + 8] = jnp.where(even_y, tiles[0], tiles[1])
    tb[COLS:COLS + 8] = jnp.where(even_y, tiles[1], tiles[0])


def edges_kernel(width, quad, ca, cb, token, sent, kept):
    even_y = (lax.axis_index("gy") & 1) == 0
    bit = (lax.axis_index("gx") & width) // width
    beside = iota((1, CY), 1) >= 96
    for k, (first, step) in enumerate(split(4)):
        for out, side in ((sent, 1 - bit), (kept, bit)):
            at = first + step * side
            out[k] = quad[at]
            for s in range(STEPS):
                a, b = ca[pl.ds(COLS + 2 * at + s, 1), :], cb[pl.ds(COLS + 2 * at + s, 1), :]
                for j, ends in enumerate((jnp.where(even_y, b, a), jnp.where(even_y, a, b))):
                    put = j * CXC + 6 + s
                    out[k, put:put + 1, :] = jnp.where(beside, ends, out[k, put:put + 1, :])


def spread_table(table):
    scaled = table[...] * 0.1
    spread = jnp.concatenate([scaled] * (CY // ZONES), axis=1)
    return [spread[k:k + 1, :] for k in range(3)]


def material_kernel(zones, table, LAM, MU, BUOY, token):
    token[...] = jnp.zeros(token.shape, F32)
    columns = [jnp.broadcast_to(row, (CX, CY)) for row in spread_table(table)]
    for z in range(NZ):
        ids = zones[z]
        for k, ref in enumerate((LAM, MU, BUOY)):
            ref[z, 0:CX, :] = take(columns[k], ids)


XX, XZ, XY, YY, YZ, ZZ = range(6)


def dx(x):
    return roll(x, RING - 1, 0) - roll(x, 1, 0)


def dy(x, seam, z):
    lane = iota((RING, CY), 1)
    if seam is None:
        return jnp.where(lane == CY - 1, 0.0, roll(x, CY - 1, 1)) - jnp.where(lane == 0, 0.0, roll(x, 1, 1))
    seam = roll(seam, -(16 * z + 3), 1)
    return jnp.where(lane == CY - 1, seam, roll(x, CY - 1, 1)) - jnp.where(lane == 0, seam, roll(x, 1, 1))


def dz(ref, f, z):
    if z == 0:
        return ref[f, 1]
    if z == NZ - 1:
        return -ref[f, NZ - 2]
    return ref[f, z + 1] - ref[f, z - 1]


def band_dy(x):
    return roll(x, CY - 1, 1) - roll(x, 1, 1)


def band_dz(x):
    lane = iota((RING, CY), 1)
    return jnp.where(lane < CY - 16, roll(x, CY - 16, 1), 0.0) - jnp.where(lane >= 16, roll(x, 16, 1), 0.0)


def seams(band, fields):
    lane = iota((RING, CY), 1)
    return {f: jnp.where(lane % 16 == 2, roll(band[f], -10, 1), band[f]) for f in fields}


def velocity_planes(planes, S, V, MU, BUOY, band, drm):
    seam = {XY: None, YY: None, YZ: None} if band is None else seams(band, (XY, YY, YZ))
    for z in planes:
        sxy, sxz, syz = S[XY, z], S[XZ, z], S[YZ, z]
        force = [
            dx(S[XX, z]) + dy(sxy, seam[XY], z) + dz(S, XZ, z),
            dx(sxy) + dy(S[YY, z], seam[YY], z) + dz(S, YZ, z),
            dx(sxz) + dy(syz, seam[YZ], z) + dz(S, ZZ, z),
        ]
        if z == NZ - 1:
            force = [force[c] + (20.0 * MU[z]) * drm(c, 0) for c in range(3)]
        for c in range(3):
            V[c, z] = V[c, z] + BUOY[z] * force[c]


def velocity_seams(planes, V, BUOY, band):
    lane = iota((RING, CY), 1)
    sign = jnp.where(lane == 0, -1.0, jnp.where(lane == CY - 1, 1.0, 0.0))
    seam = seams(band, (XY, YY, YZ))
    for z in planes:
        scale = BUOY[z] * sign
        for c, f in enumerate((XY, YY, YZ)):
            V[c, z] = V[c, z] + scale * roll(seam[f], -(16 * z + 3), 1)


def velocity_band(band, new, BM, drm):
    sxy, sxz, syz = band[XY], band[XZ], band[YZ]
    force = [
        dx(band[XX]) + band_dy(sxy) + band_dz(sxz),
        dx(sxy) + band_dy(band[YY]) + band_dz(syz),
        dx(sxz) + band_dy(syz) + band_dz(band[ZZ]),
    ]
    for c in range(3):
        if drm is not None:
            force[c] = force[c] + (20.0 * BM[1]) * drm(c, 1)
        new[6 + c] = band[6 + c] + BM[2] * force[c]


def stress_plane(z, seam, S, V, LAM, MU, fields):
    vx, vy, vz = V[0, z], V[1, z], V[2, z]
    mu = MU[z]
    if XX in fields:
        lam = LAM[z]
        xx, yy, zz = dx(vx), dy(vy, seam[7], z), dz(V, 2, z)
        theta = lam * (xx + yy + zz)
        two = mu + mu
        S[XX, z] = S[XX, z] + (theta + two * xx)
        S[YY, z] = S[YY, z] + (theta + two * yy)
        S[ZZ, z] = S[ZZ, z] + (theta + two * zz)
    if XZ in fields:
        S[XZ, z] = S[XZ, z] + mu * (dz(V, 0, z) + dx(vz))
    if XY in fields:
        S[XY, z] = S[XY, z] + mu * (dy(vx, seam[6], z) + dx(vy))
    if YZ in fields:
        S[YZ, z] = S[YZ, z] + mu * (dz(V, 1, z) + dy(vz, seam[8], z))


def stress_band(band, new, BM):
    vx, vy, vz = new[6], new[7], new[8]
    lam, mu = BM[0], BM[1]
    xx, yy, zz = dx(vx), band_dy(vy), band_dz(vz)
    theta = lam * (xx + yy + zz)
    two = mu + mu
    new[XX] = band[XX] + (theta + two * xx)
    new[YY] = band[YY] + (theta + two * yy)
    new[ZZ] = band[ZZ] + (theta + two * zz)
    new[XZ] = band[XZ] + mu * (band_dz(vx) + dx(vz))
    new[XY] = band[XY] + mu * (band_dy(vx) + dx(vy))
    new[YZ] = band[YZ] + mu * (band_dz(vy) + band_dy(vz))


ALL = (XX, XZ, XY, YY, YZ, ZZ)


def unpack_kernel(
    S_in, V_in, LAM_in, MU_in, BUOY_in, own_in, table, ra, rb,
    S, V, LAM, MU, BUOY, own, ta, tb, zone_tail,
):
    even_x = (lax.axis_index("gx") & 1) == 0
    even_y = (lax.axis_index("gy") & 1) == 0
    low = iota((8, CY), 0) < 4
    slot = iota((8, CY), 1) // HALO
    tail = slice(CX, RING)
    columns = [jnp.broadcast_to(row, (8, CY)) for row in spread_table(table)]

    def place(f, z, rows, at):
        if f < 6:
            S[f, z, CX + at:CX + at + rows.shape[0], :] = rows
        elif f < 9:
            V[f - 6, z, CX + at:CX + at + rows.shape[0], :] = rows
        else:
            zone_tail[z, at:at + rows.shape[0], :] = rows

    for f in range(WIDE):
        for q in range(NZ // 2):
            at = slice(8 * (f * 4 + q), 8 * (f * 4 + q) + 8)
            after = jnp.where(even_x, ra[at], rb[at])
            before = jnp.where(even_x, rb[at], ra[at])
            place(f, 2 * q, jnp.where(low, after, before), 0)
            place(f, 2 * q + 1, roll(jnp.where(low, before, after), 4, 0), 0)
    for f in range(WIDE, FIELDS):
        for z in range(NZ):
            at = pl.ds(ROWS_AT + (f - WIDE) * 24 + z, 3, stride=8)
            a, b = ra[at, :], rb[at, :]
            place(f, z, jnp.zeros((8, CY), F32), 0)
            place(f, z, jnp.where(even_x, a, b), 0)
            place(f, z, jnp.where(even_x, b, a), 5)
    for z in range(NZ):
        ids = zone_tail[z].astype(jnp.int32)
        for column, ref in zip(columns, (LAM, MU, BUOY)):
            ref[z, tail, :] = take(column, ids)
    for p in range(PACKS):
        lasts = jnp.zeros((8, CY), F32)
        firsts = jnp.zeros((8, CY), F32)
        for s in range(4):
            f = 4 * p + s
            if f >= FIELDS:
                continue
            for z in range(NZ):
                rows = S[f, z, tail, :] if f < 6 else V[f - 6, z, tail, :] if f < 9 else zone_tail[z]
                turned = roll(rows, 16 * z + 4 * s + 4, 1)
                at = 4 * z + s
                lasts = jnp.where(slot == at, turned, lasts)
                firsts = jnp.where(slot == (at + 1) % 32, turned, firsts)
        own_band(own, p, tail, lasts, firsts)
        ta[p] = jnp.where(even_y, lasts, firsts)
        tb[p] = jnp.where(even_y, firsts, lasts)


def inner_kernel(S, V_in, MU, BUOY, V, token):
    velocity_planes(range(0, 5), S, V, MU, BUOY, None, None)
    token[...] = jnp.zeros(token.shape, F32)


def cone_kernel(
    S_in, V_in, LAM, MU, BUOY, table, own, ca, cb, tca, tcb, building, block,
    S, V, BF, BM, BV, BW, shares,
):
    even_y = (lax.axis_index("gy") & 1) == 0
    lane8 = iota((8, CY), 1)
    sub8 = iota((8, CY), 0)
    quarter = (iota((RING, CY), 1) // 4) % 4
    columns = spread_table(table)

    for p in range(PACKS):
        at = slice(p * CX, (p + 1) * CX)
        one, two = jnp.concatenate([ca[at], tca[p]], axis=0), jnp.concatenate([cb[at], tcb[p]], axis=0)
        from_right, from_left = jnp.where(even_y, one, two), jnp.where(even_y, two, one)
        for s in range(4):
            f = 4 * p + s
            if f < FIELDS:
                BF[f] = jnp.where(
                    quarter == 0, roll(from_left, -4 * s, 1),
                    jnp.where(quarter == 3, roll(from_right, 8 - 4 * s, 1), own[f]),
                )
    ids = BF[9].astype(jnp.int32)
    for k in range(3):
        BM[k] = take(jnp.broadcast_to(columns[k], (RING, CY)), ids)

    velocity_seams(range(0, 5), V, BUOY, BF)
    velocity_band(BF, BW, BM, None)
    for c in range(3):
        BV[c] = BW[6 + c]
    seam = seams(BW, (6, 7, 8))
    for z in range(0, 4):
        stress_plane(z, seam, S, V, LAM, MU, ALL)
    stress_band(BF, BW, BM)
    velocity_planes(range(0, 3), S, V, MU, BUOY, BW, None)
    velocity_band(BW, BW, BM, None)
    stress_plane(1, seams(BW, (8,)), S, V, LAM, MU, (XZ, YZ))

    total = jnp.zeros((8, CY), F32)
    for c, f in enumerate((XZ, YZ)):
        for r in range(CX // BLOCK):
            row = jnp.sum(S[f, 1, 8 * r:8 * r + 8, :], axis=0, keepdims=True)
            total = jnp.where(sub8 == 4 * c + r, jnp.broadcast_to(row, (8, CY)), total)
    for shift in (1, 2, 4):
        total = total + roll(total, CY - shift, 1)
    total = total * (1.0 / (BLOCK * BLOCK))
    ids = jnp.broadcast_to(jnp.concatenate([block[0], block[0]], axis=1), (8, CY))
    cells = CY // BLOCK
    picked = take(total, (ids % cells) * BLOCK)
    mine = (sub8 % 4 == ids // cells) & (sub8 // 4 == lane8 // FP_DEV)
    values = jnp.sum(jnp.where(mine, picked, 0.0), axis=0, keepdims=True)
    names = jnp.concatenate([building[0], building[0]], axis=1).astype(F32)
    message = jnp.concatenate([values, names], axis=0)
    shares[...] = jnp.broadcast_to(message[None], shares.shape)


def upper_kernel(S_in, V_in, LAM, MU, BUOY, BF, BV, BW, S, V):
    velocity_planes(range(5, 7), S, V, MU, BUOY, BF, None)
    seam = {6 + c: value for c, value in seams(BV, range(3)).items()}
    for z in range(4, 6):
        stress_plane(z, seam, S, V, LAM, MU, ALL)
    velocity_planes(range(3, 5), S, V, MU, BUOY, BW, None)
    seam = seams(BW, (6, 7, 8))
    for z in range(0, 4):
        stress_plane(z, seam, S, V, LAM, MU, (XX, XY) if z == 1 else ALL)


def lower_kernel(
    S_in, V_in, LAM, MU, BUOY, BF_in, BM, source, got, kept,
    S, V, BF, vel_out, stress_out, DRM, drm_in, sems,
):
    saves = []

    def save(ref, out, first, count):
        at = pl.ds(first, count)
        copy = pltpu.make_async_copy(ref.at[:, at, pl.ds(0, CX), :], out.at[:, at], sems.at[len(saves)])
        copy.start()
        saves.append(copy)

    save(V, vel_out, 0, 5)
    save(S, stress_out, 0, 4)
    low = iota((8, CY), 0) < 4
    lane8 = iota((8, CY), 1)
    quarter8 = (lane8 // 4) % 4
    deepest = lane8 >= 16 * (NZ - 1)

    mine = ((source[...] ^ lax.axis_index("gx")) & 1) == 0
    drm_in[...] = jnp.where(mine, kept[0], got[0])

    def wide(row):
        return jnp.broadcast_to(drm_in[row:row + 1, :], (8, CY))

    for s in range(STEPS):
        both = jnp.where(lane8 >= 96, wide(6 + s), roll(wide(CXC + 6 + s), 32, 1))
        for c in range(3):
            for q in range(RING // 8):
                if q < 4:
                    rows = jnp.where(low, wide(s * CXC + 2 * q), wide(s * CXC + 2 * q + 1))
                    base = c * CYC
                else:
                    rows = jnp.where(low, wide(s * CXC + c), wide(s * CXC + 3 + c))
                    base = 3 * CYC
                DRM[s, c, 0, 8 * q:8 * q + 8, :] = take(rows, base + lane8 // COARSE)
                inner = take(rows, base + jnp.where(quarter8 == 2, CYC - 1, 0))
                at = c * 10 + 2 * q + jnp.where(low, 0, 1) + jnp.where(quarter8 == 0, 96, 0)
                value = jnp.where((quarter8 & 1) == (quarter8 >> 1), take(both, at), inner)
                DRM[s, c, 1, 8 * q:8 * q + 8, :] = jnp.where(deepest, value, 0.0)

    def drm(step):
        return lambda c, k: DRM[step, c, k]

    velocity_planes(range(7, NZ), S, V, MU, BUOY, BF, drm(0))
    velocity_band(BF, BF, BM, drm(0))
    seam = seams(BF, (6, 7, 8))
    for z in range(6, NZ):
        stress_plane(z, seam, S, V, LAM, MU, ALL)
    stress_band(BF, BF, BM)
    velocity_planes(range(5, NZ), S, V, MU, BUOY, BF, drm(1))
    velocity_band(BF, BF, BM, drm(1))
    save(V, vel_out, 5, NZ - 5)
    seam = seams(BF, (6, 7, 8))
    for z in range(4, NZ):
        stress_plane(z, seam, S, V, LAM, MU, ALL)
        save(S, stress_out, z, 1)
    for copy in saves:
        copy.wait()


def sum_kernel(n, shares, out):
    half = n // 2
    low = iota((half, CY), 1) < FP_DEV
    values = shares[:, 0, :]
    names = shares[:, 1, :].astype(jnp.int32)
    entry = [
        jnp.where(low, values[:half], roll(values[half:], FP_DEV, 1)),
        jnp.where(low, roll(values[:half], FP_DEV, 1), values[half:]),
    ]
    names = jnp.where(low, names[:half], names[half:])
    high = names // CY
    names = names % CY
    n_high = BUILDINGS // CY
    rows = iota((n_high, CY), 0)
    wanted = iota((CY, CY), 0)
    acc = jnp.zeros((6 * n_high, CY), F32)
    for k in range(half):
        hot = (jnp.broadcast_to(names[k:k + 1], (CY, CY)) == wanted).astype(F32).astype(jnp.bfloat16)
        here = jnp.broadcast_to(high[k:k + 1], (n_high, CY)) == rows
        left = []
        for c in range(2):
            rest = jnp.where(here, jnp.broadcast_to(entry[c][k:k + 1], (n_high, CY)), 0.0)
            for _ in range(3):
                piece = rest.astype(jnp.bfloat16)
                rest = rest - piece.astype(F32)
                left.append(piece.astype(F32))
        left = jnp.concatenate(left, axis=0).astype(jnp.bfloat16)
        acc = acc + lax.dot_general(left, hot, (((1,), (1,)), ((), ())), preferred_element_type=F32)
    sums = []
    for c in range(2):
        base = 3 * c * n_high
        sums.append(acc[base:base + n_high] + acc[base + n_high:base + 2 * n_high] + acc[base + 2 * n_high:base + 3 * n_high])
    for h in range(n_high):
        out[:, h * CY:(h + 1) * CY] = jnp.concatenate([sums[0][h:h + 1], sums[1][h:h + 1]], axis=0)


def pairs_near(n):
    return [(i, i ^ 1) for i in range(n)]


def pairs_far(n):
    return [(i, (i + 1) % n if i % 2 else (i - 1) % n) for i in range(n)]


def after(x, *done):
    return lax.optimization_barrier((x,) + done)[0]


def body(n_gx, n_gy, velocity, stress, zones, zone_table, regional, owner, building, block):
    n = n_gx * n_gy
    gx = lax.axis_index("gx")
    vmem = pl.BlockSpec(memory_space=pltpu.VMEM)
    hbm = pl.BlockSpec(memory_space=pltpu.HBM)
    anywhere = pl.BlockSpec(memory_space=pl.ANY)
    params = pltpu.CompilerParams(vmem_limit_bytes=VMEM_LIMIT)

    def shaped(*shape):
        return jax.ShapeDtypeStruct(shape, F32)

    def whole(shape, dtype):
        return jax.ShapeDtypeStruct(shape, dtype)

    s_ring = shaped(6, NZ, RING, CY)
    v_ring = shaped(3, NZ, RING, CY)
    m_ring = shaped(NZ, RING, CY)
    rows = shaped(ROWS, CY)
    cols = shaped(COLS, CY)
    from_hbm = [
        pltpu.with_memory_space_constraint(x, pltpu.HBM)
        for x in (velocity, stress, zones, regional, zone_table, building, block)
    ]
    gxa, gxb, regional, zone_table, building, block = pl.pallas_call(
        rows_kernel,
        out_shape=(
            rows, rows, whole(regional.shape, F32), whole(zone_table.shape, F32),
            whole(building.shape, jnp.int32), whole(block.shape, jnp.int32),
        ),
        in_specs=[hbm] * 7,
        out_specs=(vmem,) * 6,
        scratch_shapes=[
            pltpu.VMEM((2, 9, NZ, 8, CY), F32),
            pltpu.VMEM((2, NZ, 8, CY), jnp.int32),
            pltpu.SemaphoreType.DMA((10,)),
        ],
        compiler_params=params,
        name="pack_rows",
    )(*from_hbm)
    rb = lax.ppermute(gxb, "gx", pairs_far(n_gx))
    ra = lax.ppermute(gxa, "gx", pairs_near(n_gx))
    own = shaped(FIELDS, RING, CY)
    S, V, gya, gyb, own = pl.pallas_call(
        cols_kernel,
        out_shape=(s_ring, v_ring, cols, cols, own),
        in_specs=[vmem] * 3,
        out_specs=(vmem,) * 5,
        scratch_shapes=[pltpu.SemaphoreType.DMA((2,))],
        compiler_params=params,
        name="pack_columns",
    )(velocity, stress, zones)

    def across(x, width):
        return lax.ppermute(x, "gx", [(i, i ^ width) for i in range(n_gx)])

    half = shaped(n_gx // 2, CHUNK, CY)
    source, sent, kept = pl.pallas_call(
        functools.partial(slices_kernel, n_gx, n_gy),
        out_shape=(whole((CHUNK, CY), jnp.int32), half, half),
        in_specs=[vmem, pl.BlockSpec(memory_space=pltpu.SMEM)],
        out_specs=(vmem,) * 3,
        scratch_shapes=[pltpu.VMEM((n_gx * CHUNK, CY), F32)],
        compiler_params=params,
        name="slices",
    )(regional, owner)
    width = 2
    while 4 * width < n_gx:
        count = sent.shape[0]
        part = shaped(count // 2, CHUNK, CY)
        sent, kept = pl.pallas_call(
            functools.partial(trade_kernel, width),
            out_shape=(part, part),
            in_specs=[vmem] * 3,
            out_specs=(vmem,) * 2,
            scratch_shapes=[pltpu.VMEM((count, CHUNK, CY), F32)],
            compiler_params=params,
            name="trade",
        )(across(sent, width), kept, source)
        width *= 2
    LAM, MU, BUOY, made = pl.pallas_call(
        material_kernel,
        out_shape=(m_ring,) * 3 + (shaped(8, CY),),
        in_specs=[vmem] * 2,
        out_specs=(vmem,) * 4,
        compiler_params=params,
        name="materials",
    )(zones, zone_table)
    message = shaped(COLS + 8, CY)
    quad, message_a, message_b = pl.pallas_call(
        functools.partial(ends_kernel, width),
        out_shape=(shaped(4, CHUNK, CY), message, message),
        in_specs=[vmem] * 5 + [anywhere],
        out_specs=(vmem,) * 3,
        compiler_params=params,
        name="ends",
    )(across(sent, width), kept, source, gya, gyb, made)
    cb = lax.ppermute(message_b, "gy", pairs_far(n_gy))
    ca = lax.ppermute(message_a, "gy", pairs_near(n_gy))
    ends = shaped(PACKS, 8, CY)
    S, V, LAM, MU, BUOY, own, ta, tb = pl.pallas_call(
        unpack_kernel,
        out_shape=(s_ring, v_ring, m_ring, m_ring, m_ring, shaped(FIELDS, RING, CY), ends, ends),
        in_specs=[vmem] * 9,
        out_specs=(vmem,) * 8,
        scratch_shapes=[pltpu.VMEM((NZ, 8, CY), F32)],
        input_output_aliases={k: k for k in range(6)},
        compiler_params=params,
        name="unpack",
    )(S, V, LAM, MU, BUOY, own, zone_table, ra, rb)
    tcb = lax.ppermute(tb, "gy", pairs_far(n_gy))
    tca = lax.ppermute(ta, "gy", pairs_near(n_gy))
    V, token = pl.pallas_call(
        inner_kernel,
        out_shape=(v_ring, shaped(8, CY)),
        in_specs=[vmem] * 4,
        out_specs=(vmem,) * 2,
        input_output_aliases={1: 0},
        compiler_params=params,
        name="inner",
    )(S, V, MU, BUOY)
    two = shaped(2, CHUNK, CY)
    width *= 2
    sent, kept = pl.pallas_call(
        functools.partial(edges_kernel, width),
        out_shape=(two, two),
        in_specs=[vmem] * 3 + [anywhere],
        out_specs=(vmem,) * 2,
        compiler_params=params,
        name="edges",
    )(quad, ca, cb, token)
    band = shaped(3, RING, CY)
    S, V, BF, BM, BV, BW, shares = pl.pallas_call(
        cone_kernel,
        out_shape=(s_ring, v_ring, shaped(FIELDS, RING, CY), band, band, shaped(9, RING, CY), shaped(n, 2, CY)),
        in_specs=[vmem] * 13,
        out_specs=(vmem,) * 7,
        input_output_aliases={0: 0, 1: 1},
        compiler_params=params,
        name="cone",
    )(S, V, LAM, MU, BUOY, zone_table, own, ca, cb, tca, tcb, building, block)
    held = jnp.where(((source ^ gx) & width) == 0, kept, across(sent, width))
    odd = (gx & 1) != 0
    sent, kept = jnp.where(odd, held[0], held[1])[None], jnp.where(odd, held[1], held[0])[None]
    got = across(sent, 1)
    every = lax.all_to_all(shares, ("gx", "gy"), 0, 0)
    S, V = pl.pallas_call(
        upper_kernel,
        out_shape=(s_ring, v_ring),
        in_specs=[vmem] * 8,
        out_specs=(vmem,) * 2,
        input_output_aliases={0: 0, 1: 1},
        compiler_params=params,
        name="upper",
    )(S, V, LAM, MU, BUOY, BF, BV, BW)
    shear = pl.pallas_call(
        functools.partial(sum_kernel, n),
        out_shape=shaped(2, BUILDINGS),
        in_specs=[vmem],
        out_specs=vmem,
        compiler_params=params,
        name="sum_by_building",
    )(every)
    _, _, _, vel_out, stress_out = pl.pallas_call(
        lower_kernel,
        out_shape=(s_ring, v_ring, shaped(FIELDS, RING, CY), shaped(*velocity.shape), shaped(*stress.shape)),
        in_specs=[vmem] * 10,
        out_specs=(vmem, vmem, vmem, hbm, hbm),
        scratch_shapes=[
            pltpu.VMEM((STEPS, 3, 2, RING, CY), F32),
            pltpu.VMEM((CHUNK, CY), F32),
            pltpu.SemaphoreType.DMA((NZ,)),
        ],
        input_output_aliases={0: 0, 1: 1, 5: 2},
        compiler_params=params,
        name="lower",
    )(S, V, LAM, MU, BUOY, BF, BM, source, got, kept)
    return vel_out, stress_out, shear


def solution(mesh):
    n_gx, n_gy = mesh.shape["gx"], mesh.shape["gy"]
    return jax.shard_map(
        functools.partial(body, n_gx, n_gy),
        mesh=mesh,
        in_specs=(
            P(None, None, "gx", "gy"),
            P(None, None, "gx", "gy"),
            P(None, "gx", "gy"),
            P(),
            P("gx", None, None, None, "gy"),
            P(),
            P("gx", "gy", None),
            P("gx", "gy", None),
        ),
        out_specs=(P(None, None, "gx", "gy"), P(None, None, "gx", "gy"), P()),
        check_vma=False,
    )
```

```python
import functools

import jax
import jax.numpy as jnp
from jax import lax
from jax.experimental import pallas as pl
from jax.experimental.pallas import tpu as pltpu
from jax.sharding import PartitionSpec as P

CX = 32
CY = 128
NZ = 8
STEPS = 2
COARSE = 4
BLOCK = 8
ZONES = 16
BUILDINGS = 1024
FP_DEV = 64
HALO = 4
RING = CX + 2 * HALO
FIELDS = 10
WIDE = 3
ROWS_AT = WIDE * 4 * 8
ROWS = ROWS_AT + (FIELDS - WIDE) * 3 * 8
PACKS = 3
CHUNK = 16
COLS = PACKS * CX
CXC = CX // COARSE
CYC = CY // COARSE
F32 = jnp.float32
VMEM_LIMIT = 32 * 1024 * 1024


def iota(shape, dim):
    return lax.broadcasted_iota(jnp.int32, shape, dim)


def take(x, idx):
    idx = jnp.broadcast_to(idx, x.shape)
    return jnp.take_along_axis(x, idx, axis=1, mode="promise_in_bounds")


def roll(x, shift, axis):
    size = x.shape[axis]
    shift = shift % size
    return x if shift == 0 else pltpu.roll(x, shift, axis)


def rows_kernel(
    n_gy, vel, stress, zones, regional_in, table_in, building_in, block_in, owner_in,
    gxa, gxb, regional, table, building, block, source, F, Z, owner, sems,
):
    even_x = (lax.axis_index("gx") & 1) == 0
    low = iota((8, CY), 0) < 4
    loads = []
    for end, at in enumerate((0, CX - 8)):
        rows = pl.ds(at, 8)
        loads.append(pltpu.make_async_copy(stress.at[:, :, rows, :], F.at[end, pl.ds(0, 6)], sems.at[3 * end]))
        loads.append(pltpu.make_async_copy(vel.at[:, :, rows, :], F.at[end, pl.ds(6, 3)], sems.at[3 * end + 1]))
        loads.append(pltpu.make_async_copy(zones.at[:, rows, :], Z.at[end], sems.at[3 * end + 2]))
    small = ((owner_in, owner), (regional_in, regional), (table_in, table), (building_in, building), (block_in, block))
    loads += [pltpu.make_async_copy(src, dst, sems.at[6 + k]) for k, (src, dst) in enumerate(small)]
    for copy in loads:
        copy.start()
    for copy in loads:
        copy.wait()

    def tile(f, z, end):
        return F[end, f, z] if f < 9 else Z[end, z].astype(F32)

    gy = lax.axis_index("gy")
    row = iota((CHUNK, CY), 0)
    edge = (iota((CHUNK, CY), 1) >= 96) & ((row & 7) >= 6)
    sides = jnp.where(row < CXC, owner[(gy + n_gy - 1) % n_gy], owner[(gy + 1) % n_gy])
    source[...] = jnp.where(edge, sides, owner[gy])

    for f in range(WIDE):
        for q in range(NZ // 2):
            first = jnp.where(low, tile(f, 2 * q, 0), roll(tile(f, 2 * q + 1, 0), 4, 0))
            last = jnp.where(low, roll(tile(f, 2 * q + 1, 1), 4, 0), tile(f, 2 * q, 1))
            at = 8 * (f * 4 + q)
            gxa[at:at + 8, :] = jnp.where(even_x, last, first)
            gxb[at:at + 8, :] = jnp.where(even_x, first, last)
    for f in range(WIDE, FIELDS):
        for z in range(NZ):
            first, last = tile(f, z, 0), roll(tile(f, z, 1), 3, 0)
            at = pl.ds(ROWS_AT + (f - WIDE) * 24 + z, 3, stride=8)
            gxa[at, :] = jnp.where(even_x, last, first)[0:3]
            gxb[at, :] = jnp.where(even_x, first, last)[0:3]


def own_band(own, p, at, lasts, firsts):
    inner = (iota(lasts.shape, 1) // 4) % 4 == 1
    for s in range(4):
        if 4 * p + s < FIELDS:
            own[4 * p + s, at, :] = jnp.where(inner, roll(firsts, -4 * s, 1), roll(lasts, 8 - 4 * s, 1))


def cols_kernel(vel, stress, zones, S, V, gya, gyb, own, sems):
    even_y = (lax.axis_index("gy") & 1) == 0
    inner = pl.ds(0, CX)
    loads = [
        pltpu.make_async_copy(stress, S.at[:, :, inner, :], sems.at[0]),
        pltpu.make_async_copy(vel, V.at[:, :, inner, :], sems.at[1]),
    ]
    for copy in loads:
        copy.start()
    slot = iota((CX, CY), 1) // HALO

    def plane(f, z):
        if f < 6:
            return stress[f, z]
        if f < 9:
            return vel[f - 6, z]
        return zones[z].astype(F32)

    for p in range(PACKS):
        lasts = jnp.zeros((CX, CY), F32)
        firsts = jnp.zeros((CX, CY), F32)
        for s in range(4):
            f = 4 * p + s
            if f >= FIELDS:
                continue
            for z in range(NZ):
                turned = roll(plane(f, z), 16 * z + 4 * s + 4, 1)
                at = 4 * z + s
                lasts = jnp.where(slot == at, turned, lasts)
                firsts = jnp.where(slot == (at + 1) % 32, turned, firsts)
        own_band(own, p, slice(0, CX), lasts, firsts)
        gya[p * CX:(p + 1) * CX, :] = jnp.where(even_y, lasts, firsts)
        gyb[p * CX:(p + 1) * CX, :] = jnp.where(even_y, firsts, lasts)

    for copy in loads:
        copy.wait()


def split(count):
    return [(4 * (k // 2) + k % 2, 2) for k in range(count // 2)]


def slices_kernel(n_gx, R, sent, kept, slices):
    part = iota((n_gx, CY), 1) // CYC
    for s in range(STEPS):
        halves = [[R[0, s, c, :, t * CY:(t + 1) * CY] for t in range(2)] for c in range(3)]
        for r in range(CXC):
            turned = jnp.zeros((n_gx, CY), F32)
            for c in range(3):
                turned = jnp.where(part == c, roll(halves[c][r // 4], CYC * (c - r % 4), 1), turned)
            if r < 3:
                turned = jnp.where(part == 3, roll(roll(halves[r][0], n_gx - 1, 0), 96, 1), turned)
            elif r < 6:
                turned = jnp.where(part == 3, roll(halves[r - 3][1], 1, 0), turned)
            slices[pl.ds(s * CXC + r, n_gx, stride=CHUNK), :] = turned
    bit = (lax.axis_index("gx") >> 1) & 1
    for k, (at, step) in enumerate(split(n_gx)):
        for out, side in ((sent, 1 - bit), (kept, bit)):
            out[k] = slices[pl.ds(pl.multiple_of((at + step * side) * CHUNK, CHUNK), CHUNK), :]


def trade_kernel(width, got, kept, source, sent, kept_out, held):
    gx = lax.axis_index("gx")
    mine = ((source[...] ^ gx) & width) == 0
    count = got.shape[0]
    for i in range(count):
        held[i] = jnp.where(mine, kept[i], got[i])
    bit = (gx & (2 * width)) // (2 * width)
    for k, (at, step) in enumerate(split(count)):
        sent[k] = held[at + step * (1 - bit)]
        kept_out[k] = held[at + step * bit]


def ends_kernel(width, got, kept, source, gya, gyb, made, pair, ta, tb):
    ta[0:COLS] = gya[...]
    tb[0:COLS] = gyb[...]
    even_y = (lax.axis_index("gy") & 1) == 0
    mine = ((source[...] ^ lax.axis_index("gx")) & width) == 0
    lane = iota((8, CY), 1)
    sub = iota((8, CY), 0)
    digit, group = (lane - 96) % 10, (lane - 96) // 10
    row = jnp.where(digit < 8, digit, jnp.where(digit == 8, group, 3 + group))
    here = (lane >= 96) & (group < 3) & (sub == row)
    tiles = [jnp.zeros((8, CY), F32), jnp.zeros((8, CY), F32)]
    for i in range(4):
        pair[i] = jnp.where(mine, kept[i], got[i])
        for s in range(STEPS):
            tile = pair[i, s * CXC:(s + 1) * CXC, :]
            for k, col in enumerate((CYC - 1, 0)):
                idx = jnp.where(here, jnp.where(digit < 8, group * CYC, 96) + col, 0)
                ends = jnp.sum(jnp.where(here, take(tile, idx), 0.0), axis=0, keepdims=True)
                tiles[k] = jnp.where(sub == 2 * i + s, jnp.broadcast_to(ends, (8, CY)), tiles[k])
    ta[COLS:COLS + 8] = jnp.where(even_y, tiles[0], tiles[1])
    tb[COLS:COLS + 8] = jnp.where(even_y, tiles[1], tiles[0])


def edges_kernel(width, quad, ca, cb, token, sent, kept):
    even_y = (lax.axis_index("gy") & 1) == 0
    bit = (lax.axis_index("gx") & width) // width
    beside = iota((1, CY), 1) >= 96
    for k, (first, step) in enumerate(split(4)):
        for out, side in ((sent, 1 - bit), (kept, bit)):
            at = first + step * side
            out[k] = quad[at]
            for s in range(STEPS):
                a, b = ca[pl.ds(COLS + 2 * at + s, 1), :], cb[pl.ds(COLS + 2 * at + s, 1), :]
                for j, ends in enumerate((jnp.where(even_y, b, a), jnp.where(even_y, a, b))):
                    put = j * CXC + 6 + s
                    out[k, put:put + 1, :] = jnp.where(beside, ends, out[k, put:put + 1, :])


def spread_table(table):
    scaled = table[...] * 0.1
    spread = jnp.concatenate([scaled] * (CY // ZONES), axis=1)
    return [spread[k:k + 1, :] for k in range(3)]


def material_kernel(zones, table, LAM, MU, BUOY, token):
    token[...] = jnp.zeros(token.shape, F32)
    columns = [jnp.broadcast_to(row, (CX, CY)) for row in spread_table(table)]
    for z in range(NZ):
        ids = zones[z]
        for k, ref in enumerate((LAM, MU, BUOY)):
            ref[z, 0:CX, :] = take(columns[k], ids)


XX, XZ, XY, YY, YZ, ZZ = range(6)


def dx(x):
    return roll(x, RING - 1, 0) - roll(x, 1, 0)


def dy(x, seam, z):
    lane = iota((RING, CY), 1)
    if seam is None:
        return jnp.where(lane == CY - 1, 0.0, roll(x, CY - 1, 1)) - jnp.where(lane == 0, 0.0, roll(x, 1, 1))
    seam = roll(seam, -(16 * z + 3), 1)
    return jnp.where(lane == CY - 1, seam, roll(x, CY - 1, 1)) - jnp.where(lane == 0, seam, roll(x, 1, 1))


def dz(ref, f, z):
    if z == 0:
        return ref[f, 1]
    if z == NZ - 1:
        return -ref[f, NZ - 2]
    return ref[f, z + 1] - ref[f, z - 1]


def band_dy(x):
    return roll(x, CY - 1, 1) - roll(x, 1, 1)


def band_dz(x):
    lane = iota((RING, CY), 1)
    return jnp.where(lane < CY - 16, roll(x, CY - 16, 1), 0.0) - jnp.where(lane >= 16, roll(x, 16, 1), 0.0)


def seams(band, fields):
    lane = iota((RING, CY), 1)
    return {f: jnp.where(lane % 16 == 2, roll(band[f], -10, 1), band[f]) for f in fields}


ALL = (XX, XZ, XY, YY, YZ, ZZ)
FLAT, STEEP = (XX, XY), (XZ, YZ)


def moving(planes, first):
    return [(z, (0, 1) if (z % 2 == 0) == first else (2,)) for z in planes]


def every(planes):
    return [(z, (0, 1, 2)) for z in planes]


def velocity_planes(parts, S, V, MU, BUOY, band, drm):
    seam = {XY: None, YY: None, YZ: None} if band is None else seams(band, (XY, YY, YZ))
    for z, comps in parts:
        for c in comps:
            x, y, vert = ((XX, XY, XZ), (XY, YY, YZ), (XZ, YZ, ZZ))[c]
            force = dx(S[x, z]) + dy(S[y, z], seam[y], z) + dz(S, vert, z)
            if z == NZ - 1:
                force = force + (20.0 * MU[z]) * drm(c, 0)
            V[c, z] = V[c, z] + BUOY[z] * force


def velocity_seams(parts, V, BUOY, band):
    lane = iota((RING, CY), 1)
    sign = jnp.where(lane == 0, -1.0, jnp.where(lane == CY - 1, 1.0, 0.0))
    seam = seams(band, (XY, YY, YZ))
    for z, comps in parts:
        scale = BUOY[z] * sign
        for c in comps:
            V[c, z] = V[c, z] + scale * roll(seam[(XY, YY, YZ)[c]], -(16 * z + 3), 1)


def velocity_band(band, new, BM, drm):
    sxy, sxz, syz = band[XY], band[XZ], band[YZ]
    force = [
        dx(band[XX]) + band_dy(sxy) + band_dz(sxz),
        dx(sxy) + band_dy(band[YY]) + band_dz(syz),
        dx(sxz) + band_dy(syz) + band_dz(band[ZZ]),
    ]
    for c in range(3):
        if drm is not None:
            force[c] = force[c] + (20.0 * BM[1]) * drm(c, 1)
        new[6 + c] = band[6 + c] + BM[2] * force[c]


def stress_plane(z, seam, S, V, LAM, MU, fields):
    vx, vy, vz = V[0, z], V[1, z], V[2, z]
    mu = MU[z]
    if XX in fields:
        lam = LAM[z]
        xx, yy, zz = dx(vx), dy(vy, seam[7], z), dz(V, 2, z)
        theta = lam * (xx + yy + zz)
        two = mu + mu
        S[XX, z] = S[XX, z] + (theta + two * xx)
        S[YY, z] = S[YY, z] + (theta + two * yy)
        S[ZZ, z] = S[ZZ, z] + (theta + two * zz)
    if XZ in fields:
        S[XZ, z] = S[XZ, z] + mu * (dz(V, 0, z) + dx(vz))
    if XY in fields:
        S[XY, z] = S[XY, z] + mu * (dy(vx, seam[6], z) + dx(vy))
    if YZ in fields:
        S[YZ, z] = S[YZ, z] + mu * (dz(V, 1, z) + dy(vz, seam[8], z))


def stress_band(band, new, BM):
    vx, vy, vz = new[6], new[7], new[8]
    lam, mu = BM[0], BM[1]
    xx, yy, zz = dx(vx), band_dy(vy), band_dz(vz)
    theta = lam * (xx + yy + zz)
    two = mu + mu
    new[XX] = band[XX] + (theta + two * xx)
    new[YY] = band[YY] + (theta + two * yy)
    new[ZZ] = band[ZZ] + (theta + two * zz)
    new[XZ] = band[XZ] + mu * (band_dz(vx) + dx(vz))
    new[XY] = band[XY] + mu * (band_dy(vx) + dx(vy))
    new[YZ] = band[YZ] + mu * (band_dz(vy) + band_dy(vz))


def unpack_kernel(
    S_in, V_in, LAM_in, MU_in, BUOY_in, own_in, table, rb, ra,
    S, V, LAM, MU, BUOY, own, ta, tb, zone_tail,
):
    even_x = (lax.axis_index("gx") & 1) == 0
    even_y = (lax.axis_index("gy") & 1) == 0
    low = iota((8, CY), 0) < 4
    slot = iota((8, CY), 1) // HALO
    tail = slice(CX, RING)
    columns = [jnp.broadcast_to(row, (8, CY)) for row in spread_table(table)]

    def place(f, z, rows, at):
        if f < 6:
            S[f, z, CX + at:CX + at + rows.shape[0], :] = rows
        elif f < 9:
            V[f - 6, z, CX + at:CX + at + rows.shape[0], :] = rows
        else:
            zone_tail[z, at:at + rows.shape[0], :] = rows

    for f in range(WIDE):
        for q in range(NZ // 2):
            at = slice(8 * (f * 4 + q), 8 * (f * 4 + q) + 8)
            after = jnp.where(even_x, ra[at], rb[at])
            before = jnp.where(even_x, rb[at], ra[at])
            place(f, 2 * q, jnp.where(low, after, before), 0)
            place(f, 2 * q + 1, roll(jnp.where(low, before, after), 4, 0), 0)
    for f in range(WIDE, FIELDS):
        for z in range(NZ):
            at = pl.ds(ROWS_AT + (f - WIDE) * 24 + z, 3, stride=8)
            a, b = ra[at, :], rb[at, :]
            place(f, z, jnp.zeros((8, CY), F32), 0)
            place(f, z, jnp.where(even_x, a, b), 0)
            place(f, z, jnp.where(even_x, b, a), 5)
    for z in range(NZ):
        ids = zone_tail[z].astype(jnp.int32)
        for column, ref in zip(columns, (LAM, MU, BUOY)):
            ref[z, tail, :] = take(column, ids)
    for p in range(PACKS):
        lasts = jnp.zeros((8, CY), F32)
        firsts = jnp.zeros((8, CY), F32)
        for s in range(4):
            f = 4 * p + s
            if f >= FIELDS:
                continue
            for z in range(NZ):
                rows = S[f, z, tail, :] if f < 6 else V[f - 6, z, tail, :] if f < 9 else zone_tail[z]
                turned = roll(rows, 16 * z + 4 * s + 4, 1)
                at = 4 * z + s
                lasts = jnp.where(slot == at, turned, lasts)
                firsts = jnp.where(slot == (at + 1) % 32, turned, firsts)
        own_band(own, p, tail, lasts, firsts)
        ta[p] = jnp.where(even_y, lasts, firsts)
        tb[p] = jnp.where(even_y, firsts, lasts)


def inner_kernel(S, V_in, MU, BUOY, V, token):
    velocity_planes(moving(range(0, 5), True), S, V, MU, BUOY, None, None)
    token[...] = jnp.zeros(token.shape, F32)


def cone_kernel(
    S_in, V_in, LAM, MU, BUOY, table, own, ca, cb, tca, tcb, building, block,
    S, V, BF, BM, BV, BW, shares,
):
    even_y = (lax.axis_index("gy") & 1) == 0
    lane8 = iota((8, CY), 1)
    sub8 = iota((8, CY), 0)
    quarter = (iota((RING, CY), 1) // 4) % 4
    columns = spread_table(table)

    for p in range(PACKS):
        at = slice(p * CX, (p + 1) * CX)
        one, two = jnp.concatenate([ca[at], tca[p]], axis=0), jnp.concatenate([cb[at], tcb[p]], axis=0)
        from_right, from_left = jnp.where(even_y, one, two), jnp.where(even_y, two, one)
        for s in range(4):
            f = 4 * p + s
            if f < FIELDS:
                BF[f] = jnp.where(
                    quarter == 0, roll(from_left, -4 * s, 1),
                    jnp.where(quarter == 3, roll(from_right, 8 - 4 * s, 1), own[f]),
                )
    ids = BF[9].astype(jnp.int32)
    for k in range(3):
        BM[k] = take(jnp.broadcast_to(columns[k], (RING, CY)), ids)

    velocity_seams(moving(range(0, 5), True), V, BUOY, BF)
    velocity_band(BF, BW, BM, None)
    for c in range(3):
        BV[c] = BW[6 + c]
    seam = seams(BW, (6, 7, 8))
    for z in range(0, 4):
        stress_plane(z, seam, S, V, LAM, MU, (FLAT, STEEP)[z % 2])
    stress_band(BF, BW, BM)
    velocity_planes(moving(range(0, 3), True), S, V, MU, BUOY, BW, None)
    velocity_band(BW, BW, BM, None)
    stress_plane(1, seams(BW, (8,)), S, V, LAM, MU, (XZ, YZ))

    total = jnp.zeros((8, CY), F32)
    for c, f in enumerate((XZ, YZ)):
        for r in range(CX // BLOCK):
            row = jnp.sum(S[f, 1, 8 * r:8 * r + 8, :], axis=0, keepdims=True)
            total = jnp.where(sub8 == 4 * c + r, jnp.broadcast_to(row, (8, CY)), total)
    for shift in (1, 2, 4):
        total = total + roll(total, CY - shift, 1)
    total = total * (1.0 / (BLOCK * BLOCK))
    ids = jnp.broadcast_to(jnp.concatenate([block[0], block[0]], axis=1), (8, CY))
    cells = CY // BLOCK
    picked = take(total, (ids % cells) * BLOCK)
    mine = (sub8 % 4 == ids // cells) & (sub8 // 4 == lane8 // FP_DEV)
    values = jnp.sum(jnp.where(mine, picked, 0.0), axis=0, keepdims=True)
    names = jnp.concatenate([building[0], building[0]], axis=1).astype(F32)
    message = jnp.concatenate([values, names], axis=0)
    shares[...] = jnp.broadcast_to(message[None], shares.shape)


def upper_kernel(S_in, V_in, LAM, MU, BUOY, BF, BV, BW, S, V):
    velocity_planes(moving(range(0, 5), False) + every(range(5, 7)), S, V, MU, BUOY, BF, None)
    seam = {6 + c: value for c, value in seams(BV, range(3)).items()}
    for z in range(0, 6):
        stress_plane(z, seam, S, V, LAM, MU, ALL if z > 3 else (STEEP, FLAT)[z % 2])
    velocity_planes(moving(range(0, 3), False) + every(range(3, 5)), S, V, MU, BUOY, BW, None)
    seam = seams(BW, (6, 7, 8))
    for z in range(0, 4):
        stress_plane(z, seam, S, V, LAM, MU, FLAT if z == 1 else ALL)


def lower_kernel(
    S_in, V_in, LAM, MU, BUOY, BF_in, BM, source, got, kept,
    S, V, BF, vel_out, stress_out, DRM, drm_in, sems,
):
    saves = []

    def save(ref, out, first, count):
        at = pl.ds(first, count)
        copy = pltpu.make_async_copy(ref.at[:, at, pl.ds(0, CX), :], out.at[:, at], sems.at[len(saves)])
        copy.start()
        saves.append(copy)

    save(V, vel_out, 0, 5)
    save(S, stress_out, 0, 4)
    low = iota((8, CY), 0) < 4
    lane8 = iota((8, CY), 1)
    quarter8 = (lane8 // 4) % 4
    deepest = lane8 >= 16 * (NZ - 1)

    mine = ((source[...] ^ lax.axis_index("gx")) & 1) == 0
    drm_in[...] = jnp.where(mine, kept[0], got[0])

    def wide(row):
        return jnp.broadcast_to(drm_in[row:row + 1, :], (8, CY))

    for s in range(STEPS):
        both = jnp.where(lane8 >= 96, wide(6 + s), roll(wide(CXC + 6 + s), 32, 1))
        for c in range(3):
            for q in range(RING // 8):
                if q < 4:
                    rows = jnp.where(low, wide(s * CXC + 2 * q), wide(s * CXC + 2 * q + 1))
                    base = c * CYC
                else:
                    rows = jnp.where(low, wide(s * CXC + c), wide(s * CXC + 3 + c))
                    base = 3 * CYC
                DRM[s, c, 0, 8 * q:8 * q + 8, :] = take(rows, base + lane8 // COARSE)
                inner = take(rows, base + jnp.where(quarter8 == 2, CYC - 1, 0))
                at = c * 10 + 2 * q + jnp.where(low, 0, 1) + jnp.where(quarter8 == 0, 96, 0)
                value = jnp.where((quarter8 & 1) == (quarter8 >> 1), take(both, at), inner)
                DRM[s, c, 1, 8 * q:8 * q + 8, :] = jnp.where(deepest, value, 0.0)

    def drm(step):
        return lambda c, k: DRM[step, c, k]

    velocity_planes(every(range(7, NZ)), S, V, MU, BUOY, BF, drm(0))
    velocity_band(BF, BF, BM, drm(0))
    seam = seams(BF, (6, 7, 8))
    for z in range(6, NZ):
        stress_plane(z, seam, S, V, LAM, MU, ALL)
    stress_band(BF, BF, BM)
    velocity_planes(every(range(5, NZ)), S, V, MU, BUOY, BF, drm(1))
    velocity_band(BF, BF, BM, drm(1))
    save(V, vel_out, 5, NZ - 5)
    seam = seams(BF, (6, 7, 8))
    for z in range(4, NZ):
        stress_plane(z, seam, S, V, LAM, MU, ALL)
        save(S, stress_out, z, 1)
    for copy in saves:
        copy.wait()


def sum_kernel(n, shares, out):
    half = n // 2
    low = iota((half, CY), 1) < FP_DEV
    values = shares[:, 0, :]
    names = shares[:, 1, :].astype(jnp.int32)
    entry = [
        jnp.where(low, values[:half], roll(values[half:], FP_DEV, 1)),
        jnp.where(low, roll(values[:half], FP_DEV, 1), values[half:]),
    ]
    names = jnp.where(low, names[:half], names[half:])
    high = names // CY
    names = names % CY
    n_high = BUILDINGS // CY
    rows = iota((n_high, CY), 0)
    wanted = iota((CY, CY), 0)
    acc = jnp.zeros((6 * n_high, CY), F32)
    for k in range(half):
        hot = (jnp.broadcast_to(names[k:k + 1], (CY, CY)) == wanted).astype(F32).astype(jnp.bfloat16)
        here = jnp.broadcast_to(high[k:k + 1], (n_high, CY)) == rows
        left = []
        for c in range(2):
            rest = jnp.where(here, jnp.broadcast_to(entry[c][k:k + 1], (n_high, CY)), 0.0)
            for _ in range(3):
                piece = rest.astype(jnp.bfloat16)
                rest = rest - piece.astype(F32)
                left.append(piece.astype(F32))
        left = jnp.concatenate(left, axis=0).astype(jnp.bfloat16)
        acc = acc + lax.dot_general(left, hot, (((1,), (1,)), ((), ())), preferred_element_type=F32)
    sums = []
    for c in range(2):
        base = 3 * c * n_high
        sums.append(acc[base:base + n_high] + acc[base + n_high:base + 2 * n_high] + acc[base + 2 * n_high:base + 3 * n_high])
    for h in range(n_high):
        out[:, h * CY:(h + 1) * CY] = jnp.concatenate([sums[0][h:h + 1], sums[1][h:h + 1]], axis=0)


def pairs_near(n):
    return [(i, i ^ 1) for i in range(n)]


def pairs_far(n):
    return [(i, (i + 1) % n if i % 2 else (i - 1) % n) for i in range(n)]


def after(x, *done):
    return lax.optimization_barrier((x,) + done)[0]


def body(n_gx, n_gy, velocity, stress, zones, zone_table, regional, owner, building, block):
    n = n_gx * n_gy
    gx = lax.axis_index("gx")
    vmem = pl.BlockSpec(memory_space=pltpu.VMEM)
    hbm = pl.BlockSpec(memory_space=pltpu.HBM)
    anywhere = pl.BlockSpec(memory_space=pl.ANY)
    params = pltpu.CompilerParams(vmem_limit_bytes=VMEM_LIMIT)

    def shaped(*shape):
        return jax.ShapeDtypeStruct(shape, F32)

    def whole(shape, dtype):
        return jax.ShapeDtypeStruct(shape, dtype)

    s_ring = shaped(6, NZ, RING, CY)
    v_ring = shaped(3, NZ, RING, CY)
    m_ring = shaped(NZ, RING, CY)
    rows = shaped(ROWS, CY)
    cols = shaped(COLS, CY)
    from_hbm = [
        pltpu.with_memory_space_constraint(x, pltpu.HBM)
        for x in (velocity, stress, zones, regional, zone_table, building, block, owner)
    ]
    gxa, gxb, regional, zone_table, building, block, source = pl.pallas_call(
        functools.partial(rows_kernel, n_gy),
        out_shape=(
            rows, rows, whole(regional.shape, F32), whole(zone_table.shape, F32),
            whole(building.shape, jnp.int32), whole(block.shape, jnp.int32), whole((CHUNK, CY), jnp.int32),
        ),
        in_specs=[hbm] * 8,
        out_specs=(vmem,) * 7,
        scratch_shapes=[
            pltpu.VMEM((2, 9, NZ, 8, CY), F32),
            pltpu.VMEM((2, NZ, 8, CY), jnp.int32),
            pltpu.SMEM(owner.shape, jnp.int32),
            pltpu.SemaphoreType.DMA((11,)),
        ],
        compiler_params=params,
        name="pack_rows",
    )(*from_hbm)
    rb = lax.ppermute(gxb, "gx", pairs_far(n_gx))
    ra = lax.ppermute(gxa, "gx", pairs_near(n_gx))
    own = shaped(FIELDS, RING, CY)
    S, V, gya, gyb, own = pl.pallas_call(
        cols_kernel,
        out_shape=(s_ring, v_ring, cols, cols, own),
        in_specs=[vmem] * 3,
        out_specs=(vmem,) * 5,
        scratch_shapes=[pltpu.SemaphoreType.DMA((2,))],
        compiler_params=params,
        name="pack_columns",
    )(velocity, stress, zones)

    def across(x, width):
        return lax.ppermute(x, "gx", [(i, i ^ width) for i in range(n_gx)])

    half = shaped(n_gx // 2, CHUNK, CY)
    sent, kept = pl.pallas_call(
        functools.partial(slices_kernel, n_gx),
        out_shape=(half, half),
        in_specs=[vmem],
        out_specs=(vmem,) * 2,
        scratch_shapes=[pltpu.VMEM((n_gx * CHUNK, CY), F32)],
        compiler_params=params,
        name="slices",
    )(regional)
    width = 2
    while 4 * width < n_gx:
        count = sent.shape[0]
        part = shaped(count // 2, CHUNK, CY)
        sent, kept = pl.pallas_call(
            functools.partial(trade_kernel, width),
            out_shape=(part, part),
            in_specs=[vmem] * 3,
            out_specs=(vmem,) * 2,
            scratch_shapes=[pltpu.VMEM((count, CHUNK, CY), F32)],
            compiler_params=params,
            name="trade",
        )(across(sent, width), kept, source)
        width *= 2
    LAM, MU, BUOY, made = pl.pallas_call(
        material_kernel,
        out_shape=(m_ring,) * 3 + (shaped(8, CY),),
        in_specs=[vmem] * 2,
        out_specs=(vmem,) * 4,
        compiler_params=params,
        name="materials",
    )(zones, zone_table)
    message = shaped(COLS + 8, CY)
    quad, message_a, message_b = pl.pallas_call(
        functools.partial(ends_kernel, width),
        out_shape=(shaped(4, CHUNK, CY), message, message),
        in_specs=[vmem] * 5 + [anywhere],
        out_specs=(vmem,) * 3,
        compiler_params=params,
        name="ends",
    )(across(sent, width), kept, source, gya, gyb, made)
    cb = lax.ppermute(message_b, "gy", pairs_far(n_gy))
    ca = lax.ppermute(message_a, "gy", pairs_near(n_gy))
    ends = shaped(PACKS, 8, CY)
    S, V, LAM, MU, BUOY, own, ta, tb = pl.pallas_call(
        unpack_kernel,
        out_shape=(s_ring, v_ring, m_ring, m_ring, m_ring, shaped(FIELDS, RING, CY), ends, ends),
        in_specs=[vmem] * 9,
        out_specs=(vmem,) * 8,
        scratch_shapes=[pltpu.VMEM((NZ, 8, CY), F32)],
        input_output_aliases={k: k for k in range(6)},
        compiler_params=params,
        name="unpack",
    )(S, V, LAM, MU, BUOY, own, zone_table, rb, ra)
    tcb = lax.ppermute(tb, "gy", pairs_far(n_gy))
    tca = lax.ppermute(ta, "gy", pairs_near(n_gy))
    V, token = pl.pallas_call(
        inner_kernel,
        out_shape=(v_ring, shaped(8, CY)),
        in_specs=[vmem] * 4,
        out_specs=(vmem,) * 2,
        input_output_aliases={1: 0},
        compiler_params=params,
        name="inner",
    )(S, V, MU, BUOY)
    two = shaped(2, CHUNK, CY)
    width *= 2
    sent, kept = pl.pallas_call(
        functools.partial(edges_kernel, width),
        out_shape=(two, two),
        in_specs=[vmem] * 3 + [anywhere],
        out_specs=(vmem,) * 2,
        compiler_params=params,
        name="edges",
    )(quad, ca, cb, token)
    band = shaped(3, RING, CY)
    S, V, BF, BM, BV, BW, shares = pl.pallas_call(
        cone_kernel,
        out_shape=(s_ring, v_ring, shaped(FIELDS, RING, CY), band, band, shaped(9, RING, CY), shaped(n, 2, CY)),
        in_specs=[vmem] * 13,
        out_specs=(vmem,) * 7,
        input_output_aliases={0: 0, 1: 1},
        compiler_params=params,
        name="cone",
    )(S, V, LAM, MU, BUOY, zone_table, own, ca, cb, tca, tcb, building, block)
    held = jnp.where(((source ^ gx) & width) == 0, kept, across(sent, width))
    odd = (gx & 1) != 0
    sent, kept = jnp.where(odd, held[0], held[1])[None], jnp.where(odd, held[1], held[0])[None]
    got = across(sent, 1)
    gathered = lax.all_to_all(shares, ("gx", "gy"), 0, 0)
    S, V = pl.pallas_call(
        upper_kernel,
        out_shape=(s_ring, v_ring),
        in_specs=[vmem] * 8,
        out_specs=(vmem,) * 2,
        input_output_aliases={0: 0, 1: 1},
        compiler_params=params,
        name="upper",
    )(S, V, LAM, MU, BUOY, BF, BV, BW)
    shear = pl.pallas_call(
        functools.partial(sum_kernel, n),
        out_shape=shaped(2, BUILDINGS),
        in_specs=[vmem],
        out_specs=vmem,
        compiler_params=params,
        name="sum_by_building",
    )(gathered)
    _, _, _, vel_out, stress_out = pl.pallas_call(
        lower_kernel,
        out_shape=(s_ring, v_ring, shaped(FIELDS, RING, CY), shaped(*velocity.shape), shaped(*stress.shape)),
        in_specs=[vmem] * 10,
        out_specs=(vmem, vmem, vmem, hbm, hbm),
        scratch_shapes=[
            pltpu.VMEM((STEPS, 3, 2, RING, CY), F32),
            pltpu.VMEM((CHUNK, CY), F32),
            pltpu.SemaphoreType.DMA((NZ,)),
        ],
        input_output_aliases={0: 0, 1: 1, 5: 2},
        compiler_params=params,
        name="lower",
    )(S, V, LAM, MU, BUOY, BF, BM, source, got, kept)
    return vel_out, stress_out, shear


def solution(mesh):
    n_gx, n_gy = mesh.shape["gx"], mesh.shape["gy"]
    return jax.shard_map(
        functools.partial(body, n_gx, n_gy),
        mesh=mesh,
        in_specs=(
            P(None, None, "gx", "gy"),
            P(None, None, "gx", "gy"),
            P(None, "gx", "gy"),
            P(),
            P("gx", None, None, None, "gy"),
            P(),
            P("gx", "gy", None),
            P("gx", "gy", None),
        ),
        out_specs=(P(None, None, "gx", "gy"), P(None, None, "gx", "gy"), P()),
        check_vma=False,
    )
```

```python
import functools

import jax
import jax.numpy as jnp
from jax import lax
from jax.experimental import pallas as pl
from jax.experimental.pallas import tpu as pltpu
from jax.sharding import PartitionSpec as P

CX = 32
CY = 128
NZ = 8
STEPS = 2
COARSE = 4
BLOCK = 8
ZONES = 16
BUILDINGS = 1024
FP_DEV = 64
HALO = 4
RING = CX + 2 * HALO
FIELDS = 10
WIDE = 3
ROWS_AT = WIDE * 4 * 8
ROWS = ROWS_AT + (FIELDS - WIDE) * 3 * 8
PACKS = 3
CHUNK = 16
COLS = PACKS * CX
CXC = CX // COARSE
CYC = CY // COARSE
F32 = jnp.float32
VMEM_LIMIT = 32 * 1024 * 1024


def iota(shape, dim):
    return lax.broadcasted_iota(jnp.int32, shape, dim)


def take(x, idx):
    idx = jnp.broadcast_to(idx, x.shape)
    return jnp.take_along_axis(x, idx, axis=1, mode="promise_in_bounds")


def roll(x, shift, axis):
    size = x.shape[axis]
    shift = shift % size
    return x if shift == 0 else pltpu.roll(x, shift, axis)


def rows_kernel(
    n_gy, vel, stress, zones, regional_in, table_in, building_in, block_in, owner_in,
    gxa, gxb, regional, table, building, block, source, F, Z, owner, sems,
):
    even_x = (lax.axis_index("gx") & 1) == 0
    low = iota((8, CY), 0) < 4
    loads = []
    for end, at in enumerate((0, CX - HALO)):
        rows, to = pl.ds(at, HALO), pl.ds(HALO * end, HALO)
        loads.append(pltpu.make_async_copy(stress.at[:, :, rows, :], F.at[end, pl.ds(0, 6), :, to], sems.at[3 * end]))
        loads.append(pltpu.make_async_copy(vel.at[:, :, rows, :], F.at[end, pl.ds(6, 3), :, to], sems.at[3 * end + 1]))
        loads.append(pltpu.make_async_copy(zones.at[:, rows, :], Z.at[end, :, to], sems.at[3 * end + 2]))
    small = ((owner_in, owner), (regional_in, regional), (table_in, table), (building_in, building), (block_in, block))
    loads += [pltpu.make_async_copy(src, dst, sems.at[6 + k]) for k, (src, dst) in enumerate(small)]
    for copy in loads:
        copy.start()
    for copy in loads:
        copy.wait()

    def tile(f, z, end):
        return F[end, f, z] if f < 9 else Z[end, z].astype(F32)

    gy = lax.axis_index("gy")
    row = iota((CHUNK, CY), 0)
    edge = (iota((CHUNK, CY), 1) >= 96) & ((row & 7) >= 6)
    sides = jnp.where(row < CXC, owner[(gy + n_gy - 1) % n_gy], owner[(gy + 1) % n_gy])
    source[...] = jnp.where(edge, sides, owner[gy])

    for f in range(WIDE):
        for q in range(NZ // 2):
            first = jnp.where(low, tile(f, 2 * q, 0), roll(tile(f, 2 * q + 1, 0), 4, 0))
            last = jnp.where(low, roll(tile(f, 2 * q + 1, 1), 4, 0), tile(f, 2 * q, 1))
            at = 8 * (f * 4 + q)
            gxa[at:at + 8, :] = jnp.where(even_x, last, first)
            gxb[at:at + 8, :] = jnp.where(even_x, first, last)
    for f in range(WIDE, FIELDS):
        for z in range(NZ):
            first, last = tile(f, z, 0), roll(tile(f, z, 1), 3, 0)
            at = pl.ds(ROWS_AT + (f - WIDE) * 24 + z, 3, stride=8)
            gxa[at, :] = jnp.where(even_x, last, first)[0:3]
            gxb[at, :] = jnp.where(even_x, first, last)[0:3]


def own_band(own, p, at, lasts, firsts):
    inner = (iota(lasts.shape, 1) // 4) % 4 == 1
    for s in range(4):
        if 4 * p + s < FIELDS:
            own[4 * p + s, at, :] = jnp.where(inner, roll(firsts, -4 * s, 1), roll(lasts, 8 - 4 * s, 1))


def cols_kernel(vel, stress, zones, S, V, gya, gyb, own, sems):
    even_y = (lax.axis_index("gy") & 1) == 0
    inner = pl.ds(0, CX)
    loads = [
        pltpu.make_async_copy(stress, S.at[:, :, inner, :], sems.at[0]),
        pltpu.make_async_copy(vel, V.at[:, :, inner, :], sems.at[1]),
    ]
    for copy in loads:
        copy.start()
    slot = iota((CX, CY), 1) // HALO

    def plane(f, z):
        if f < 6:
            return stress[f, z]
        if f < 9:
            return vel[f - 6, z]
        return zones[z].astype(F32)

    for p in range(PACKS):
        lasts = jnp.zeros((CX, CY), F32)
        firsts = jnp.zeros((CX, CY), F32)
        for s in range(4):
            f = 4 * p + s
            if f >= FIELDS:
                continue
            for z in range(NZ):
                turned = roll(plane(f, z), 16 * z + 4 * s + 4, 1)
                at = 4 * z + s
                lasts = jnp.where(slot == at, turned, lasts)
                firsts = jnp.where(slot == (at + 1) % 32, turned, firsts)
        own_band(own, p, slice(0, CX), lasts, firsts)
        gya[p * CX:(p + 1) * CX, :] = jnp.where(even_y, lasts, firsts)
        gyb[p * CX:(p + 1) * CX, :] = jnp.where(even_y, firsts, lasts)

    for copy in loads:
        copy.wait()


def split(count):
    return [(4 * (k // 2) + k % 2, 2) for k in range(count // 2)]


def slices_kernel(n_gx, R, sent, kept, slices):
    part = iota((n_gx, CY), 1) // CYC
    for s in range(STEPS):
        halves = [[R[0, s, c, :, t * CY:(t + 1) * CY] for t in range(2)] for c in range(3)]
        for r in range(CXC):
            turned = jnp.zeros((n_gx, CY), F32)
            for c in range(3):
                turned = jnp.where(part == c, roll(halves[c][r // 4], CYC * (c - r % 4), 1), turned)
            if r < 3:
                turned = jnp.where(part == 3, roll(roll(halves[r][0], n_gx - 1, 0), 96, 1), turned)
            elif r < 6:
                turned = jnp.where(part == 3, roll(halves[r - 3][1], 1, 0), turned)
            slices[pl.ds(s * CXC + r, n_gx, stride=CHUNK), :] = turned
    bit = (lax.axis_index("gx") >> 1) & 1
    for k, (at, step) in enumerate(split(n_gx)):
        for out, side in ((sent, 1 - bit), (kept, bit)):
            out[k] = slices[pl.ds(pl.multiple_of((at + step * side) * CHUNK, CHUNK), CHUNK), :]


def trade_kernel(width, got, kept, source, sent, kept_out, held):
    gx = lax.axis_index("gx")
    mine = ((source[...] ^ gx) & width) == 0
    count = got.shape[0]
    for i in range(count):
        held[i] = jnp.where(mine, kept[i], got[i])
    bit = (gx & (2 * width)) // (2 * width)
    for k, (at, step) in enumerate(split(count)):
        sent[k] = held[at + step * (1 - bit)]
        kept_out[k] = held[at + step * bit]


def ends_kernel(width, got, kept, source, gya, gyb, made, pair, ta, tb):
    ta[0:COLS] = gya[...]
    tb[0:COLS] = gyb[...]
    even_y = (lax.axis_index("gy") & 1) == 0
    mine = ((source[...] ^ lax.axis_index("gx")) & width) == 0
    lane = iota((8, CY), 1)
    sub = iota((8, CY), 0)
    digit, group = (lane - 96) % 10, (lane - 96) // 10
    row = jnp.where(digit < 8, digit, jnp.where(digit == 8, group, 3 + group))
    here = (lane >= 96) & (group < 3) & (sub == row)
    tiles = [jnp.zeros((8, CY), F32), jnp.zeros((8, CY), F32)]
    for i in range(4):
        pair[i] = jnp.where(mine, kept[i], got[i])
        for s in range(STEPS):
            tile = pair[i, s * CXC:(s + 1) * CXC, :]
            for k, col in enumerate((CYC - 1, 0)):
                idx = jnp.where(here, jnp.where(digit < 8, group * CYC, 96) + col, 0)
                ends = jnp.sum(jnp.where(here, take(tile, idx), 0.0), axis=0, keepdims=True)
                tiles[k] = jnp.where(sub == 2 * i + s, jnp.broadcast_to(ends, (8, CY)), tiles[k])
    ta[COLS:COLS + 8] = jnp.where(even_y, tiles[0], tiles[1])
    tb[COLS:COLS + 8] = jnp.where(even_y, tiles[1], tiles[0])


def band_rows(BF, BM, own, table, left, right, p, at):
    quarter = (iota(left.shape, 1) // 4) % 4
    for s in range(4):
        f = 4 * p + s
        if f < FIELDS:
            BF[f, at, :] = jnp.where(
                quarter == 0, roll(left, -4 * s, 1),
                jnp.where(quarter == 3, roll(right, 8 - 4 * s, 1), own[f, at, :]),
            )
        if f == FIELDS - 1:
            ids = BF[f, at, :].astype(jnp.int32)
            for k, column in enumerate(spread_table(table)):
                BM[k, at, :] = take(jnp.broadcast_to(column, left.shape), ids)


def edges_kernel(width, quad, cb, ca, token, own, table, sent, kept, BF, BM):
    even_y = (lax.axis_index("gy") & 1) == 0
    for p in range(PACKS):
        at = slice(p * CX, (p + 1) * CX)
        left, right = jnp.where(even_y, cb[at], ca[at]), jnp.where(even_y, ca[at], cb[at])
        band_rows(BF, BM, own, table, left, right, p, slice(0, CX))
    bit = (lax.axis_index("gx") & width) // width
    beside = iota((1, CY), 1) >= 96
    for k, (first, step) in enumerate(split(4)):
        for out, side in ((sent, 1 - bit), (kept, bit)):
            at = first + step * side
            out[k] = quad[at]
            for s in range(STEPS):
                a, b = ca[pl.ds(COLS + 2 * at + s, 1), :], cb[pl.ds(COLS + 2 * at + s, 1), :]
                for j, ends in enumerate((jnp.where(even_y, b, a), jnp.where(even_y, a, b))):
                    put = j * CXC + 6 + s
                    out[k, put:put + 1, :] = jnp.where(beside, ends, out[k, put:put + 1, :])


def spread_table(table):
    scaled = table[...] * 0.1
    spread = jnp.concatenate([scaled] * (CY // ZONES), axis=1)
    return [spread[k:k + 1, :] for k in range(3)]


def material_kernel(zones, table, LAM, MU, BUOY, token):
    token[...] = jnp.zeros(token.shape, F32)
    columns = [jnp.broadcast_to(row, (CX, CY)) for row in spread_table(table)]
    for z in range(NZ):
        ids = zones[z]
        for k, ref in enumerate((LAM, MU, BUOY)):
            ref[z, 0:CX, :] = take(columns[k], ids)


XX, XZ, XY, YY, YZ, ZZ = range(6)


def dx(x):
    return roll(x, RING - 1, 0) - roll(x, 1, 0)


def dy(x, seam, z):
    lane = iota((RING, CY), 1)
    if seam is None:
        return jnp.where(lane == CY - 1, 0.0, roll(x, CY - 1, 1)) - jnp.where(lane == 0, 0.0, roll(x, 1, 1))
    seam = roll(seam, -(16 * z + 3), 1)
    return jnp.where(lane == CY - 1, seam, roll(x, CY - 1, 1)) - jnp.where(lane == 0, seam, roll(x, 1, 1))


def dz(ref, f, z):
    if z == 0:
        return ref[f, 1]
    if z == NZ - 1:
        return -ref[f, NZ - 2]
    return ref[f, z + 1] - ref[f, z - 1]


def band_dy(x):
    return roll(x, CY - 1, 1) - roll(x, 1, 1)


def band_dz(x):
    lane = iota((RING, CY), 1)
    return jnp.where(lane < CY - 16, roll(x, CY - 16, 1), 0.0) - jnp.where(lane >= 16, roll(x, 16, 1), 0.0)


def seams(band, fields):
    lane = iota((RING, CY), 1)
    return {f: jnp.where(lane % 16 == 2, roll(band[f], -10, 1), band[f]) for f in fields}


ALL = (XX, XZ, XY, YY, YZ, ZZ)
FLAT, STEEP = (XX, XY), (XZ, YZ)


def moving(planes, first):
    return [(z, (0, 1) if (z % 2 == 0) == first else (2,)) for z in planes]


def every(planes):
    return [(z, (0, 1, 2)) for z in planes]


def velocity_planes(parts, S, V, MU, BUOY, band, drm):
    seam = {XY: None, YY: None, YZ: None} if band is None else seams(band, (XY, YY, YZ))
    for z, comps in parts:
        for c in comps:
            x, y, vert = ((XX, XY, XZ), (XY, YY, YZ), (XZ, YZ, ZZ))[c]
            force = dx(S[x, z]) + dy(S[y, z], seam[y], z) + dz(S, vert, z)
            if z == NZ - 1:
                force = force + (20.0 * MU[z]) * drm(c, 0)
            V[c, z] = V[c, z] + BUOY[z] * force


def velocity_seams(parts, V, BUOY, band):
    lane = iota((RING, CY), 1)
    sign = jnp.where(lane == 0, -1.0, jnp.where(lane == CY - 1, 1.0, 0.0))
    seam = seams(band, (XY, YY, YZ))
    for z, comps in parts:
        scale = BUOY[z] * sign
        for c in comps:
            V[c, z] = V[c, z] + scale * roll(seam[(XY, YY, YZ)[c]], -(16 * z + 3), 1)


def velocity_band(band, new, BM, drm):
    sxy, sxz, syz = band[XY], band[XZ], band[YZ]
    force = [
        dx(band[XX]) + band_dy(sxy) + band_dz(sxz),
        dx(sxy) + band_dy(band[YY]) + band_dz(syz),
        dx(sxz) + band_dy(syz) + band_dz(band[ZZ]),
    ]
    for c in range(3):
        if drm is not None:
            force[c] = force[c] + (20.0 * BM[1]) * drm(c, 1)
        new[6 + c] = band[6 + c] + BM[2] * force[c]


def stress_plane(z, seam, S, V, LAM, MU, fields):
    vx, vy, vz = V[0, z], V[1, z], V[2, z]
    mu = MU[z]
    if XX in fields:
        lam = LAM[z]
        xx, yy, zz = dx(vx), dy(vy, seam[7], z), dz(V, 2, z)
        theta = lam * (xx + yy + zz)
        two = mu + mu
        S[XX, z] = S[XX, z] + (theta + two * xx)
        S[YY, z] = S[YY, z] + (theta + two * yy)
        S[ZZ, z] = S[ZZ, z] + (theta + two * zz)
    if XZ in fields:
        S[XZ, z] = S[XZ, z] + mu * (dz(V, 0, z) + dx(vz))
    if XY in fields:
        S[XY, z] = S[XY, z] + mu * (dy(vx, seam[6], z) + dx(vy))
    if YZ in fields:
        S[YZ, z] = S[YZ, z] + mu * (dz(V, 1, z) + dy(vz, seam[8], z))


def stress_band(band, new, BM):
    vx, vy, vz = new[6], new[7], new[8]
    lam, mu = BM[0], BM[1]
    xx, yy, zz = dx(vx), band_dy(vy), band_dz(vz)
    theta = lam * (xx + yy + zz)
    two = mu + mu
    new[XX] = band[XX] + (theta + two * xx)
    new[YY] = band[YY] + (theta + two * yy)
    new[ZZ] = band[ZZ] + (theta + two * zz)
    new[XZ] = band[XZ] + mu * (band_dz(vx) + dx(vz))
    new[XY] = band[XY] + mu * (band_dy(vx) + dx(vy))
    new[YZ] = band[YZ] + mu * (band_dz(vy) + band_dy(vz))


def unpack_kernel(
    S_in, V_in, LAM_in, MU_in, BUOY_in, own_in, table, rb, ra,
    S, V, LAM, MU, BUOY, own, ta, tb, zone_tail,
):
    even_x = (lax.axis_index("gx") & 1) == 0
    even_y = (lax.axis_index("gy") & 1) == 0
    low = iota((8, CY), 0) < 4
    slot = iota((8, CY), 1) // HALO
    tail = slice(CX, RING)
    columns = [jnp.broadcast_to(row, (8, CY)) for row in spread_table(table)]

    def place(f, z, rows, at):
        if f < 6:
            S[f, z, CX + at:CX + at + rows.shape[0], :] = rows
        elif f < 9:
            V[f - 6, z, CX + at:CX + at + rows.shape[0], :] = rows
        else:
            zone_tail[z, at:at + rows.shape[0], :] = rows

    for f in range(WIDE):
        for q in range(NZ // 2):
            at = slice(8 * (f * 4 + q), 8 * (f * 4 + q) + 8)
            after = jnp.where(even_x, ra[at], rb[at])
            before = jnp.where(even_x, rb[at], ra[at])
            place(f, 2 * q, jnp.where(low, after, before), 0)
            place(f, 2 * q + 1, roll(jnp.where(low, before, after), 4, 0), 0)
    for f in range(WIDE, FIELDS):
        for z in range(NZ):
            at = pl.ds(ROWS_AT + (f - WIDE) * 24 + z, 3, stride=8)
            a, b = ra[at, :], rb[at, :]
            place(f, z, jnp.zeros((8, CY), F32), 0)
            place(f, z, jnp.where(even_x, a, b), 0)
            place(f, z, jnp.where(even_x, b, a), 5)
    for z in range(NZ):
        ids = zone_tail[z].astype(jnp.int32)
        for column, ref in zip(columns, (LAM, MU, BUOY)):
            ref[z, tail, :] = take(column, ids)
    for p in range(PACKS):
        lasts = jnp.zeros((8, CY), F32)
        firsts = jnp.zeros((8, CY), F32)
        for s in range(4):
            f = 4 * p + s
            if f >= FIELDS:
                continue
            for z in range(NZ):
                rows = S[f, z, tail, :] if f < 6 else V[f - 6, z, tail, :] if f < 9 else zone_tail[z]
                turned = roll(rows, 16 * z + 4 * s + 4, 1)
                at = 4 * z + s
                lasts = jnp.where(slot == at, turned, lasts)
                firsts = jnp.where(slot == (at + 1) % 32, turned, firsts)
        own_band(own, p, tail, lasts, firsts)
        ta[p] = jnp.where(even_y, lasts, firsts)
        tb[p] = jnp.where(even_y, firsts, lasts)


def inner_kernel(S, V_in, MU, BUOY, V, token):
    velocity_planes(moving(range(0, 5), True), S, V, MU, BUOY, None, None)
    token[...] = jnp.zeros(token.shape, F32)


def cone_kernel(
    S_in, V_in, LAM, MU, BUOY, BF_in, BM_in, table, own, tcb, tca, building, block,
    S, V, BF, BM, BV, BW, shares,
):
    even_y = (lax.axis_index("gy") & 1) == 0
    lane8 = iota((8, CY), 1)
    sub8 = iota((8, CY), 0)
    for p in range(PACKS):
        left, right = jnp.where(even_y, tcb[p], tca[p]), jnp.where(even_y, tca[p], tcb[p])
        band_rows(BF, BM, own, table, left, right, p, slice(CX, RING))

    velocity_seams(moving(range(0, 5), True), V, BUOY, BF)
    velocity_band(BF, BW, BM, None)
    for c in range(3):
        BV[c] = BW[6 + c]
    seam = seams(BW, (6, 7, 8))
    for z in range(0, 4):
        stress_plane(z, seam, S, V, LAM, MU, (FLAT, STEEP)[z % 2])
    stress_band(BF, BW, BM)
    velocity_planes(moving(range(0, 3), True), S, V, MU, BUOY, BW, None)
    velocity_band(BW, BW, BM, None)
    stress_plane(1, seams(BW, (8,)), S, V, LAM, MU, (XZ, YZ))

    total = jnp.zeros((8, CY), F32)
    for c, f in enumerate((XZ, YZ)):
        for r in range(CX // BLOCK):
            row = jnp.sum(S[f, 1, 8 * r:8 * r + 8, :], axis=0, keepdims=True)
            total = jnp.where(sub8 == 4 * c + r, jnp.broadcast_to(row, (8, CY)), total)
    for shift in (1, 2, 4):
        total = total + roll(total, CY - shift, 1)
    total = total * (1.0 / (BLOCK * BLOCK))
    ids = jnp.broadcast_to(jnp.concatenate([block[0], block[0]], axis=1), (8, CY))
    cells = CY // BLOCK
    picked = take(total, (ids % cells) * BLOCK)
    mine = (sub8 % 4 == ids // cells) & (sub8 // 4 == lane8 // FP_DEV)
    values = jnp.sum(jnp.where(mine, picked, 0.0), axis=0, keepdims=True)
    names = jnp.concatenate([building[0], building[0]], axis=1).astype(F32)
    message = jnp.concatenate([values, names], axis=0)
    shares[...] = jnp.broadcast_to(message[None], shares.shape)


def upper_kernel(S_in, V_in, LAM, MU, BUOY, BF, BV, BW, S, V):
    velocity_planes(moving(range(0, 5), False) + every(range(5, 7)), S, V, MU, BUOY, BF, None)
    seam = {6 + c: value for c, value in seams(BV, range(3)).items()}
    for z in range(0, 6):
        stress_plane(z, seam, S, V, LAM, MU, ALL if z > 3 else (STEEP, FLAT)[z % 2])
    velocity_planes(moving(range(0, 3), False) + every(range(3, 5)), S, V, MU, BUOY, BW, None)
    seam = seams(BW, (6, 7, 8))
    for z in range(0, 4):
        stress_plane(z, seam, S, V, LAM, MU, FLAT if z == 1 else ALL)


def lower_kernel(
    S_in, V_in, LAM, MU, BUOY, BF_in, BM, source, got, kept,
    S, V, BF, vel_out, stress_out, DRM, drm_in, sems,
):
    saves = []

    def save(ref, out, first, count):
        at = pl.ds(first, count)
        copy = pltpu.make_async_copy(ref.at[:, at, pl.ds(0, CX), :], out.at[:, at], sems.at[len(saves)])
        copy.start()
        saves.append(copy)

    save(V, vel_out, 0, 5)
    save(S, stress_out, 0, 4)
    low = iota((8, CY), 0) < 4
    lane8 = iota((8, CY), 1)
    quarter8 = (lane8 // 4) % 4
    deepest = lane8 >= 16 * (NZ - 1)

    mine = ((source[...] ^ lax.axis_index("gx")) & 1) == 0
    drm_in[...] = jnp.where(mine, kept[0], got[0])

    def wide(row):
        return jnp.broadcast_to(drm_in[row:row + 1, :], (8, CY))

    for s in range(STEPS):
        both = jnp.where(lane8 >= 96, wide(6 + s), roll(wide(CXC + 6 + s), 32, 1))
        for c in range(3):
            for q in range(RING // 8):
                if q < 4:
                    rows = jnp.where(low, wide(s * CXC + 2 * q), wide(s * CXC + 2 * q + 1))
                    base = c * CYC
                else:
                    rows = jnp.where(low, wide(s * CXC + c), wide(s * CXC + 3 + c))
                    base = 3 * CYC
                DRM[s, c, 0, 8 * q:8 * q + 8, :] = take(rows, base + lane8 // COARSE)
                inner = take(rows, base + jnp.where(quarter8 == 2, CYC - 1, 0))
                at = c * 10 + 2 * q + jnp.where(low, 0, 1) + jnp.where(quarter8 == 0, 96, 0)
                value = jnp.where((quarter8 & 1) == (quarter8 >> 1), take(both, at), inner)
                DRM[s, c, 1, 8 * q:8 * q + 8, :] = jnp.where(deepest, value, 0.0)

    def drm(step):
        return lambda c, k: DRM[step, c, k]

    velocity_planes(every(range(7, NZ)), S, V, MU, BUOY, BF, drm(0))
    velocity_band(BF, BF, BM, drm(0))
    seam = seams(BF, (6, 7, 8))
    for z in range(6, NZ):
        stress_plane(z, seam, S, V, LAM, MU, ALL)
    stress_band(BF, BF, BM)
    velocity_planes(every(range(5, NZ)), S, V, MU, BUOY, BF, drm(1))
    velocity_band(BF, BF, BM, drm(1))
    save(V, vel_out, 5, NZ - 5)
    seam = seams(BF, (6, 7, 8))
    for z in range(4, NZ):
        stress_plane(z, seam, S, V, LAM, MU, ALL)
        save(S, stress_out, z, 1)
    for copy in saves:
        copy.wait()


def sum_kernel(n, shares, out):
    half = n // 2
    n_high = BUILDINGS // CY
    low = iota((half, CY), 1) < FP_DEV
    values = shares[:, 0, :]
    names = shares[:, 1, :].astype(jnp.int32)
    names = jnp.where(low, names[:half], names[half:])
    high, names = names // CY, names % CY
    pieces = []
    for rest in (
        jnp.where(low, values[:half], roll(values[half:], FP_DEV, 1)),
        jnp.where(low, roll(values[:half], FP_DEV, 1), values[half:]),
    ):
        for _ in range(3):
            piece = rest.astype(jnp.bfloat16).astype(F32)
            rest = rest - piece
            pieces.append(piece)
    rows = iota((n_high, CY), 0)
    wanted = iota((CY, CY), 0)
    left, hot = [], []
    for k in range(half):
        here = jnp.broadcast_to(high[k:k + 1], (n_high, CY)) == rows
        parts = [jnp.where(here, jnp.broadcast_to(piece[k:k + 1], (n_high, CY)), 0.0) for piece in pieces]
        left.append(jnp.concatenate(parts, axis=0).astype(jnp.bfloat16))
        hot.append((jnp.broadcast_to(names[k:k + 1], (CY, CY)) == wanted).astype(F32).astype(jnp.bfloat16))
    acc = lax.dot_general(
        jnp.concatenate(left, axis=1), jnp.concatenate(hot, axis=1), (((1,), (1,)), ((), ())), preferred_element_type=F32,
    )
    sums = []
    for c in range(2):
        base = 3 * c * n_high
        sums.append(acc[base:base + n_high] + acc[base + n_high:base + 2 * n_high] + acc[base + 2 * n_high:base + 3 * n_high])
    for h in range(n_high):
        out[:, h * CY:(h + 1) * CY] = jnp.concatenate([sums[0][h:h + 1], sums[1][h:h + 1]], axis=0)


def pairs_near(n):
    return [(i, i ^ 1) for i in range(n)]


def pairs_far(n):
    return [(i, (i + 1) % n if i % 2 else (i - 1) % n) for i in range(n)]


def after(x, *done):
    return lax.optimization_barrier((x,) + done)[0]


def body(n_gx, n_gy, velocity, stress, zones, zone_table, regional, owner, building, block):
    n = n_gx * n_gy
    gx = lax.axis_index("gx")
    vmem = pl.BlockSpec(memory_space=pltpu.VMEM)
    hbm = pl.BlockSpec(memory_space=pltpu.HBM)
    anywhere = pl.BlockSpec(memory_space=pl.ANY)
    params = pltpu.CompilerParams(vmem_limit_bytes=VMEM_LIMIT)

    def shaped(*shape):
        return jax.ShapeDtypeStruct(shape, F32)

    def whole(shape, dtype):
        return jax.ShapeDtypeStruct(shape, dtype)

    s_ring = shaped(6, NZ, RING, CY)
    v_ring = shaped(3, NZ, RING, CY)
    m_ring = shaped(NZ, RING, CY)
    rows = shaped(ROWS, CY)
    cols = shaped(COLS, CY)
    from_hbm = [
        pltpu.with_memory_space_constraint(x, pltpu.HBM)
        for x in (velocity, stress, zones, regional, zone_table, building, block, owner)
    ]
    gxa, gxb, regional, zone_table, building, block, source = pl.pallas_call(
        functools.partial(rows_kernel, n_gy),
        out_shape=(
            rows, rows, whole(regional.shape, F32), whole(zone_table.shape, F32),
            whole(building.shape, jnp.int32), whole(block.shape, jnp.int32), whole((CHUNK, CY), jnp.int32),
        ),
        in_specs=[hbm] * 8,
        out_specs=(vmem,) * 7,
        scratch_shapes=[
            pltpu.VMEM((2, 9, NZ, 8, CY), F32),
            pltpu.VMEM((2, NZ, 8, CY), jnp.int32),
            pltpu.SMEM(owner.shape, jnp.int32),
            pltpu.SemaphoreType.DMA((11,)),
        ],
        compiler_params=params,
        name="pack_rows",
    )(*from_hbm)
    rb = lax.ppermute(gxb, "gx", pairs_far(n_gx))
    ra = lax.ppermute(gxa, "gx", pairs_near(n_gx))
    own = shaped(FIELDS, RING, CY)
    S, V, gya, gyb, own = pl.pallas_call(
        cols_kernel,
        out_shape=(s_ring, v_ring, cols, cols, own),
        in_specs=[vmem] * 3,
        out_specs=(vmem,) * 5,
        scratch_shapes=[pltpu.SemaphoreType.DMA((2,))],
        compiler_params=params,
        name="pack_columns",
    )(velocity, stress, zones)

    def across(x, width):
        return lax.ppermute(x, "gx", [(i, i ^ width) for i in range(n_gx)])

    half = shaped(n_gx // 2, CHUNK, CY)
    sent, kept = pl.pallas_call(
        functools.partial(slices_kernel, n_gx),
        out_shape=(half, half),
        in_specs=[vmem],
        out_specs=(vmem,) * 2,
        scratch_shapes=[pltpu.VMEM((n_gx * CHUNK, CY), F32)],
        compiler_params=params,
        name="slices",
    )(regional)
    width = 2
    while 4 * width < n_gx:
        count = sent.shape[0]
        part = shaped(count // 2, CHUNK, CY)
        sent, kept = pl.pallas_call(
            functools.partial(trade_kernel, width),
            out_shape=(part, part),
            in_specs=[vmem] * 3,
            out_specs=(vmem,) * 2,
            scratch_shapes=[pltpu.VMEM((count, CHUNK, CY), F32)],
            compiler_params=params,
            name="trade",
        )(across(sent, width), kept, source)
        width *= 2
    LAM, MU, BUOY, made = pl.pallas_call(
        material_kernel,
        out_shape=(m_ring,) * 3 + (shaped(8, CY),),
        in_specs=[vmem] * 2,
        out_specs=(vmem,) * 4,
        compiler_params=params,
        name="materials",
    )(zones, zone_table)
    message = shaped(COLS + 8, CY)
    quad, message_a, message_b = pl.pallas_call(
        functools.partial(ends_kernel, width),
        out_shape=(shaped(4, CHUNK, CY), message, message),
        in_specs=[vmem] * 5 + [anywhere],
        out_specs=(vmem,) * 3,
        compiler_params=params,
        name="ends",
    )(across(sent, width), kept, source, gya, gyb, made)
    cb = lax.ppermute(message_b, "gy", pairs_far(n_gy))
    ca = lax.ppermute(message_a, "gy", pairs_near(n_gy))
    ends = shaped(PACKS, 8, CY)
    S, V, LAM, MU, BUOY, own, ta, tb = pl.pallas_call(
        unpack_kernel,
        out_shape=(s_ring, v_ring, m_ring, m_ring, m_ring, shaped(FIELDS, RING, CY), ends, ends),
        in_specs=[vmem] * 9,
        out_specs=(vmem,) * 8,
        scratch_shapes=[pltpu.VMEM((NZ, 8, CY), F32)],
        input_output_aliases={k: k for k in range(6)},
        compiler_params=params,
        name="unpack",
    )(S, V, LAM, MU, BUOY, own, zone_table, rb, ra)
    tcb = lax.ppermute(tb, "gy", pairs_far(n_gy))
    tca = lax.ppermute(ta, "gy", pairs_near(n_gy))
    V, token = pl.pallas_call(
        inner_kernel,
        out_shape=(v_ring, shaped(8, CY)),
        in_specs=[vmem] * 4,
        out_specs=(vmem,) * 2,
        input_output_aliases={1: 0},
        compiler_params=params,
        name="inner",
    )(S, V, MU, BUOY)
    two = shaped(2, CHUNK, CY)
    band = shaped(3, RING, CY)
    width *= 2
    sent, kept, BF, BM = pl.pallas_call(
        functools.partial(edges_kernel, width),
        out_shape=(two, two, shaped(FIELDS, RING, CY), band),
        in_specs=[vmem] * 3 + [anywhere] + [vmem] * 2,
        out_specs=(vmem,) * 4,
        compiler_params=params,
        name="edges",
    )(quad, cb, ca, token, own, zone_table)
    S, V, BF, BM, BV, BW, shares = pl.pallas_call(
        cone_kernel,
        out_shape=(s_ring, v_ring, shaped(FIELDS, RING, CY), band, band, shaped(9, RING, CY), shaped(n, 2, CY)),
        in_specs=[vmem] * 13,
        out_specs=(vmem,) * 7,
        input_output_aliases={0: 0, 1: 1, 5: 2, 6: 3},
        compiler_params=params,
        name="cone",
    )(S, V, LAM, MU, BUOY, BF, BM, zone_table, own, tcb, tca, building, block)
    held = jnp.where(((source ^ gx) & width) == 0, kept, across(sent, width))
    odd = (gx & 1) != 0
    sent, kept = jnp.where(odd, held[0], held[1])[None], jnp.where(odd, held[1], held[0])[None]
    got = across(sent, 1)
    gathered = lax.all_to_all(shares, ("gx", "gy"), 0, 0)
    S, V = pl.pallas_call(
        upper_kernel,
        out_shape=(s_ring, v_ring),
        in_specs=[vmem] * 8,
        out_specs=(vmem,) * 2,
        input_output_aliases={0: 0, 1: 1},
        compiler_params=params,
        name="upper",
    )(S, V, LAM, MU, BUOY, BF, BV, BW)
    shear = pl.pallas_call(
        functools.partial(sum_kernel, n),
        out_shape=shaped(2, BUILDINGS),
        in_specs=[vmem],
        out_specs=vmem,
        compiler_params=params,
        name="sum_by_building",
    )(gathered)
    _, _, _, vel_out, stress_out = pl.pallas_call(
        lower_kernel,
        out_shape=(s_ring, v_ring, shaped(FIELDS, RING, CY), shaped(*velocity.shape), shaped(*stress.shape)),
        in_specs=[vmem] * 10,
        out_specs=(vmem, vmem, vmem, hbm, hbm),
        scratch_shapes=[
            pltpu.VMEM((STEPS, 3, 2, RING, CY), F32),
            pltpu.VMEM((CHUNK, CY), F32),
            pltpu.SemaphoreType.DMA((NZ,)),
        ],
        input_output_aliases={0: 0, 1: 1, 5: 2},
        compiler_params=params,
        name="lower",
    )(S, V, LAM, MU, BUOY, BF, BM, source, got, kept)
    return vel_out, stress_out, shear


def solution(mesh):
    n_gx, n_gy = mesh.shape["gx"], mesh.shape["gy"]
    return jax.shard_map(
        functools.partial(body, n_gx, n_gy),
        mesh=mesh,
        in_specs=(
            P(None, None, "gx", "gy"),
            P(None, None, "gx", "gy"),
            P(None, "gx", "gy"),
            P(),
            P("gx", None, None, None, "gy"),
            P(),
            P("gx", "gy", None),
            P("gx", "gy", None),
        ),
        out_specs=(P(None, None, "gx", "gy"), P(None, None, "gx", "gy"), P()),
        check_vma=False,
    )
```

```python
import functools

import jax
import jax.numpy as jnp
from jax import lax
from jax.experimental import pallas as pl
from jax.experimental.pallas import tpu as pltpu
from jax.sharding import PartitionSpec as P

CX = 32
CY = 128
NZ = 8
STEPS = 2
COARSE = 4
BLOCK = 8
ZONES = 16
BUILDINGS = 1024
FP_DEV = 64
HALO = 4
RING = CX + 2 * HALO
FIELDS = 10
WIDE = 3
WIDE_AT = (FIELDS - WIDE) * 3 * 8
ROWS = WIDE_AT + WIDE * 4 * 8
PACKS = 3
CHUNK = 16
COLS = PACKS * CX
CXC = CX // COARSE
CYC = CY // COARSE
F32 = jnp.float32
VMEM_LIMIT = 32 * 1024 * 1024


def iota(shape, dim):
    return lax.broadcasted_iota(jnp.int32, shape, dim)


def take(x, idx):
    idx = jnp.broadcast_to(idx, x.shape)
    return jnp.take_along_axis(x, idx, axis=1, mode="promise_in_bounds")


def roll(x, shift, axis):
    size = x.shape[axis]
    shift = shift % size
    return x if shift == 0 else pltpu.roll(x, shift, axis)


def rows_kernel(
    n_gy, vel, stress, zones, regional_in, table_in, building_in, block_in, owner_in,
    gxa, gxb, regional, table, building, block, source, F, Z, owner, sems,
):
    even_x = (lax.axis_index("gx") & 1) == 0
    low = iota((8, CY), 0) < 4
    loads = []
    for end, at in enumerate((0, CX - HALO)):
        rows, to = pl.ds(at, HALO), pl.ds(HALO * end, HALO)
        loads.append(pltpu.make_async_copy(stress.at[:, :, rows, :], F.at[end, pl.ds(0, 6), :, to], sems.at[3 * end]))
        loads.append(pltpu.make_async_copy(vel.at[:, :, rows, :], F.at[end, pl.ds(6, 3), :, to], sems.at[3 * end + 1]))
        loads.append(pltpu.make_async_copy(zones.at[:, rows, :], Z.at[end, :, to], sems.at[3 * end + 2]))
    small = ((owner_in, owner), (regional_in, regional), (table_in, table), (building_in, building), (block_in, block))
    loads += [pltpu.make_async_copy(src, dst, sems.at[6 + k]) for k, (src, dst) in enumerate(small)]
    for copy in loads:
        copy.start()
    for copy in loads:
        copy.wait()

    def tile(f, z, end):
        return F[end, f, z] if f < 9 else Z[end, z].astype(F32)

    gy = lax.axis_index("gy")
    row = iota((CHUNK, CY), 0)
    edge = (iota((CHUNK, CY), 1) >= 96) & ((row & 7) >= 6)
    sides = jnp.where(row < CXC, owner[(gy + n_gy - 1) % n_gy], owner[(gy + 1) % n_gy])
    source[...] = jnp.where(edge, sides, owner[gy])

    for f in range(WIDE):
        for q in range(NZ // 2):
            first = jnp.where(low, tile(f, 2 * q, 0), roll(tile(f, 2 * q + 1, 0), 4, 0))
            last = jnp.where(low, roll(tile(f, 2 * q + 1, 1), 4, 0), tile(f, 2 * q, 1))
            at = WIDE_AT + 8 * (f * 4 + q)
            gxa[at:at + 8, :] = jnp.where(even_x, last, first)
            gxb[at:at + 8, :] = jnp.where(even_x, first, last)
    for f in range(WIDE, FIELDS):
        for z in range(NZ):
            first, last = tile(f, z, 0), roll(tile(f, z, 1), 3, 0)
            at = pl.ds((f - WIDE) * 24 + z, 3, stride=8)
            gxa[at, :] = jnp.where(even_x, last, first)[0:3]
            gxb[at, :] = jnp.where(even_x, first, last)[0:3]


def own_band(own, p, at, lasts, firsts):
    inner = (iota(lasts.shape, 1) // 4) % 4 == 1
    for s in range(4):
        if 4 * p + s < FIELDS:
            own[4 * p + s, at, :] = jnp.where(inner, roll(firsts, -4 * s, 1), roll(lasts, 8 - 4 * s, 1))


def cols_kernel(vel, stress, zones, S, V, gya, gyb, own, sems):
    even_y = (lax.axis_index("gy") & 1) == 0
    inner = pl.ds(0, CX)
    loads = [
        pltpu.make_async_copy(stress, S.at[:, :, inner, :], sems.at[0]),
        pltpu.make_async_copy(vel, V.at[:, :, inner, :], sems.at[1]),
    ]
    for copy in loads:
        copy.start()
    slot = iota((CX, CY), 1) // HALO

    def plane(f, z):
        if f < 6:
            return stress[f, z]
        if f < 9:
            return vel[f - 6, z]
        return zones[z].astype(F32)

    for p in range(PACKS):
        lasts = jnp.zeros((CX, CY), F32)
        firsts = jnp.zeros((CX, CY), F32)
        for s in range(4):
            f = 4 * p + s
            if f >= FIELDS:
                continue
            for z in range(NZ):
                turned = roll(plane(f, z), 16 * z + 4 * s + 4, 1)
                at = 4 * z + s
                lasts = jnp.where(slot == at, turned, lasts)
                firsts = jnp.where(slot == (at + 1) % 32, turned, firsts)
        own_band(own, p, slice(0, CX), lasts, firsts)
        gya[p * CX:(p + 1) * CX, :] = jnp.where(even_y, lasts, firsts)
        gyb[p * CX:(p + 1) * CX, :] = jnp.where(even_y, firsts, lasts)

    for copy in loads:
        copy.wait()


def split(count):
    return [(4 * (k // 2) + k % 2, 2) for k in range(count // 2)]


def slices_kernel(n_gx, R, sent, kept, slices):
    part = iota((n_gx, CY), 1) // CYC
    for s in range(STEPS):
        halves = [[R[0, s, c, :, t * CY:(t + 1) * CY] for t in range(2)] for c in range(3)]
        for r in range(CXC):
            turned = jnp.zeros((n_gx, CY), F32)
            for c in range(3):
                turned = jnp.where(part == c, roll(halves[c][r // 4], CYC * (c - r % 4), 1), turned)
            if r < 3:
                turned = jnp.where(part == 3, roll(roll(halves[r][0], n_gx - 1, 0), 96, 1), turned)
            elif r < 6:
                turned = jnp.where(part == 3, roll(halves[r - 3][1], 1, 0), turned)
            slices[pl.ds(s * CXC + r, n_gx, stride=CHUNK), :] = turned
    bit = (lax.axis_index("gx") >> 1) & 1
    for k, (at, step) in enumerate(split(n_gx)):
        for out, side in ((sent, 1 - bit), (kept, bit)):
            out[k] = slices[pl.ds(pl.multiple_of((at + step * side) * CHUNK, CHUNK), CHUNK), :]


def trade_kernel(width, got, kept, source, sent, kept_out, held):
    gx = lax.axis_index("gx")
    mine = ((source[...] ^ gx) & width) == 0
    count = got.shape[0]
    for i in range(count):
        held[i] = jnp.where(mine, kept[i], got[i])
    bit = (gx & (2 * width)) // (2 * width)
    for k, (at, step) in enumerate(split(count)):
        sent[k] = held[at + step * (1 - bit)]
        kept_out[k] = held[at + step * bit]


def ends_kernel(width, got, kept, source, gya, gyb, made, pair, ta, tb):
    ta[0:COLS] = gya[...]
    tb[0:COLS] = gyb[...]
    even_y = (lax.axis_index("gy") & 1) == 0
    mine = ((source[...] ^ lax.axis_index("gx")) & width) == 0
    lane = iota((8, CY), 1)
    sub = iota((8, CY), 0)
    digit, group = (lane - 96) % 10, (lane - 96) // 10
    row = jnp.where(digit < 8, digit, jnp.where(digit == 8, group, 3 + group))
    here = (lane >= 96) & (group < 3) & (sub == row)
    tiles = [jnp.zeros((8, CY), F32), jnp.zeros((8, CY), F32)]
    for i in range(4):
        pair[i] = jnp.where(mine, kept[i], got[i])
        for s in range(STEPS):
            tile = pair[i, s * CXC:(s + 1) * CXC, :]
            for k, col in enumerate((CYC - 1, 0)):
                idx = jnp.where(here, jnp.where(digit < 8, group * CYC, 96) + col, 0)
                ends = jnp.sum(jnp.where(here, take(tile, idx), 0.0), axis=0, keepdims=True)
                tiles[k] = jnp.where(sub == 2 * i + s, jnp.broadcast_to(ends, (8, CY)), tiles[k])
    ta[COLS:COLS + 8] = jnp.where(even_y, tiles[0], tiles[1])
    tb[COLS:COLS + 8] = jnp.where(even_y, tiles[1], tiles[0])


def band_rows(BF, BM, own, table, left, right, p, at):
    quarter = (iota(left.shape, 1) // 4) % 4
    for s in range(4):
        f = 4 * p + s
        if f < FIELDS:
            BF[f, at, :] = jnp.where(
                quarter == 0, roll(left, -4 * s, 1),
                jnp.where(quarter == 3, roll(right, 8 - 4 * s, 1), own[f, at, :]),
            )
        if f == FIELDS - 1:
            ids = BF[f, at, :].astype(jnp.int32)
            for k, column in enumerate(spread_table(table)):
                BM[k, at, :] = take(jnp.broadcast_to(column, left.shape), ids)


def edges_kernel(width, quad, cb, ca, token, own, table, sent, kept, BF, BM):
    even_y = (lax.axis_index("gy") & 1) == 0
    for p in range(PACKS):
        at = slice(p * CX, (p + 1) * CX)
        left, right = jnp.where(even_y, cb[at], ca[at]), jnp.where(even_y, ca[at], cb[at])
        band_rows(BF, BM, own, table, left, right, p, slice(0, CX))
    bit = (lax.axis_index("gx") & width) // width
    beside = iota((1, CY), 1) >= 96
    for k, (first, step) in enumerate(split(4)):
        for out, side in ((sent, 1 - bit), (kept, bit)):
            at = first + step * side
            out[k] = quad[at]
            for s in range(STEPS):
                a, b = ca[pl.ds(COLS + 2 * at + s, 1), :], cb[pl.ds(COLS + 2 * at + s, 1), :]
                for j, ends in enumerate((jnp.where(even_y, b, a), jnp.where(even_y, a, b))):
                    put = j * CXC + 6 + s
                    out[k, put:put + 1, :] = jnp.where(beside, ends, out[k, put:put + 1, :])


def spread_table(table):
    scaled = table[...] * 0.1
    spread = jnp.concatenate([scaled] * (CY // ZONES), axis=1)
    return [spread[k:k + 1, :] for k in range(3)]


def material_kernel(zones, table, LAM, MU, BUOY, token):
    token[...] = jnp.zeros(token.shape, F32)
    columns = [jnp.broadcast_to(row, (CX, CY)) for row in spread_table(table)]
    for z in range(NZ):
        ids = zones[z]
        for k, ref in enumerate((LAM, MU, BUOY)):
            ref[z, 0:CX, :] = take(columns[k], ids)


XX, XZ, XY, YY, YZ, ZZ = range(6)


def dx(x):
    return roll(x, RING - 1, 0) - roll(x, 1, 0)


def dy(x, seam, z):
    lane = iota((RING, CY), 1)
    if seam is None:
        return jnp.where(lane == CY - 1, 0.0, roll(x, CY - 1, 1)) - jnp.where(lane == 0, 0.0, roll(x, 1, 1))
    seam = roll(seam, -(16 * z + 3), 1)
    return jnp.where(lane == CY - 1, seam, roll(x, CY - 1, 1)) - jnp.where(lane == 0, seam, roll(x, 1, 1))


def dz(ref, f, z):
    if z == 0:
        return ref[f, 1]
    if z == NZ - 1:
        return -ref[f, NZ - 2]
    return ref[f, z + 1] - ref[f, z - 1]


def band_dy(x):
    return roll(x, CY - 1, 1) - roll(x, 1, 1)


def band_dz(x):
    lane = iota((RING, CY), 1)
    return jnp.where(lane < CY - 16, roll(x, CY - 16, 1), 0.0) - jnp.where(lane >= 16, roll(x, 16, 1), 0.0)


def seams(band, fields):
    lane = iota((RING, CY), 1)
    return {f: jnp.where(lane % 16 == 2, roll(band[f], -10, 1), band[f]) for f in fields}


ALL = (XX, XZ, XY, YY, YZ, ZZ)
FLAT, STEEP = (XX, XY), (XZ, YZ)


def moving(planes, first):
    return [(z, (0, 1) if (z % 2 == 0) == first else (2,)) for z in planes]


def every(planes):
    return [(z, (0, 1, 2)) for z in planes]


def velocity_planes(parts, S, V, MU, BUOY, band, drm):
    seam = {XY: None, YY: None, YZ: None} if band is None else seams(band, (XY, YY, YZ))
    for z, comps in parts:
        for c in comps:
            x, y, vert = ((XX, XY, XZ), (XY, YY, YZ), (XZ, YZ, ZZ))[c]
            force = dx(S[x, z]) + dy(S[y, z], seam[y], z) + dz(S, vert, z)
            if z == NZ - 1:
                force = force + (20.0 * MU[z]) * drm(c, 0)
            V[c, z] = V[c, z] + BUOY[z] * force


def velocity_seams(parts, V, BUOY, band):
    lane = iota((RING, CY), 1)
    sign = jnp.where(lane == 0, -1.0, jnp.where(lane == CY - 1, 1.0, 0.0))
    seam = seams(band, (XY, YY, YZ))
    for z, comps in parts:
        scale = BUOY[z] * sign
        for c in comps:
            V[c, z] = V[c, z] + scale * roll(seam[(XY, YY, YZ)[c]], -(16 * z + 3), 1)


def velocity_band(band, new, BM, drm):
    sxy, sxz, syz = band[XY], band[XZ], band[YZ]
    force = [
        dx(band[XX]) + band_dy(sxy) + band_dz(sxz),
        dx(sxy) + band_dy(band[YY]) + band_dz(syz),
        dx(sxz) + band_dy(syz) + band_dz(band[ZZ]),
    ]
    for c in range(3):
        if drm is not None:
            force[c] = force[c] + (20.0 * BM[1]) * drm(c, 1)
        new[6 + c] = band[6 + c] + BM[2] * force[c]


def stress_plane(z, seam, S, V, LAM, MU, fields):
    vx, vy, vz = V[0, z], V[1, z], V[2, z]
    mu = MU[z]
    if XX in fields:
        lam = LAM[z]
        xx, yy, zz = dx(vx), dy(vy, seam[7], z), dz(V, 2, z)
        theta = lam * (xx + yy + zz)
        two = mu + mu
        S[XX, z] = S[XX, z] + (theta + two * xx)
        S[YY, z] = S[YY, z] + (theta + two * yy)
        S[ZZ, z] = S[ZZ, z] + (theta + two * zz)
    if XZ in fields:
        S[XZ, z] = S[XZ, z] + mu * (dz(V, 0, z) + dx(vz))
    if XY in fields:
        S[XY, z] = S[XY, z] + mu * (dy(vx, seam[6], z) + dx(vy))
    if YZ in fields:
        S[YZ, z] = S[YZ, z] + mu * (dz(V, 1, z) + dy(vz, seam[8], z))


def stress_band(band, new, BM):
    vx, vy, vz = new[6], new[7], new[8]
    lam, mu = BM[0], BM[1]
    xx, yy, zz = dx(vx), band_dy(vy), band_dz(vz)
    theta = lam * (xx + yy + zz)
    two = mu + mu
    new[XX] = band[XX] + (theta + two * xx)
    new[YY] = band[YY] + (theta + two * yy)
    new[ZZ] = band[ZZ] + (theta + two * zz)
    new[XZ] = band[XZ] + mu * (band_dz(vx) + dx(vz))
    new[XY] = band[XY] + mu * (band_dy(vx) + dx(vy))
    new[YZ] = band[YZ] + mu * (band_dz(vy) + band_dy(vz))


def unpack_kernel(
    S_in, V_in, LAM_in, MU_in, BUOY_in, own_in, table, rb, ra,
    S, V, LAM, MU, BUOY, own, ta, tb, zone_tail,
):
    even_x = (lax.axis_index("gx") & 1) == 0
    even_y = (lax.axis_index("gy") & 1) == 0
    low = iota((8, CY), 0) < 4
    slot = iota((8, CY), 1) // HALO
    tail = slice(CX, RING)
    columns = [jnp.broadcast_to(row, (8, CY)) for row in spread_table(table)]

    def place(f, z, rows):
        if f < 6:
            S[f, z, tail, :] = rows
        elif f < 9:
            V[f - 6, z, tail, :] = rows
        else:
            zone_tail[z] = rows

    for f in range(WIDE):
        for q in range(NZ // 2):
            at = slice(WIDE_AT + 8 * (f * 4 + q), WIDE_AT + 8 * (f * 4 + q) + 8)
            after = jnp.where(even_x, ra[at], rb[at])
            before = jnp.where(even_x, rb[at], ra[at])
            place(f, 2 * q, jnp.where(low, after, before))
            place(f, 2 * q + 1, roll(jnp.where(low, before, after), 4, 0))
    sub = iota((8, CY), 0)
    for f in range(WIDE, FIELDS):
        for z in range(NZ):
            at = pl.ds((f - WIDE) * 24 + z, 8, stride=8)
            a, b = ra[at, :], rb[at, :]
            after, before = jnp.where(even_x, a, b), roll(jnp.where(even_x, b, a), 5, 0)
            place(f, z, jnp.where(sub < 3, after, jnp.where(sub >= 5, before, 0.0)))
    for z in range(NZ):
        ids = zone_tail[z].astype(jnp.int32)
        for column, ref in zip(columns, (LAM, MU, BUOY)):
            ref[z, tail, :] = take(column, ids)
    for p in range(PACKS):
        lasts = jnp.zeros((8, CY), F32)
        firsts = jnp.zeros((8, CY), F32)
        for s in range(4):
            f = 4 * p + s
            if f >= FIELDS:
                continue
            for z in range(NZ):
                rows = S[f, z, tail, :] if f < 6 else V[f - 6, z, tail, :] if f < 9 else zone_tail[z]
                turned = roll(rows, 16 * z + 4 * s + 4, 1)
                at = 4 * z + s
                lasts = jnp.where(slot == at, turned, lasts)
                firsts = jnp.where(slot == (at + 1) % 32, turned, firsts)
        own_band(own, p, tail, lasts, firsts)
        ta[p] = jnp.where(even_y, lasts, firsts)
        tb[p] = jnp.where(even_y, firsts, lasts)


def inner_kernel(S, V_in, MU, BUOY, V, token):
    velocity_planes(moving(range(0, 5), True), S, V, MU, BUOY, None, None)
    token[...] = jnp.zeros(token.shape, F32)


def cone_kernel(
    S_in, V_in, LAM, MU, BUOY, BF_in, BM_in, table, own, tcb, tca, building, block,
    S, V, BF, BM, BV, BW, shares,
):
    even_y = (lax.axis_index("gy") & 1) == 0
    lane8 = iota((8, CY), 1)
    sub8 = iota((8, CY), 0)
    for p in range(PACKS):
        left, right = jnp.where(even_y, tcb[p], tca[p]), jnp.where(even_y, tca[p], tcb[p])
        band_rows(BF, BM, own, table, left, right, p, slice(CX, RING))

    velocity_seams(moving(range(0, 5), True), V, BUOY, BF)
    velocity_band(BF, BW, BM, None)
    for c in range(3):
        BV[c] = BW[6 + c]
    seam = seams(BW, (6, 7, 8))
    for z in range(0, 4):
        stress_plane(z, seam, S, V, LAM, MU, (FLAT, STEEP)[z % 2])
    stress_band(BF, BW, BM)
    velocity_planes(moving(range(0, 3), True), S, V, MU, BUOY, BW, None)
    velocity_band(BW, BW, BM, None)
    stress_plane(1, seams(BW, (8,)), S, V, LAM, MU, (XZ, YZ))

    total = jnp.zeros((8, CY), F32)
    for c, f in enumerate((XZ, YZ)):
        for r in range(CX // BLOCK):
            row = jnp.sum(S[f, 1, 8 * r:8 * r + 8, :], axis=0, keepdims=True)
            total = jnp.where(sub8 == 4 * c + r, jnp.broadcast_to(row, (8, CY)), total)
    for shift in (1, 2, 4):
        total = total + roll(total, CY - shift, 1)
    total = total * (1.0 / (BLOCK * BLOCK))
    ids = jnp.broadcast_to(jnp.concatenate([block[0], block[0]], axis=1), (8, CY))
    cells = CY // BLOCK
    picked = take(total, (ids % cells) * BLOCK)
    mine = (sub8 % 4 == ids // cells) & (sub8 // 4 == lane8 // FP_DEV)
    values = jnp.sum(jnp.where(mine, picked, 0.0), axis=0, keepdims=True)
    names = jnp.concatenate([building[0], building[0]], axis=1).astype(F32)
    message = jnp.concatenate([values, names], axis=0)
    shares[...] = jnp.broadcast_to(message[None], shares.shape)


def upper_kernel(S_in, V_in, LAM, MU, BUOY, BF, BV, BW, S, V):
    velocity_planes(moving(range(0, 5), False) + every(range(5, 7)), S, V, MU, BUOY, BF, None)
    seam = {6 + c: value for c, value in seams(BV, range(3)).items()}
    for z in range(0, 6):
        stress_plane(z, seam, S, V, LAM, MU, ALL if z > 3 else (STEEP, FLAT)[z % 2])
    velocity_planes(moving(range(0, 3), False) + every(range(3, 5)), S, V, MU, BUOY, BW, None)
    seam = seams(BW, (6, 7, 8))
    for z in range(0, 4):
        stress_plane(z, seam, S, V, LAM, MU, FLAT if z == 1 else ALL)


def lower_kernel(
    S_in, V_in, LAM, MU, BUOY, BF_in, BM, source, got, kept,
    S, V, BF, vel_out, stress_out, DRM, drm_in, sems,
):
    saves = []

    def save(ref, out, first, count):
        at = pl.ds(first, count)
        copy = pltpu.make_async_copy(ref.at[:, at, pl.ds(0, CX), :], out.at[:, at], sems.at[len(saves)])
        copy.start()
        saves.append(copy)

    save(V, vel_out, 0, 5)
    save(S, stress_out, 0, 4)
    low = iota((8, CY), 0) < 4
    lane8 = iota((8, CY), 1)
    quarter8 = (lane8 // 4) % 4
    deepest = lane8 >= 16 * (NZ - 1)

    mine = ((source[...] ^ lax.axis_index("gx")) & 1) == 0
    drm_in[...] = jnp.where(mine, kept[0], got[0])

    def wide(row):
        return jnp.broadcast_to(drm_in[row:row + 1, :], (8, CY))

    for s in range(STEPS):
        both = jnp.where(lane8 >= 96, wide(6 + s), roll(wide(CXC + 6 + s), 32, 1))
        for c in range(3):
            for q in range(RING // 8):
                if q < 4:
                    rows = jnp.where(low, wide(s * CXC + 2 * q), wide(s * CXC + 2 * q + 1))
                    base = c * CYC
                else:
                    rows = jnp.where(low, wide(s * CXC + c), wide(s * CXC + 3 + c))
                    base = 3 * CYC
                DRM[s, c, 0, 8 * q:8 * q + 8, :] = take(rows, base + lane8 // COARSE)
                inner = take(rows, base + jnp.where(quarter8 == 2, CYC - 1, 0))
                at = c * 10 + 2 * q + jnp.where(low, 0, 1) + jnp.where(quarter8 == 0, 96, 0)
                value = jnp.where((quarter8 & 1) == (quarter8 >> 1), take(both, at), inner)
                DRM[s, c, 1, 8 * q:8 * q + 8, :] = jnp.where(deepest, value, 0.0)

    def drm(step):
        return lambda c, k: DRM[step, c, k]

    velocity_planes(every(range(7, NZ)), S, V, MU, BUOY, BF, drm(0))
    velocity_band(BF, BF, BM, drm(0))
    seam = seams(BF, (6, 7, 8))
    for z in range(6, NZ):
        stress_plane(z, seam, S, V, LAM, MU, ALL)
    stress_band(BF, BF, BM)
    velocity_planes(every(range(5, NZ)), S, V, MU, BUOY, BF, drm(1))
    velocity_band(BF, BF, BM, drm(1))
    save(V, vel_out, 5, NZ - 5)
    seam = seams(BF, (6, 7, 8))
    for z in range(4, NZ):
        stress_plane(z, seam, S, V, LAM, MU, ALL)
        save(S, stress_out, z, 1)
    for copy in saves:
        copy.wait()


def sum_kernel(n, shares, out):
    half = n // 2
    n_high = BUILDINGS // CY
    low = iota((half, CY), 1) < FP_DEV
    values = shares[:, 0, :]
    names = shares[:, 1, :].astype(jnp.int32)
    names = jnp.where(low, names[:half], names[half:])
    high, names = names // CY, names % CY
    pieces = []
    for rest in (
        jnp.where(low, values[:half], roll(values[half:], FP_DEV, 1)),
        jnp.where(low, roll(values[:half], FP_DEV, 1), values[half:]),
    ):
        for _ in range(3):
            piece = rest.astype(jnp.bfloat16).astype(F32)
            rest = rest - piece
            pieces.append(piece)
    rows = iota((n_high, CY), 0)
    wanted = iota((CY, CY), 0)
    left, hot = [], []
    for k in range(half):
        here = jnp.broadcast_to(high[k:k + 1], (n_high, CY)) == rows
        parts = [jnp.where(here, jnp.broadcast_to(piece[k:k + 1], (n_high, CY)), 0.0) for piece in pieces]
        left.append(jnp.concatenate(parts, axis=0).astype(jnp.bfloat16))
        hot.append((jnp.broadcast_to(names[k:k + 1], (CY, CY)) == wanted).astype(F32).astype(jnp.bfloat16))
    acc = lax.dot_general(
        jnp.concatenate(left, axis=1), jnp.concatenate(hot, axis=1), (((1,), (1,)), ((), ())), preferred_element_type=F32,
    )
    sums = []
    for c in range(2):
        base = 3 * c * n_high
        sums.append(acc[base:base + n_high] + acc[base + n_high:base + 2 * n_high] + acc[base + 2 * n_high:base + 3 * n_high])
    for h in range(n_high):
        out[:, h * CY:(h + 1) * CY] = jnp.concatenate([sums[0][h:h + 1], sums[1][h:h + 1]], axis=0)


def pairs_near(n):
    return [(i, i ^ 1) for i in range(n)]


def pairs_far(n):
    return [(i, (i + 1) % n if i % 2 else (i - 1) % n) for i in range(n)]


def after(x, *done):
    return lax.optimization_barrier((x,) + done)[0]


def body(n_gx, n_gy, velocity, stress, zones, zone_table, regional, owner, building, block):
    n = n_gx * n_gy
    gx = lax.axis_index("gx")
    vmem = pl.BlockSpec(memory_space=pltpu.VMEM)
    hbm = pl.BlockSpec(memory_space=pltpu.HBM)
    anywhere = pl.BlockSpec(memory_space=pl.ANY)
    params = pltpu.CompilerParams(vmem_limit_bytes=VMEM_LIMIT)

    def shaped(*shape):
        return jax.ShapeDtypeStruct(shape, F32)

    def whole(shape, dtype):
        return jax.ShapeDtypeStruct(shape, dtype)

    s_ring = shaped(6, NZ, RING, CY)
    v_ring = shaped(3, NZ, RING, CY)
    m_ring = shaped(NZ, RING, CY)
    rows = shaped(ROWS, CY)
    cols = shaped(COLS, CY)
    from_hbm = [
        pltpu.with_memory_space_constraint(x, pltpu.HBM)
        for x in (velocity, stress, zones, regional, zone_table, building, block, owner)
    ]
    gxa, gxb, regional, zone_table, building, block, source = pl.pallas_call(
        functools.partial(rows_kernel, n_gy),
        out_shape=(
            rows, rows, whole(regional.shape, F32), whole(zone_table.shape, F32),
            whole(building.shape, jnp.int32), whole(block.shape, jnp.int32), whole((CHUNK, CY), jnp.int32),
        ),
        in_specs=[hbm] * 8,
        out_specs=(vmem,) * 7,
        scratch_shapes=[
            pltpu.VMEM((2, 9, NZ, 8, CY), F32),
            pltpu.VMEM((2, NZ, 8, CY), jnp.int32),
            pltpu.SMEM(owner.shape, jnp.int32),
            pltpu.SemaphoreType.DMA((11,)),
        ],
        compiler_params=params,
        name="pack_rows",
    )(*from_hbm)
    rb = lax.ppermute(gxb, "gx", pairs_far(n_gx))
    ra = lax.ppermute(gxa, "gx", pairs_near(n_gx))
    own = shaped(FIELDS, RING, CY)
    S, V, gya, gyb, own = pl.pallas_call(
        cols_kernel,
        out_shape=(s_ring, v_ring, cols, cols, own),
        in_specs=[vmem] * 3,
        out_specs=(vmem,) * 5,
        scratch_shapes=[pltpu.SemaphoreType.DMA((2,))],
        compiler_params=params,
        name="pack_columns",
    )(velocity, stress, zones)

    def across(x, width):
        return lax.ppermute(x, "gx", [(i, i ^ width) for i in range(n_gx)])

    half = shaped(n_gx // 2, CHUNK, CY)
    sent, kept = pl.pallas_call(
        functools.partial(slices_kernel, n_gx),
        out_shape=(half, half),
        in_specs=[vmem],
        out_specs=(vmem,) * 2,
        scratch_shapes=[pltpu.VMEM((n_gx * CHUNK, CY), F32)],
        compiler_params=params,
        name="slices",
    )(regional)
    width = 2
    while 4 * width < n_gx:
        count = sent.shape[0]
        part = shaped(count // 2, CHUNK, CY)
        sent, kept = pl.pallas_call(
            functools.partial(trade_kernel, width),
            out_shape=(part, part),
            in_specs=[vmem] * 3,
            out_specs=(vmem,) * 2,
            scratch_shapes=[pltpu.VMEM((count, CHUNK, CY), F32)],
            compiler_params=params,
            name="trade",
        )(across(sent, width), kept, source)
        width *= 2
    LAM, MU, BUOY, made = pl.pallas_call(
        material_kernel,
        out_shape=(m_ring,) * 3 + (shaped(8, CY),),
        in_specs=[vmem] * 2,
        out_specs=(vmem,) * 4,
        compiler_params=params,
        name="materials",
    )(zones, zone_table)
    message = shaped(COLS + 8, CY)
    quad, message_a, message_b = pl.pallas_call(
        functools.partial(ends_kernel, width),
        out_shape=(shaped(4, CHUNK, CY), message, message),
        in_specs=[vmem] * 5 + [anywhere],
        out_specs=(vmem,) * 3,
        compiler_params=params,
        name="ends",
    )(across(sent, width), kept, source, gya, gyb, made)
    cb = lax.ppermute(message_b, "gy", pairs_far(n_gy))
    ca = lax.ppermute(message_a, "gy", pairs_near(n_gy))
    ends = shaped(PACKS, 8, CY)
    S, V, LAM, MU, BUOY, own, ta, tb = pl.pallas_call(
        unpack_kernel,
        out_shape=(s_ring, v_ring, m_ring, m_ring, m_ring, shaped(FIELDS, RING, CY), ends, ends),
        in_specs=[vmem] * 9,
        out_specs=(vmem,) * 8,
        scratch_shapes=[pltpu.VMEM((NZ, 8, CY), F32)],
        input_output_aliases={k: k for k in range(6)},
        compiler_params=params,
        name="unpack",
    )(S, V, LAM, MU, BUOY, own, zone_table, rb, ra)
    tcb = lax.ppermute(tb, "gy", pairs_far(n_gy))
    tca = lax.ppermute(ta, "gy", pairs_near(n_gy))
    V, token = pl.pallas_call(
        inner_kernel,
        out_shape=(v_ring, shaped(8, CY)),
        in_specs=[vmem] * 4,
        out_specs=(vmem,) * 2,
        input_output_aliases={1: 0},
        compiler_params=params,
        name="inner",
    )(S, V, MU, BUOY)
    two = shaped(2, CHUNK, CY)
    band = shaped(3, RING, CY)
    width *= 2
    sent, kept, BF, BM = pl.pallas_call(
        functools.partial(edges_kernel, width),
        out_shape=(two, two, shaped(FIELDS, RING, CY), band),
        in_specs=[vmem] * 3 + [anywhere] + [vmem] * 2,
        out_specs=(vmem,) * 4,
        compiler_params=params,
        name="edges",
    )(quad, cb, ca, token, own, zone_table)
    S, V, BF, BM, BV, BW, shares = pl.pallas_call(
        cone_kernel,
        out_shape=(s_ring, v_ring, shaped(FIELDS, RING, CY), band, band, shaped(9, RING, CY), shaped(n, 2, CY)),
        in_specs=[vmem] * 13,
        out_specs=(vmem,) * 7,
        input_output_aliases={0: 0, 1: 1, 5: 2, 6: 3},
        compiler_params=params,
        name="cone",
    )(S, V, LAM, MU, BUOY, BF, BM, zone_table, own, tcb, tca, building, block)
    held = jnp.where(((source ^ gx) & width) == 0, kept, across(sent, width))
    odd = (gx & 1) != 0
    sent, kept = jnp.where(odd, held[0], held[1])[None], jnp.where(odd, held[1], held[0])[None]
    got = across(sent, 1)
    gathered = lax.all_to_all(shares, ("gx", "gy"), 0, 0)
    S, V = pl.pallas_call(
        upper_kernel,
        out_shape=(s_ring, v_ring),
        in_specs=[vmem] * 8,
        out_specs=(vmem,) * 2,
        input_output_aliases={0: 0, 1: 1},
        compiler_params=params,
        name="upper",
    )(S, V, LAM, MU, BUOY, BF, BV, BW)
    shear = pl.pallas_call(
        functools.partial(sum_kernel, n),
        out_shape=shaped(2, BUILDINGS),
        in_specs=[vmem],
        out_specs=vmem,
        compiler_params=params,
        name="sum_by_building",
    )(gathered)
    _, _, _, vel_out, stress_out = pl.pallas_call(
        lower_kernel,
        out_shape=(s_ring, v_ring, shaped(FIELDS, RING, CY), shaped(*velocity.shape), shaped(*stress.shape)),
        in_specs=[vmem] * 10,
        out_specs=(vmem, vmem, vmem, hbm, hbm),
        scratch_shapes=[
            pltpu.VMEM((STEPS, 3, 2, RING, CY), F32),
            pltpu.VMEM((CHUNK, CY), F32),
            pltpu.SemaphoreType.DMA((NZ,)),
        ],
        input_output_aliases={0: 0, 1: 1, 5: 2},
        compiler_params=params,
        name="lower",
    )(S, V, LAM, MU, BUOY, BF, BM, source, got, kept)
    return vel_out, stress_out, shear


def solution(mesh):
    n_gx, n_gy = mesh.shape["gx"], mesh.shape["gy"]
    return jax.shard_map(
        functools.partial(body, n_gx, n_gy),
        mesh=mesh,
        in_specs=(
            P(None, None, "gx", "gy"),
            P(None, None, "gx", "gy"),
            P(None, "gx", "gy"),
            P(),
            P("gx", None, None, None, "gy"),
            P(),
            P("gx", "gy", None),
            P("gx", "gy", None),
        ),
        out_specs=(P(None, None, "gx", "gy"), P(None, None, "gx", "gy"), P()),
        check_vma=False,
    )
```

```python
import functools

import jax
import jax.numpy as jnp
from jax import lax
from jax.experimental import pallas as pl
from jax.experimental.pallas import tpu as pltpu
from jax.sharding import PartitionSpec as P

CX = 32
CY = 128
NZ = 8
STEPS = 2
COARSE = 4
BLOCK = 8
ZONES = 16
BUILDINGS = 1024
FP_DEV = 64
HALO = 4
RING = CX + 2 * HALO
FIELDS = 10
WIDE = 3
WIDE_AT = (FIELDS - WIDE) * 3 * 8
ROWS = WIDE_AT + WIDE * 4 * 8
PACKS = 3
CHUNK = 16
COLS = PACKS * CX
CXC = CX // COARSE
CYC = CY // COARSE
F32 = jnp.float32
VMEM_LIMIT = 32 * 1024 * 1024


def iota(shape, dim):
    return lax.broadcasted_iota(jnp.int32, shape, dim)


def take(x, idx):
    idx = jnp.broadcast_to(idx, x.shape)
    return jnp.take_along_axis(x, idx, axis=1, mode="promise_in_bounds")


def roll(x, shift, axis):
    size = x.shape[axis]
    shift = shift % size
    return x if shift == 0 else pltpu.roll(x, shift, axis)


def rows_kernel(
    n_gy, vel, stress, zones, regional_in, table_in, building_in, block_in, owner_in,
    gxa, gxb, regional, table, building, block, source, F, Z, owner, sems,
):
    even_x = (lax.axis_index("gx") & 1) == 0
    low = iota((8, CY), 0) < 4
    loads = []
    for end, at in enumerate((0, CX - HALO)):
        rows, to = pl.ds(at, HALO), pl.ds(HALO * end, HALO)
        loads.append(pltpu.make_async_copy(stress.at[:, :, rows, :], F.at[end, pl.ds(0, 6), :, to], sems.at[3 * end]))
        loads.append(pltpu.make_async_copy(vel.at[:, :, rows, :], F.at[end, pl.ds(6, 3), :, to], sems.at[3 * end + 1]))
        loads.append(pltpu.make_async_copy(zones.at[:, rows, :], Z.at[end, :, to], sems.at[3 * end + 2]))
    small = ((owner_in, owner), (regional_in, regional), (table_in, table), (building_in, building), (block_in, block))
    loads += [pltpu.make_async_copy(src, dst, sems.at[6 + k]) for k, (src, dst) in enumerate(small)]
    for copy in loads:
        copy.start()
    for copy in loads:
        copy.wait()

    def tile(f, z, end):
        return F[end, f, z] if f < 9 else Z[end, z].astype(F32)

    gy = lax.axis_index("gy")
    row = iota((CHUNK, CY), 0)
    edge = (iota((CHUNK, CY), 1) >= 96) & ((row & 7) >= 6)
    sides = jnp.where(row < CXC, owner[(gy + n_gy - 1) % n_gy], owner[(gy + 1) % n_gy])
    source[...] = jnp.where(edge, sides, owner[gy])

    for f in range(WIDE):
        for q in range(NZ // 2):
            first = jnp.where(low, tile(f, 2 * q, 0), roll(tile(f, 2 * q + 1, 0), 4, 0))
            last = jnp.where(low, roll(tile(f, 2 * q + 1, 1), 4, 0), tile(f, 2 * q, 1))
            at = WIDE_AT + 8 * (f * 4 + q)
            gxa[at:at + 8, :] = jnp.where(even_x, last, first)
            gxb[at:at + 8, :] = jnp.where(even_x, first, last)
    for f in range(WIDE, FIELDS):
        for z in range(NZ):
            first, last = tile(f, z, 0), roll(tile(f, z, 1), 3, 0)
            at = pl.ds((f - WIDE) * 24 + z, 3, stride=8)
            gxa[at, :] = jnp.where(even_x, last, first)[0:3]
            gxb[at, :] = jnp.where(even_x, first, last)[0:3]


def own_band(own, p, at, lasts, firsts):
    inner = (iota(lasts.shape, 1) // 4) % 4 == 1
    for s in range(4):
        if 4 * p + s < FIELDS:
            own[4 * p + s, at, :] = jnp.where(inner, roll(firsts, -4 * s, 1), roll(lasts, 8 - 4 * s, 1))


def cols_kernel(vel, stress, zones, S, V, gya, gyb, own, sems):
    even_y = (lax.axis_index("gy") & 1) == 0
    inner = pl.ds(0, CX)
    loads = [
        pltpu.make_async_copy(stress, S.at[:, :, inner, :], sems.at[0]),
        pltpu.make_async_copy(vel, V.at[:, :, inner, :], sems.at[1]),
    ]
    for copy in loads:
        copy.start()
    slot = iota((CX, CY), 1) // HALO

    def plane(f, z):
        if f < 6:
            return stress[f, z]
        if f < 9:
            return vel[f - 6, z]
        return zones[z].astype(F32)

    for p in range(PACKS):
        lasts = jnp.zeros((CX, CY), F32)
        firsts = jnp.zeros((CX, CY), F32)
        for s in range(4):
            f = 4 * p + s
            if f >= FIELDS:
                continue
            for z in range(NZ):
                turned = roll(plane(f, z), 16 * z + 4 * s + 4, 1)
                at = 4 * z + s
                lasts = jnp.where(slot == at, turned, lasts)
                firsts = jnp.where(slot == (at + 1) % 32, turned, firsts)
        own_band(own, p, slice(0, CX), lasts, firsts)
        gya[p * CX:(p + 1) * CX, :] = jnp.where(even_y, lasts, firsts)
        gyb[p * CX:(p + 1) * CX, :] = jnp.where(even_y, firsts, lasts)

    for copy in loads:
        copy.wait()


def split(count):
    return [(4 * (k // 2) + k % 2, 2) for k in range(count // 2)]


def slices_kernel(n_gx, R, sent, kept, slices):
    part = iota((n_gx, CY), 1) // CYC
    for s in range(STEPS):
        halves = [[R[0, s, c, :, t * CY:(t + 1) * CY] for t in range(2)] for c in range(3)]
        for r in range(CXC):
            turned = jnp.zeros((n_gx, CY), F32)
            for c in range(3):
                turned = jnp.where(part == c, roll(halves[c][r // 4], CYC * (c - r % 4), 1), turned)
            if r < 3:
                turned = jnp.where(part == 3, roll(roll(halves[r][0], n_gx - 1, 0), 96, 1), turned)
            elif r < 6:
                turned = jnp.where(part == 3, roll(halves[r - 3][1], 1, 0), turned)
            slices[pl.ds(s * CXC + r, n_gx, stride=CHUNK), :] = turned
    bit = (lax.axis_index("gx") >> 1) & 1
    for k, (at, step) in enumerate(split(n_gx)):
        for out, side in ((sent, 1 - bit), (kept, bit)):
            out[k] = slices[pl.ds(pl.multiple_of((at + step * side) * CHUNK, CHUNK), CHUNK), :]


def trade_kernel(width, got, kept, source, sent, kept_out, held):
    gx = lax.axis_index("gx")
    mine = ((source[...] ^ gx) & width) == 0
    count = got.shape[0]
    for i in range(count):
        held[i] = jnp.where(mine, kept[i], got[i])
    bit = (gx & (2 * width)) // (2 * width)
    for k, (at, step) in enumerate(split(count)):
        sent[k] = held[at + step * (1 - bit)]
        kept_out[k] = held[at + step * bit]


def ends_kernel(width, got, kept, source, gya, gyb, made, pair, ta, tb):
    ta[0:COLS] = gya[...]
    tb[0:COLS] = gyb[...]
    even_y = (lax.axis_index("gy") & 1) == 0
    mine = ((source[...] ^ lax.axis_index("gx")) & width) == 0
    lane = iota((8, CY), 1)
    sub = iota((8, CY), 0)
    digit, group = (lane - 96) % 10, (lane - 96) // 10
    row = jnp.where(digit < 8, digit, jnp.where(digit == 8, group, 3 + group))
    here = (lane >= 96) & (group < 3) & (sub == row)
    tiles = [jnp.zeros((8, CY), F32), jnp.zeros((8, CY), F32)]
    for i in range(4):
        pair[i] = jnp.where(mine, kept[i], got[i])
        for s in range(STEPS):
            tile = pair[i, s * CXC:(s + 1) * CXC, :]
            for k, col in enumerate((CYC - 1, 0)):
                idx = jnp.where(here, jnp.where(digit < 8, group * CYC, 96) + col, 0)
                ends = jnp.sum(jnp.where(here, take(tile, idx), 0.0), axis=0, keepdims=True)
                tiles[k] = jnp.where(sub == 2 * i + s, jnp.broadcast_to(ends, (8, CY)), tiles[k])
    ta[COLS:COLS + 8] = jnp.where(even_y, tiles[0], tiles[1])
    tb[COLS:COLS + 8] = jnp.where(even_y, tiles[1], tiles[0])


def band_rows(BF, BM, own, table, left, right, p, at):
    quarter = (iota(left.shape, 1) // 4) % 4
    for s in range(4):
        f = 4 * p + s
        if f < FIELDS:
            BF[f, at, :] = jnp.where(
                quarter == 0, roll(left, -4 * s, 1),
                jnp.where(quarter == 3, roll(right, 8 - 4 * s, 1), own[f, at, :]),
            )
        if f == FIELDS - 1:
            ids = BF[f, at, :].astype(jnp.int32)
            for k, column in enumerate(spread_table(table)):
                BM[k, at, :] = take(jnp.broadcast_to(column, left.shape), ids)


def edges_kernel(width, quad, cb, ca, token, own, table, sent, kept, BF, BM):
    even_y = (lax.axis_index("gy") & 1) == 0
    for p in range(PACKS):
        at = slice(p * CX, (p + 1) * CX)
        left, right = jnp.where(even_y, cb[at], ca[at]), jnp.where(even_y, ca[at], cb[at])
        band_rows(BF, BM, own, table, left, right, p, slice(0, CX))
    bit = (lax.axis_index("gx") & width) // width
    beside = iota((1, CY), 1) >= 96
    for k, (first, step) in enumerate(split(4)):
        for out, side in ((sent, 1 - bit), (kept, bit)):
            at = first + step * side
            out[k] = quad[at]
            for s in range(STEPS):
                a, b = ca[pl.ds(COLS + 2 * at + s, 1), :], cb[pl.ds(COLS + 2 * at + s, 1), :]
                for j, ends in enumerate((jnp.where(even_y, b, a), jnp.where(even_y, a, b))):
                    put = j * CXC + 6 + s
                    out[k, put:put + 1, :] = jnp.where(beside, ends, out[k, put:put + 1, :])


def spread_table(table):
    scaled = table[...] * 0.1
    spread = jnp.concatenate([scaled] * (CY // ZONES), axis=1)
    return [spread[k:k + 1, :] for k in range(3)]


def material_kernel(zones, table, LAM, MU, BUOY, token):
    token[...] = jnp.zeros(token.shape, F32)
    columns = [jnp.broadcast_to(row, (CX, CY)) for row in spread_table(table)]
    for z in range(NZ):
        ids = zones[z]
        for k, ref in enumerate((LAM, MU, BUOY)):
            ref[z, 0:CX, :] = take(columns[k], ids)


XX, XZ, XY, YY, YZ, ZZ = range(6)


def dx(x):
    return roll(x, RING - 1, 0) - roll(x, 1, 0)


def dy(x, seam, z):
    lane = iota((RING, CY), 1)
    if seam is None:
        return jnp.where(lane == CY - 1, 0.0, roll(x, CY - 1, 1)) - jnp.where(lane == 0, 0.0, roll(x, 1, 1))
    seam = roll(seam, -(16 * z + 3), 1)
    return jnp.where(lane == CY - 1, seam, roll(x, CY - 1, 1)) - jnp.where(lane == 0, seam, roll(x, 1, 1))


def dz(ref, f, z):
    if z == 0:
        return ref[f, 1]
    if z == NZ - 1:
        return -ref[f, NZ - 2]
    return ref[f, z + 1] - ref[f, z - 1]


def band_dy(x):
    return roll(x, CY - 1, 1) - roll(x, 1, 1)


def band_dz(x):
    lane = iota((RING, CY), 1)
    return jnp.where(lane < CY - 16, roll(x, CY - 16, 1), 0.0) - jnp.where(lane >= 16, roll(x, 16, 1), 0.0)


def seams(band, fields):
    lane = iota((RING, CY), 1)
    return {f: jnp.where(lane % 16 == 2, roll(band[f], -10, 1), band[f]) for f in fields}


ALL = (XX, XZ, XY, YY, YZ, ZZ)
FLAT, STEEP = (XX, XY), (XZ, YZ)


def moving(planes, first):
    return [(z, (0, 1) if (z % 2 == 0) == first else (2,)) for z in planes]


def every(planes):
    return [(z, (0, 1, 2)) for z in planes]


def velocity_planes(parts, S, V, MU, BUOY, band, drm):
    seam = {XY: None, YY: None, YZ: None} if band is None else seams(band, (XY, YY, YZ))
    for z, comps in parts:
        for c in comps:
            x, y, vert = ((XX, XY, XZ), (XY, YY, YZ), (XZ, YZ, ZZ))[c]
            force = dx(S[x, z]) + dy(S[y, z], seam[y], z) + dz(S, vert, z)
            if z == NZ - 1:
                force = force + (20.0 * MU[z]) * drm(c, 0)
            V[c, z] = V[c, z] + BUOY[z] * force


def velocity_seams(parts, V, BUOY, band):
    lane = iota((RING, CY), 1)
    sign = jnp.where(lane == 0, -1.0, jnp.where(lane == CY - 1, 1.0, 0.0))
    seam = seams(band, (XY, YY, YZ))
    for z, comps in parts:
        scale = BUOY[z] * sign
        for c in comps:
            V[c, z] = V[c, z] + scale * roll(seam[(XY, YY, YZ)[c]], -(16 * z + 3), 1)


def velocity_band(band, new, BM, drm, comps=(0, 1, 2)):
    for c in comps:
        x, y, vert = ((XX, XY, XZ), (XY, YY, YZ), (XZ, YZ, ZZ))[c]
        force = dx(band[x]) + band_dy(band[y]) + band_dz(band[vert])
        if drm is not None:
            force = force + (20.0 * BM[1]) * drm(c, 1)
        new[6 + c] = band[6 + c] + BM[2] * force


def stress_plane(z, seam, S, V, LAM, MU, fields):
    vx, vy, vz = V[0, z], V[1, z], V[2, z]
    mu = MU[z]
    if XX in fields:
        lam = LAM[z]
        xx, yy, zz = dx(vx), dy(vy, seam[7], z), dz(V, 2, z)
        theta = lam * (xx + yy + zz)
        two = mu + mu
        S[XX, z] = S[XX, z] + (theta + two * xx)
        S[YY, z] = S[YY, z] + (theta + two * yy)
        S[ZZ, z] = S[ZZ, z] + (theta + two * zz)
    if XZ in fields:
        S[XZ, z] = S[XZ, z] + mu * (dz(V, 0, z) + dx(vz))
    if XY in fields:
        S[XY, z] = S[XY, z] + mu * (dy(vx, seam[6], z) + dx(vy))
    if YZ in fields:
        S[YZ, z] = S[YZ, z] + mu * (dz(V, 1, z) + dy(vz, seam[8], z))


def stress_band(band, new, BM):
    vx, vy, vz = new[6], new[7], new[8]
    lam, mu = BM[0], BM[1]
    xx, yy, zz = dx(vx), band_dy(vy), band_dz(vz)
    theta = lam * (xx + yy + zz)
    two = mu + mu
    new[XX] = band[XX] + (theta + two * xx)
    new[YY] = band[YY] + (theta + two * yy)
    new[ZZ] = band[ZZ] + (theta + two * zz)
    new[XZ] = band[XZ] + mu * (band_dz(vx) + dx(vz))
    new[XY] = band[XY] + mu * (band_dy(vx) + dx(vy))
    new[YZ] = band[YZ] + mu * (band_dz(vy) + band_dy(vz))


def unpack_kernel(
    S_in, V_in, LAM_in, MU_in, BUOY_in, own_in, table, rb, ra,
    S, V, LAM, MU, BUOY, own, ta, tb, zone_tail,
):
    even_x = (lax.axis_index("gx") & 1) == 0
    even_y = (lax.axis_index("gy") & 1) == 0
    low = iota((8, CY), 0) < 4
    slot = iota((8, CY), 1) // HALO
    tail = slice(CX, RING)
    columns = [jnp.broadcast_to(row, (8, CY)) for row in spread_table(table)]

    def place(f, z, rows):
        if f < 6:
            S[f, z, tail, :] = rows
        elif f < 9:
            V[f - 6, z, tail, :] = rows
        else:
            zone_tail[z] = rows

    for f in range(WIDE):
        for q in range(NZ // 2):
            at = slice(WIDE_AT + 8 * (f * 4 + q), WIDE_AT + 8 * (f * 4 + q) + 8)
            after = jnp.where(even_x, ra[at], rb[at])
            before = jnp.where(even_x, rb[at], ra[at])
            place(f, 2 * q, jnp.where(low, after, before))
            place(f, 2 * q + 1, roll(jnp.where(low, before, after), 4, 0))
    sub = iota((8, CY), 0)
    for f in range(WIDE, FIELDS):
        for z in range(NZ):
            at = pl.ds((f - WIDE) * 24 + z, 8, stride=8)
            a, b = ra[at, :], rb[at, :]
            after, before = jnp.where(even_x, a, b), roll(jnp.where(even_x, b, a), 5, 0)
            place(f, z, jnp.where(sub < 3, after, jnp.where(sub >= 5, before, 0.0)))
    for z in range(NZ):
        ids = zone_tail[z].astype(jnp.int32)
        for column, ref in zip(columns, (LAM, MU, BUOY)):
            ref[z, tail, :] = take(column, ids)
    for p in range(PACKS):
        lasts = jnp.zeros((8, CY), F32)
        firsts = jnp.zeros((8, CY), F32)
        for s in range(4):
            f = 4 * p + s
            if f >= FIELDS:
                continue
            for z in range(NZ):
                rows = S[f, z, tail, :] if f < 6 else V[f - 6, z, tail, :] if f < 9 else zone_tail[z]
                turned = roll(rows, 16 * z + 4 * s + 4, 1)
                at = 4 * z + s
                lasts = jnp.where(slot == at, turned, lasts)
                firsts = jnp.where(slot == (at + 1) % 32, turned, firsts)
        own_band(own, p, tail, lasts, firsts)
        ta[p] = jnp.where(even_y, lasts, firsts)
        tb[p] = jnp.where(even_y, firsts, lasts)


def inner_kernel(S, V_in, MU, BUOY, V, token):
    velocity_planes(moving(range(0, 5), True), S, V, MU, BUOY, None, None)
    token[...] = jnp.zeros(token.shape, F32)


def cone_kernel(
    S_in, V_in, LAM, MU, BUOY, BF_in, BM_in, table, own, tcb, tca, building, block,
    S, V, BF, BM, BV, BW, shares,
):
    even_y = (lax.axis_index("gy") & 1) == 0
    lane8 = iota((8, CY), 1)
    sub8 = iota((8, CY), 0)
    for p in range(PACKS):
        left, right = jnp.where(even_y, tcb[p], tca[p]), jnp.where(even_y, tca[p], tcb[p])
        band_rows(BF, BM, own, table, left, right, p, slice(CX, RING))

    velocity_seams(moving(range(0, 5), True), V, BUOY, BF)
    velocity_band(BF, BW, BM, None)
    for c in range(3):
        BV[c] = BW[6 + c]
    seam = seams(BW, (6, 7, 8))
    for z in range(0, 4):
        stress_plane(z, seam, S, V, LAM, MU, (FLAT, STEEP)[z % 2])
    stress_band(BF, BW, BM)
    velocity_planes(moving(range(0, 3), True), S, V, MU, BUOY, BW, None)
    velocity_band(BW, BW, BM, None, (2,))
    stress_plane(1, seams(BW, (8,)), S, V, LAM, MU, (XZ, YZ))

    total = jnp.zeros((8, CY), F32)
    for c, f in enumerate((XZ, YZ)):
        for r in range(CX // BLOCK):
            row = jnp.sum(S[f, 1, 8 * r:8 * r + 8, :], axis=0, keepdims=True)
            total = jnp.where(sub8 == 4 * c + r, jnp.broadcast_to(row, (8, CY)), total)
    for shift in (1, 2, 4):
        total = total + roll(total, CY - shift, 1)
    total = total * (1.0 / (BLOCK * BLOCK))
    ids = jnp.broadcast_to(jnp.concatenate([block[0], block[0]], axis=1), (8, CY))
    cells = CY // BLOCK
    picked = take(total, (ids % cells) * BLOCK)
    mine = (sub8 % 4 == ids // cells) & (sub8 // 4 == lane8 // FP_DEV)
    values = jnp.sum(jnp.where(mine, picked, 0.0), axis=0, keepdims=True)
    names = jnp.concatenate([building[0], building[0]], axis=1).astype(F32)
    message = jnp.concatenate([values, names], axis=0)
    shares[...] = jnp.broadcast_to(message[None], shares.shape)


def upper_kernel(S_in, V_in, LAM, MU, BUOY, BF, BM, BV, BW_in, S, V, BW):
    velocity_planes(moving(range(0, 5), False) + every(range(5, 7)), S, V, MU, BUOY, BF, None)
    seam = {6 + c: value for c, value in seams(BV, range(3)).items()}
    for z in range(0, 6):
        stress_plane(z, seam, S, V, LAM, MU, ALL if z > 3 else (STEEP, FLAT)[z % 2])
    velocity_planes(moving(range(0, 3), False) + every(range(3, 5)), S, V, MU, BUOY, BW, None)
    velocity_band(BW, BW, BM, None, (0, 1))
    seam = seams(BW, (6, 7, 8))
    for z in range(0, 4):
        stress_plane(z, seam, S, V, LAM, MU, FLAT if z == 1 else ALL)


def lower_kernel(
    S_in, V_in, LAM, MU, BUOY, BF_in, BM, source, got, kept,
    S, V, BF, vel_out, stress_out, DRM, drm_in, sems,
):
    saves = []

    def save(ref, out, first, count):
        at = pl.ds(first, count)
        copy = pltpu.make_async_copy(ref.at[:, at, pl.ds(0, CX), :], out.at[:, at], sems.at[len(saves)])
        copy.start()
        saves.append(copy)

    save(V, vel_out, 0, 5)
    save(S, stress_out, 0, 4)
    low = iota((8, CY), 0) < 4
    lane8 = iota((8, CY), 1)
    quarter8 = (lane8 // 4) % 4
    deepest = lane8 >= 16 * (NZ - 1)

    mine = ((source[...] ^ lax.axis_index("gx")) & 1) == 0
    drm_in[...] = jnp.where(mine, kept[0], got[0])

    def wide(row):
        return jnp.broadcast_to(drm_in[row:row + 1, :], (8, CY))

    for s in range(STEPS):
        both = jnp.where(lane8 >= 96, wide(6 + s), roll(wide(CXC + 6 + s), 32, 1))
        for c in range(3):
            for q in range(RING // 8):
                if q < 4:
                    rows = jnp.where(low, wide(s * CXC + 2 * q), wide(s * CXC + 2 * q + 1))
                    base = c * CYC
                else:
                    rows = jnp.where(low, wide(s * CXC + c), wide(s * CXC + 3 + c))
                    base = 3 * CYC
                DRM[s, c, 0, 8 * q:8 * q + 8, :] = take(rows, base + lane8 // COARSE)
                inner = take(rows, base + jnp.where(quarter8 == 2, CYC - 1, 0))
                at = c * 10 + 2 * q + jnp.where(low, 0, 1) + jnp.where(quarter8 == 0, 96, 0)
                value = jnp.where((quarter8 & 1) == (quarter8 >> 1), take(both, at), inner)
                DRM[s, c, 1, 8 * q:8 * q + 8, :] = jnp.where(deepest, value, 0.0)

    def drm(step):
        return lambda c, k: DRM[step, c, k]

    velocity_planes(every(range(7, NZ)), S, V, MU, BUOY, BF, drm(0))
    velocity_band(BF, BF, BM, drm(0))
    seam = seams(BF, (6, 7, 8))
    for z in range(6, NZ):
        stress_plane(z, seam, S, V, LAM, MU, ALL)
    stress_band(BF, BF, BM)
    velocity_planes(every(range(5, NZ)), S, V, MU, BUOY, BF, drm(1))
    velocity_band(BF, BF, BM, drm(1))
    save(V, vel_out, 5, NZ - 5)
    seam = seams(BF, (6, 7, 8))
    for z in range(4, NZ):
        stress_plane(z, seam, S, V, LAM, MU, ALL)
        save(S, stress_out, z, 1)
    for copy in saves:
        copy.wait()


def sum_kernel(n, shares, out):
    half = n // 2
    n_high = BUILDINGS // CY
    low = iota((half, CY), 1) < FP_DEV
    values = shares[:, 0, :]
    names = shares[:, 1, :].astype(jnp.int32)
    names = jnp.where(low, names[:half], names[half:])
    high, names = names // CY, names % CY
    pieces = []
    for rest in (
        jnp.where(low, values[:half], roll(values[half:], FP_DEV, 1)),
        jnp.where(low, roll(values[:half], FP_DEV, 1), values[half:]),
    ):
        for _ in range(3):
            piece = rest.astype(jnp.bfloat16).astype(F32)
            rest = rest - piece
            pieces.append(piece)
    rows = iota((n_high, CY), 0)
    wanted = iota((CY, CY), 0)
    left, hot = [], []
    for k in range(half):
        here = jnp.broadcast_to(high[k:k + 1], (n_high, CY)) == rows
        parts = [jnp.where(here, jnp.broadcast_to(piece[k:k + 1], (n_high, CY)), 0.0) for piece in pieces]
        left.append(jnp.concatenate(parts, axis=0).astype(jnp.bfloat16))
        hot.append((jnp.broadcast_to(names[k:k + 1], (CY, CY)) == wanted).astype(F32).astype(jnp.bfloat16))
    acc = lax.dot_general(
        jnp.concatenate(left, axis=1), jnp.concatenate(hot, axis=1), (((1,), (1,)), ((), ())), preferred_element_type=F32,
    )
    sums = []
    for c in range(2):
        base = 3 * c * n_high
        sums.append(acc[base:base + n_high] + acc[base + n_high:base + 2 * n_high] + acc[base + 2 * n_high:base + 3 * n_high])
    for h in range(n_high):
        out[:, h * CY:(h + 1) * CY] = jnp.concatenate([sums[0][h:h + 1], sums[1][h:h + 1]], axis=0)


def pairs_near(n):
    return [(i, i ^ 1) for i in range(n)]


def pairs_far(n):
    return [(i, (i + 1) % n if i % 2 else (i - 1) % n) for i in range(n)]


def after(x, *done):
    return lax.optimization_barrier((x,) + done)[0]


def body(n_gx, n_gy, velocity, stress, zones, zone_table, regional, owner, building, block):
    n = n_gx * n_gy
    gx = lax.axis_index("gx")
    vmem = pl.BlockSpec(memory_space=pltpu.VMEM)
    hbm = pl.BlockSpec(memory_space=pltpu.HBM)
    anywhere = pl.BlockSpec(memory_space=pl.ANY)
    params = pltpu.CompilerParams(vmem_limit_bytes=VMEM_LIMIT)

    def shaped(*shape):
        return jax.ShapeDtypeStruct(shape, F32)

    def whole(shape, dtype):
        return jax.ShapeDtypeStruct(shape, dtype)

    s_ring = shaped(6, NZ, RING, CY)
    v_ring = shaped(3, NZ, RING, CY)
    m_ring = shaped(NZ, RING, CY)
    rows = shaped(ROWS, CY)
    cols = shaped(COLS, CY)
    from_hbm = [
        pltpu.with_memory_space_constraint(x, pltpu.HBM)
        for x in (velocity, stress, zones, regional, zone_table, building, block, owner)
    ]
    gxa, gxb, regional, zone_table, building, block, source = pl.pallas_call(
        functools.partial(rows_kernel, n_gy),
        out_shape=(
            rows, rows, whole(regional.shape, F32), whole(zone_table.shape, F32),
            whole(building.shape, jnp.int32), whole(block.shape, jnp.int32), whole((CHUNK, CY), jnp.int32),
        ),
        in_specs=[hbm] * 8,
        out_specs=(vmem,) * 7,
        scratch_shapes=[
            pltpu.VMEM((2, 9, NZ, 8, CY), F32),
            pltpu.VMEM((2, NZ, 8, CY), jnp.int32),
            pltpu.SMEM(owner.shape, jnp.int32),
            pltpu.SemaphoreType.DMA((11,)),
        ],
        compiler_params=params,
        name="pack_rows",
    )(*from_hbm)
    rb = lax.ppermute(gxb, "gx", pairs_far(n_gx))
    ra = lax.ppermute(gxa, "gx", pairs_near(n_gx))
    own = shaped(FIELDS, RING, CY)
    S, V, gya, gyb, own = pl.pallas_call(
        cols_kernel,
        out_shape=(s_ring, v_ring, cols, cols, own),
        in_specs=[vmem] * 3,
        out_specs=(vmem,) * 5,
        scratch_shapes=[pltpu.SemaphoreType.DMA((2,))],
        compiler_params=params,
        name="pack_columns",
    )(velocity, stress, zones)

    def across(x, width):
        return lax.ppermute(x, "gx", [(i, i ^ width) for i in range(n_gx)])

    half = shaped(n_gx // 2, CHUNK, CY)
    sent, kept = pl.pallas_call(
        functools.partial(slices_kernel, n_gx),
        out_shape=(half, half),
        in_specs=[vmem],
        out_specs=(vmem,) * 2,
        scratch_shapes=[pltpu.VMEM((n_gx * CHUNK, CY), F32)],
        compiler_params=params,
        name="slices",
    )(regional)
    width = 2
    while 4 * width < n_gx:
        count = sent.shape[0]
        part = shaped(count // 2, CHUNK, CY)
        sent, kept = pl.pallas_call(
            functools.partial(trade_kernel, width),
            out_shape=(part, part),
            in_specs=[vmem] * 3,
            out_specs=(vmem,) * 2,
            scratch_shapes=[pltpu.VMEM((count, CHUNK, CY), F32)],
            compiler_params=params,
            name="trade",
        )(across(sent, width), kept, source)
        width *= 2
    LAM, MU, BUOY, made = pl.pallas_call(
        material_kernel,
        out_shape=(m_ring,) * 3 + (shaped(8, CY),),
        in_specs=[vmem] * 2,
        out_specs=(vmem,) * 4,
        compiler_params=params,
        name="materials",
    )(zones, zone_table)
    message = shaped(COLS + 8, CY)
    quad, message_a, message_b = pl.pallas_call(
        functools.partial(ends_kernel, width),
        out_shape=(shaped(4, CHUNK, CY), message, message),
        in_specs=[vmem] * 5 + [anywhere],
        out_specs=(vmem,) * 3,
        compiler_params=params,
        name="ends",
    )(across(sent, width), kept, source, gya, gyb, made)
    cb = lax.ppermute(message_b, "gy", pairs_far(n_gy))
    ca = lax.ppermute(message_a, "gy", pairs_near(n_gy))
    ends = shaped(PACKS, 8, CY)
    S, V, LAM, MU, BUOY, own, ta, tb = pl.pallas_call(
        unpack_kernel,
        out_shape=(s_ring, v_ring, m_ring, m_ring, m_ring, shaped(FIELDS, RING, CY), ends, ends),
        in_specs=[vmem] * 9,
        out_specs=(vmem,) * 8,
        scratch_shapes=[pltpu.VMEM((NZ, 8, CY), F32)],
        input_output_aliases={k: k for k in range(6)},
        compiler_params=params,
        name="unpack",
    )(S, V, LAM, MU, BUOY, own, zone_table, rb, ra)
    tcb = lax.ppermute(tb, "gy", pairs_far(n_gy))
    tca = lax.ppermute(ta, "gy", pairs_near(n_gy))
    V, token = pl.pallas_call(
        inner_kernel,
        out_shape=(v_ring, shaped(8, CY)),
        in_specs=[vmem] * 4,
        out_specs=(vmem,) * 2,
        input_output_aliases={1: 0},
        compiler_params=params,
        name="inner",
    )(S, V, MU, BUOY)
    two = shaped(2, CHUNK, CY)
    band = shaped(3, RING, CY)
    width *= 2
    sent, kept, BF, BM = pl.pallas_call(
        functools.partial(edges_kernel, width),
        out_shape=(two, two, shaped(FIELDS, RING, CY), band),
        in_specs=[vmem] * 3 + [anywhere] + [vmem] * 2,
        out_specs=(vmem,) * 4,
        compiler_params=params,
        name="edges",
    )(quad, cb, ca, token, own, zone_table)
    S, V, BF, BM, BV, BW, shares = pl.pallas_call(
        cone_kernel,
        out_shape=(s_ring, v_ring, shaped(FIELDS, RING, CY), band, band, shaped(9, RING, CY), shaped(n, 2, CY)),
        in_specs=[vmem] * 13,
        out_specs=(vmem,) * 7,
        input_output_aliases={0: 0, 1: 1, 5: 2, 6: 3},
        compiler_params=params,
        name="cone",
    )(S, V, LAM, MU, BUOY, BF, BM, zone_table, own, tcb, tca, building, block)
    held = jnp.where(((source ^ gx) & width) == 0, kept, across(sent, width))
    odd = (gx & 1) != 0
    sent, kept = jnp.where(odd, held[0], held[1])[None], jnp.where(odd, held[1], held[0])[None]
    got = across(sent, 1)
    gathered = lax.all_to_all(shares, ("gx", "gy"), 0, 0)
    S, V, _ = pl.pallas_call(
        upper_kernel,
        out_shape=(s_ring, v_ring, shaped(9, RING, CY)),
        in_specs=[vmem] * 9,
        out_specs=(vmem,) * 3,
        input_output_aliases={0: 0, 1: 1, 8: 2},
        compiler_params=params,
        name="upper",
    )(S, V, LAM, MU, BUOY, BF, BM, BV, BW)
    shear = pl.pallas_call(
        functools.partial(sum_kernel, n),
        out_shape=shaped(2, BUILDINGS),
        in_specs=[vmem],
        out_specs=vmem,
        compiler_params=params,
        name="sum_by_building",
    )(gathered)
    _, _, _, vel_out, stress_out = pl.pallas_call(
        lower_kernel,
        out_shape=(s_ring, v_ring, shaped(FIELDS, RING, CY), shaped(*velocity.shape), shaped(*stress.shape)),
        in_specs=[vmem] * 10,
        out_specs=(vmem, vmem, vmem, hbm, hbm),
        scratch_shapes=[
            pltpu.VMEM((STEPS, 3, 2, RING, CY), F32),
            pltpu.VMEM((CHUNK, CY), F32),
            pltpu.SemaphoreType.DMA((NZ,)),
        ],
        input_output_aliases={0: 0, 1: 1, 5: 2},
        compiler_params=params,
        name="lower",
    )(S, V, LAM, MU, BUOY, BF, BM, source, got, kept)
    return vel_out, stress_out, shear


def solution(mesh):
    n_gx, n_gy = mesh.shape["gx"], mesh.shape["gy"]
    return jax.shard_map(
        functools.partial(body, n_gx, n_gy),
        mesh=mesh,
        in_specs=(
            P(None, None, "gx", "gy"),
            P(None, None, "gx", "gy"),
            P(None, "gx", "gy"),
            P(),
            P("gx", None, None, None, "gy"),
            P(),
            P("gx", "gy", None),
            P("gx", "gy", None),
        ),
        out_specs=(P(None, None, "gx", "gy"), P(None, None, "gx", "gy"), P()),
        check_vma=False,
    )
```

```python
import functools

import jax
import jax.numpy as jnp
from jax import lax
from jax.experimental import pallas as pl
from jax.experimental.pallas import tpu as pltpu
from jax.sharding import PartitionSpec as P

CX = 32
CY = 128
NZ = 8
STEPS = 2
COARSE = 4
BLOCK = 8
ZONES = 16
BUILDINGS = 1024
FP_DEV = 64
HALO = 4
RING = CX + 2 * HALO
FIELDS = 10
WIDE = 3
WIDE_AT = (FIELDS - WIDE) * 3 * 8
ROWS = WIDE_AT + WIDE * 4 * 8
PACKS = 3
CHUNK = 16
COLS = PACKS * CX
CXC = CX // COARSE
CYC = CY // COARSE
F32 = jnp.float32
VMEM_LIMIT = 32 * 1024 * 1024


def iota(shape, dim):
    return lax.broadcasted_iota(jnp.int32, shape, dim)


def take(x, idx):
    idx = jnp.broadcast_to(idx, x.shape)
    return jnp.take_along_axis(x, idx, axis=1, mode="promise_in_bounds")


def roll(x, shift, axis):
    size = x.shape[axis]
    shift = shift % size
    return x if shift == 0 else pltpu.roll(x, shift, axis)


def rows_kernel(
    n_gy, vel, stress, zones, regional_in, table_in, building_in, block_in, owner_in,
    gxa, gxb, regional, table, building, block, source, F, Z, owner, sems,
):
    even_x = (lax.axis_index("gx") & 1) == 0
    low = iota((8, CY), 0) < 4
    loads = []
    for end, at in enumerate((0, CX - HALO)):
        rows, to = pl.ds(at, HALO), pl.ds(HALO * end, HALO)
        loads.append(pltpu.make_async_copy(stress.at[:, :, rows, :], F.at[end, pl.ds(0, 6), :, to], sems.at[3 * end]))
        loads.append(pltpu.make_async_copy(vel.at[:, :, rows, :], F.at[end, pl.ds(6, 3), :, to], sems.at[3 * end + 1]))
        loads.append(pltpu.make_async_copy(zones.at[:, rows, :], Z.at[end, :, to], sems.at[3 * end + 2]))
    small = ((owner_in, owner), (regional_in, regional), (table_in, table), (building_in, building), (block_in, block))
    loads += [pltpu.make_async_copy(src, dst, sems.at[6 + k]) for k, (src, dst) in enumerate(small)]
    for copy in loads:
        copy.start()
    for copy in loads:
        copy.wait()

    def tile(f, z, end):
        return F[end, f, z] if f < 9 else Z[end, z].astype(F32)

    gy = lax.axis_index("gy")
    row = iota((CHUNK, CY), 0)
    edge = (iota((CHUNK, CY), 1) >= 96) & ((row & 7) >= 6)
    sides = jnp.where(row < CXC, owner[(gy + n_gy - 1) % n_gy], owner[(gy + 1) % n_gy])
    source[...] = jnp.where(edge, sides, owner[gy])

    for f in range(WIDE):
        for q in range(NZ // 2):
            first = jnp.where(low, tile(f, 2 * q, 0), roll(tile(f, 2 * q + 1, 0), 4, 0))
            last = jnp.where(low, roll(tile(f, 2 * q + 1, 1), 4, 0), tile(f, 2 * q, 1))
            at = WIDE_AT + 8 * (f * 4 + q)
            gxa[at:at + 8, :] = jnp.where(even_x, last, first)
            gxb[at:at + 8, :] = jnp.where(even_x, first, last)
    for f in range(WIDE, FIELDS):
        for z in range(NZ):
            first, last = tile(f, z, 0), roll(tile(f, z, 1), 3, 0)
            at = pl.ds((f - WIDE) * 24 + z, 3, stride=8)
            gxa[at, :] = jnp.where(even_x, last, first)[0:3]
            gxb[at, :] = jnp.where(even_x, first, last)[0:3]


def own_band(own, p, at, lasts, firsts):
    inner = (iota(lasts.shape, 1) // 4) % 4 == 1
    for s in range(4):
        if 4 * p + s < FIELDS:
            own[4 * p + s, at, :] = jnp.where(inner, roll(firsts, -4 * s, 1), roll(lasts, 8 - 4 * s, 1))


def cols_kernel(vel, stress, zones, S, V, gya, gyb, own, sems):
    even_y = (lax.axis_index("gy") & 1) == 0
    inner = pl.ds(0, CX)
    loads = [
        pltpu.make_async_copy(stress, S.at[:, :, inner, :], sems.at[0]),
        pltpu.make_async_copy(vel, V.at[:, :, inner, :], sems.at[1]),
    ]
    for copy in loads:
        copy.start()
    slot = iota((CX, CY), 1) // HALO

    def plane(f, z):
        if f < 6:
            return stress[f, z]
        if f < 9:
            return vel[f - 6, z]
        return zones[z].astype(F32)

    for p in range(PACKS):
        lasts = jnp.zeros((CX, CY), F32)
        firsts = jnp.zeros((CX, CY), F32)
        for s in range(4):
            f = 4 * p + s
            if f >= FIELDS:
                continue
            for z in range(NZ):
                turned = roll(plane(f, z), 16 * z + 4 * s + 4, 1)
                at = 4 * z + s
                lasts = jnp.where(slot == at, turned, lasts)
                firsts = jnp.where(slot == (at + 1) % 32, turned, firsts)
        own_band(own, p, slice(0, CX), lasts, firsts)
        gya[p * CX:(p + 1) * CX, :] = jnp.where(even_y, lasts, firsts)
        gyb[p * CX:(p + 1) * CX, :] = jnp.where(even_y, firsts, lasts)

    for copy in loads:
        copy.wait()


def split(count):
    return [(4 * (k // 2) + k % 2, 2) for k in range(count // 2)]


def slices_kernel(n_gx, R, sent, kept, slices):
    part = iota((n_gx, CY), 1) // CYC
    for s in range(STEPS):
        halves = [[R[0, s, c, :, t * CY:(t + 1) * CY] for t in range(2)] for c in range(3)]
        for r in range(CXC):
            turned = jnp.zeros((n_gx, CY), F32)
            for c in range(3):
                turned = jnp.where(part == c, roll(halves[c][r // 4], CYC * (c - r % 4), 1), turned)
            if r < 3:
                turned = jnp.where(part == 3, roll(roll(halves[r][0], n_gx - 1, 0), 96, 1), turned)
            elif r < 6:
                turned = jnp.where(part == 3, roll(halves[r - 3][1], 1, 0), turned)
            slices[pl.ds(s * CXC + r, n_gx, stride=CHUNK), :] = turned
    bit = (lax.axis_index("gx") >> 1) & 1
    for k, (at, step) in enumerate(split(n_gx)):
        for out, side in ((sent, 1 - bit), (kept, bit)):
            out[k] = slices[pl.ds(pl.multiple_of((at + step * side) * CHUNK, CHUNK), CHUNK), :]


def trade_kernel(width, got, kept, source, sent, kept_out, held):
    gx = lax.axis_index("gx")
    mine = ((source[...] ^ gx) & width) == 0
    count = got.shape[0]
    for i in range(count):
        held[i] = jnp.where(mine, kept[i], got[i])
    bit = (gx & (2 * width)) // (2 * width)
    for k, (at, step) in enumerate(split(count)):
        sent[k] = held[at + step * (1 - bit)]
        kept_out[k] = held[at + step * bit]


def ends_kernel(width, got, kept, source, gya, gyb, made, pair, ta, tb):
    ta[0:COLS] = gya[...]
    tb[0:COLS] = gyb[...]
    even_y = (lax.axis_index("gy") & 1) == 0
    mine = ((source[...] ^ lax.axis_index("gx")) & width) == 0
    lane = iota((8, CY), 1)
    sub = iota((8, CY), 0)
    digit, group = (lane - 96) % 10, (lane - 96) // 10
    row = jnp.where(digit < 8, digit, jnp.where(digit == 8, group, 3 + group))
    here = (lane >= 96) & (group < 3) & (sub == row)
    tiles = [jnp.zeros((8, CY), F32), jnp.zeros((8, CY), F32)]
    for i in range(4):
        pair[i] = jnp.where(mine, kept[i], got[i])
        for s in range(STEPS):
            tile = pair[i, s * CXC:(s + 1) * CXC, :]
            for k, col in enumerate((CYC - 1, 0)):
                idx = jnp.where(here, jnp.where(digit < 8, group * CYC, 96) + col, 0)
                ends = jnp.sum(jnp.where(here, take(tile, idx), 0.0), axis=0, keepdims=True)
                tiles[k] = jnp.where(sub == 2 * i + s, jnp.broadcast_to(ends, (8, CY)), tiles[k])
    ta[COLS:COLS + 8] = jnp.where(even_y, tiles[0], tiles[1])
    tb[COLS:COLS + 8] = jnp.where(even_y, tiles[1], tiles[0])


def band_rows(BF, BM, own, table, left, right, p, at):
    quarter = (iota(left.shape, 1) // 4) % 4
    for s in range(4):
        f = 4 * p + s
        if f < FIELDS:
            BF[f, at, :] = jnp.where(
                quarter == 0, roll(left, -4 * s, 1),
                jnp.where(quarter == 3, roll(right, 8 - 4 * s, 1), own[f, at, :]),
            )
        if f == FIELDS - 1:
            ids = BF[f, at, :].astype(jnp.int32)
            for k, column in enumerate(spread_table(table)):
                BM[k, at, :] = take(jnp.broadcast_to(column, left.shape), ids)


def edges_kernel(width, quad, cb, ca, token, own, table, sent, kept, BF, BM):
    even_y = (lax.axis_index("gy") & 1) == 0
    for p in range(PACKS):
        at = slice(p * CX, (p + 1) * CX)
        left, right = jnp.where(even_y, cb[at], ca[at]), jnp.where(even_y, ca[at], cb[at])
        band_rows(BF, BM, own, table, left, right, p, slice(0, CX))
    bit = (lax.axis_index("gx") & width) // width
    beside = iota((1, CY), 1) >= 96
    for k, (first, step) in enumerate(split(4)):
        for out, side in ((sent, 1 - bit), (kept, bit)):
            at = first + step * side
            out[k] = quad[at]
            for s in range(STEPS):
                a, b = ca[pl.ds(COLS + 2 * at + s, 1), :], cb[pl.ds(COLS + 2 * at + s, 1), :]
                for j, ends in enumerate((jnp.where(even_y, b, a), jnp.where(even_y, a, b))):
                    put = j * CXC + 6 + s
                    out[k, put:put + 1, :] = jnp.where(beside, ends, out[k, put:put + 1, :])


def spread_table(table):
    scaled = table[...] * 0.1
    spread = jnp.concatenate([scaled] * (CY // ZONES), axis=1)
    return [spread[k:k + 1, :] for k in range(3)]


def material_kernel(zones, table, LAM, MU, BUOY, token):
    token[...] = jnp.zeros(token.shape, F32)
    columns = [jnp.broadcast_to(row, (CX, CY)) for row in spread_table(table)]
    for z in range(NZ):
        ids = zones[z]
        for k, ref in enumerate((LAM, MU, BUOY)):
            ref[z, 0:CX, :] = take(columns[k], ids)


XX, XZ, XY, YY, YZ, ZZ = range(6)


def dx(x):
    return roll(x, RING - 1, 0) - roll(x, 1, 0)


def dy(x, seam, z):
    lane = iota((RING, CY), 1)
    if seam is None:
        return jnp.where(lane == CY - 1, 0.0, roll(x, CY - 1, 1)) - jnp.where(lane == 0, 0.0, roll(x, 1, 1))
    seam = roll(seam, -(16 * z + 3), 1)
    return jnp.where(lane == CY - 1, seam, roll(x, CY - 1, 1)) - jnp.where(lane == 0, seam, roll(x, 1, 1))


def dz(ref, f, z):
    if z == 0:
        return ref[f, 1]
    if z == NZ - 1:
        return -ref[f, NZ - 2]
    return ref[f, z + 1] - ref[f, z - 1]


def band_dy(x):
    return roll(x, CY - 1, 1) - roll(x, 1, 1)


def band_dz(x):
    lane = iota((RING, CY), 1)
    return jnp.where(lane < CY - 16, roll(x, CY - 16, 1), 0.0) - jnp.where(lane >= 16, roll(x, 16, 1), 0.0)


def seams(band, fields):
    lane = iota((RING, CY), 1)
    return {f: jnp.where(lane % 16 == 2, roll(band[f], -10, 1), band[f]) for f in fields}


ALL = (XX, XZ, XY, YY, YZ, ZZ)
FLAT, STEEP = (XX, XY), (XZ, YZ)


def moving(planes, first):
    return [(z, (0, 1) if (z % 2 == 0) == first else (2,)) for z in planes]


def every(planes):
    return [(z, (0, 1, 2)) for z in planes]


def velocity_planes(parts, S, V, MU, BUOY, band, drm):
    seam = {XY: None, YY: None, YZ: None} if band is None else seams(band, (XY, YY, YZ))
    for z, comps in parts:
        for c in comps:
            x, y, vert = ((XX, XY, XZ), (XY, YY, YZ), (XZ, YZ, ZZ))[c]
            force = dx(S[x, z]) + dy(S[y, z], seam[y], z) + dz(S, vert, z)
            if z == NZ - 1:
                force = force + (20.0 * MU[z]) * drm(c, 0)
            V[c, z] = V[c, z] + BUOY[z] * force


def velocity_seams(parts, V, BUOY, band):
    lane = iota((RING, CY), 1)
    sign = jnp.where(lane == 0, -1.0, jnp.where(lane == CY - 1, 1.0, 0.0))
    seam = seams(band, (XY, YY, YZ))
    for z, comps in parts:
        scale = BUOY[z] * sign
        for c in comps:
            V[c, z] = V[c, z] + scale * roll(seam[(XY, YY, YZ)[c]], -(16 * z + 3), 1)


def velocity_band(band, new, BM, drm, comps=(0, 1, 2)):
    for c in comps:
        x, y, vert = ((XX, XY, XZ), (XY, YY, YZ), (XZ, YZ, ZZ))[c]
        force = dx(band[x]) + band_dy(band[y]) + band_dz(band[vert])
        if drm is not None:
            force = force + (20.0 * BM[1]) * drm(c, 1)
        new[6 + c] = band[6 + c] + BM[2] * force


def stress_plane(z, seam, S, V, LAM, MU, fields):
    vx, vy, vz = V[0, z], V[1, z], V[2, z]
    mu = MU[z]
    if XX in fields:
        lam = LAM[z]
        xx, yy, zz = dx(vx), dy(vy, seam[7], z), dz(V, 2, z)
        theta = lam * (xx + yy + zz)
        two = mu + mu
        S[XX, z] = S[XX, z] + (theta + two * xx)
        S[YY, z] = S[YY, z] + (theta + two * yy)
        S[ZZ, z] = S[ZZ, z] + (theta + two * zz)
    if XZ in fields:
        S[XZ, z] = S[XZ, z] + mu * (dz(V, 0, z) + dx(vz))
    if XY in fields:
        S[XY, z] = S[XY, z] + mu * (dy(vx, seam[6], z) + dx(vy))
    if YZ in fields:
        S[YZ, z] = S[YZ, z] + mu * (dz(V, 1, z) + dy(vz, seam[8], z))


def stress_band(band, new, BM, keep_xx=True):
    vx, vy, vz = new[6], new[7], new[8]
    lam, mu = BM[0], BM[1]
    xx, yy, zz = dx(vx), band_dy(vy), band_dz(vz)
    theta = lam * (xx + yy + zz)
    two = mu + mu
    if keep_xx:
        new[XX] = band[XX] + (theta + two * xx)
    new[YY] = band[YY] + (theta + two * yy)
    new[ZZ] = band[ZZ] + (theta + two * zz)
    new[XZ] = band[XZ] + mu * (band_dz(vx) + dx(vz))
    new[XY] = band[XY] + mu * (band_dy(vx) + dx(vy))
    new[YZ] = band[YZ] + mu * (band_dz(vy) + band_dy(vz))


def unpack_kernel(
    S_in, V_in, LAM_in, MU_in, BUOY_in, own_in, table, rb, ra,
    S, V, LAM, MU, BUOY, own, ta, tb, zone_tail,
):
    even_x = (lax.axis_index("gx") & 1) == 0
    even_y = (lax.axis_index("gy") & 1) == 0
    low = iota((8, CY), 0) < 4
    slot = iota((8, CY), 1) // HALO
    tail = slice(CX, RING)
    columns = [jnp.broadcast_to(row, (8, CY)) for row in spread_table(table)]

    def place(f, z, rows):
        if f < 6:
            S[f, z, tail, :] = rows
        elif f < 9:
            V[f - 6, z, tail, :] = rows
        else:
            zone_tail[z] = rows

    for f in range(WIDE):
        for q in range(NZ // 2):
            at = slice(WIDE_AT + 8 * (f * 4 + q), WIDE_AT + 8 * (f * 4 + q) + 8)
            after = jnp.where(even_x, ra[at], rb[at])
            before = jnp.where(even_x, rb[at], ra[at])
            place(f, 2 * q, jnp.where(low, after, before))
            place(f, 2 * q + 1, roll(jnp.where(low, before, after), 4, 0))
    sub = iota((8, CY), 0)
    for f in range(WIDE, FIELDS):
        for z in range(NZ):
            at = pl.ds((f - WIDE) * 24 + z, 8, stride=8)
            a, b = ra[at, :], rb[at, :]
            after, before = jnp.where(even_x, a, b), roll(jnp.where(even_x, b, a), 5, 0)
            place(f, z, jnp.where(sub < 3, after, jnp.where(sub >= 5, before, 0.0)))
    for z in range(NZ):
        ids = zone_tail[z].astype(jnp.int32)
        for column, ref in zip(columns, (LAM, MU, BUOY)):
            ref[z, tail, :] = take(column, ids)
    for p in range(PACKS):
        lasts = jnp.zeros((8, CY), F32)
        firsts = jnp.zeros((8, CY), F32)
        for s in range(4):
            f = 4 * p + s
            if f >= FIELDS:
                continue
            for z in range(NZ):
                rows = S[f, z, tail, :] if f < 6 else V[f - 6, z, tail, :] if f < 9 else zone_tail[z]
                turned = roll(rows, 16 * z + 4 * s + 4, 1)
                at = 4 * z + s
                lasts = jnp.where(slot == at, turned, lasts)
                firsts = jnp.where(slot == (at + 1) % 32, turned, firsts)
        own_band(own, p, tail, lasts, firsts)
        ta[p] = jnp.where(even_y, lasts, firsts)
        tb[p] = jnp.where(even_y, firsts, lasts)


def inner_kernel(S, V_in, MU, BUOY, V, token):
    velocity_planes(moving(range(0, 5), True), S, V, MU, BUOY, None, None)
    token[...] = jnp.zeros(token.shape, F32)


def cone_kernel(
    S_in, V_in, LAM, MU, BUOY, BF_in, BM_in, table, own, tcb, tca, building, block,
    S, V, BF, BM, BV, BW, shares,
):
    even_y = (lax.axis_index("gy") & 1) == 0
    lane8 = iota((8, CY), 1)
    sub8 = iota((8, CY), 0)
    for p in range(PACKS):
        left, right = jnp.where(even_y, tcb[p], tca[p]), jnp.where(even_y, tca[p], tcb[p])
        band_rows(BF, BM, own, table, left, right, p, slice(CX, RING))

    velocity_seams(moving(range(0, 5), True), V, BUOY, BF)
    velocity_band(BF, BW, BM, None)
    for c in range(3):
        BV[c] = BW[6 + c]
    seam = seams(BW, (6, 7, 8))
    for z in range(0, 4):
        stress_plane(z, seam, S, V, LAM, MU, (FLAT, STEEP)[z % 2])
    stress_band(BF, BW, BM, False)
    velocity_planes(moving(range(0, 3), True), S, V, MU, BUOY, BW, None)
    velocity_band(BW, BW, BM, None, (2,))
    stress_plane(1, seams(BW, (8,)), S, V, LAM, MU, (XZ, YZ))

    total = jnp.zeros((8, CY), F32)
    for c, f in enumerate((XZ, YZ)):
        for r in range(CX // BLOCK):
            row = jnp.sum(S[f, 1, 8 * r:8 * r + 8, :], axis=0, keepdims=True)
            total = jnp.where(sub8 == 4 * c + r, jnp.broadcast_to(row, (8, CY)), total)
    for shift in (1, 2, 4):
        total = total + roll(total, CY - shift, 1)
    total = total * (1.0 / (BLOCK * BLOCK))
    ids = jnp.broadcast_to(jnp.concatenate([block[0], block[0]], axis=1), (8, CY))
    cells = CY // BLOCK
    picked = take(total, (ids % cells) * BLOCK)
    mine = (sub8 % 4 == ids // cells) & (sub8 // 4 == lane8 // FP_DEV)
    values = jnp.sum(jnp.where(mine, picked, 0.0), axis=0, keepdims=True)
    names = jnp.concatenate([building[0], building[0]], axis=1).astype(F32)
    message = jnp.concatenate([values, names], axis=0)
    shares[...] = jnp.broadcast_to(message[None], shares.shape)


def upper_kernel(S_in, V_in, LAM, MU, BUOY, BF, BM, BV, BW_in, S, V, BW):
    velocity_planes(moving(range(0, 5), False) + every(range(5, 7)), S, V, MU, BUOY, BF, None)
    seam = {6 + c: value for c, value in seams(BV, range(3)).items()}
    for z in range(0, 6):
        stress_plane(z, seam, S, V, LAM, MU, ALL if z > 3 else (STEEP, FLAT)[z % 2])
    velocity_planes(moving(range(0, 3), False) + every(range(3, 5)), S, V, MU, BUOY, BW, None)
    vx, vy, vz = BV[0], BV[1], BV[2]
    xx, yy, zz = dx(vx), band_dy(vy), band_dz(vz)
    BW[XX] = BF[XX] + (BM[0] * (xx + yy + zz) + (BM[1] + BM[1]) * xx)
    velocity_band(BW, BW, BM, None, (0, 1))
    seam = seams(BW, (6, 7, 8))
    for z in range(0, 4):
        stress_plane(z, seam, S, V, LAM, MU, FLAT if z == 1 else ALL)


def lower_kernel(
    S_in, V_in, LAM, MU, BUOY, BF_in, BM, source, got, kept,
    S, V, BF, vel_out, stress_out, DRM, drm_in, sems,
):
    saves = []

    def save(ref, out, first, count):
        at = pl.ds(first, count)
        copy = pltpu.make_async_copy(ref.at[:, at, pl.ds(0, CX), :], out.at[:, at], sems.at[len(saves)])
        copy.start()
        saves.append(copy)

    save(V, vel_out, 0, 5)
    save(S, stress_out, 0, 4)
    low = iota((8, CY), 0) < 4
    lane8 = iota((8, CY), 1)
    quarter8 = (lane8 // 4) % 4
    deepest = lane8 >= 16 * (NZ - 1)

    mine = ((source[...] ^ lax.axis_index("gx")) & 1) == 0
    drm_in[...] = jnp.where(mine, kept[0], got[0])

    def wide(row):
        return jnp.broadcast_to(drm_in[row:row + 1, :], (8, CY))

    for s in range(STEPS):
        both = jnp.where(lane8 >= 96, wide(6 + s), roll(wide(CXC + 6 + s), 32, 1))
        for c in range(3):
            for q in range(RING // 8):
                if q < 4:
                    rows = jnp.where(low, wide(s * CXC + 2 * q), wide(s * CXC + 2 * q + 1))
                    base = c * CYC
                else:
                    rows = jnp.where(low, wide(s * CXC + c), wide(s * CXC + 3 + c))
                    base = 3 * CYC
                DRM[s, c, 0, 8 * q:8 * q + 8, :] = take(rows, base + lane8 // COARSE)
                inner = take(rows, base + jnp.where(quarter8 == 2, CYC - 1, 0))
                at = c * 10 + 2 * q + jnp.where(low, 0, 1) + jnp.where(quarter8 == 0, 96, 0)
                value = jnp.where((quarter8 & 1) == (quarter8 >> 1), take(both, at), inner)
                DRM[s, c, 1, 8 * q:8 * q + 8, :] = jnp.where(deepest, value, 0.0)

    def drm(step):
        return lambda c, k: DRM[step, c, k]

    velocity_planes(every(range(7, NZ)), S, V, MU, BUOY, BF, drm(0))
    velocity_band(BF, BF, BM, drm(0))
    seam = seams(BF, (6, 7, 8))
    for z in range(6, NZ):
        stress_plane(z, seam, S, V, LAM, MU, ALL)
    stress_band(BF, BF, BM)
    velocity_planes(every(range(5, NZ)), S, V, MU, BUOY, BF, drm(1))
    velocity_band(BF, BF, BM, drm(1))
    save(V, vel_out, 5, NZ - 5)
    seam = seams(BF, (6, 7, 8))
    for z in range(4, NZ):
        stress_plane(z, seam, S, V, LAM, MU, ALL)
        save(S, stress_out, z, 1)
    for copy in saves:
        copy.wait()


def sum_kernel(n, shares, out):
    half = n // 2
    n_high = BUILDINGS // CY
    low = iota((half, CY), 1) < FP_DEV
    values = shares[:, 0, :]
    names = shares[:, 1, :].astype(jnp.int32)
    names = jnp.where(low, names[:half], names[half:])
    high, names = names // CY, names % CY
    pieces = []
    for rest in (
        jnp.where(low, values[:half], roll(values[half:], FP_DEV, 1)),
        jnp.where(low, roll(values[:half], FP_DEV, 1), values[half:]),
    ):
        for _ in range(3):
            piece = rest.astype(jnp.bfloat16).astype(F32)
            rest = rest - piece
            pieces.append(piece)
    rows = iota((n_high, CY), 0)
    wanted = iota((CY, CY), 0)
    left, hot = [], []
    for k in range(half):
        here = jnp.broadcast_to(high[k:k + 1], (n_high, CY)) == rows
        parts = [jnp.where(here, jnp.broadcast_to(piece[k:k + 1], (n_high, CY)), 0.0) for piece in pieces]
        left.append(jnp.concatenate(parts, axis=0).astype(jnp.bfloat16))
        hot.append((jnp.broadcast_to(names[k:k + 1], (CY, CY)) == wanted).astype(F32).astype(jnp.bfloat16))
    acc = lax.dot_general(
        jnp.concatenate(left, axis=1), jnp.concatenate(hot, axis=1), (((1,), (1,)), ((), ())), preferred_element_type=F32,
    )
    sums = []
    for c in range(2):
        base = 3 * c * n_high
        sums.append(acc[base:base + n_high] + acc[base + n_high:base + 2 * n_high] + acc[base + 2 * n_high:base + 3 * n_high])
    for h in range(n_high):
        out[:, h * CY:(h + 1) * CY] = jnp.concatenate([sums[0][h:h + 1], sums[1][h:h + 1]], axis=0)


def pairs_near(n):
    return [(i, i ^ 1) for i in range(n)]


def pairs_far(n):
    return [(i, (i + 1) % n if i % 2 else (i - 1) % n) for i in range(n)]


def after(x, *done):
    return lax.optimization_barrier((x,) + done)[0]


def body(n_gx, n_gy, velocity, stress, zones, zone_table, regional, owner, building, block):
    n = n_gx * n_gy
    gx = lax.axis_index("gx")
    vmem = pl.BlockSpec(memory_space=pltpu.VMEM)
    hbm = pl.BlockSpec(memory_space=pltpu.HBM)
    anywhere = pl.BlockSpec(memory_space=pl.ANY)
    params = pltpu.CompilerParams(vmem_limit_bytes=VMEM_LIMIT)

    def shaped(*shape):
        return jax.ShapeDtypeStruct(shape, F32)

    def whole(shape, dtype):
        return jax.ShapeDtypeStruct(shape, dtype)

    s_ring = shaped(6, NZ, RING, CY)
    v_ring = shaped(3, NZ, RING, CY)
    m_ring = shaped(NZ, RING, CY)
    rows = shaped(ROWS, CY)
    cols = shaped(COLS, CY)
    from_hbm = [
        pltpu.with_memory_space_constraint(x, pltpu.HBM)
        for x in (velocity, stress, zones, regional, zone_table, building, block, owner)
    ]
    gxa, gxb, regional, zone_table, building, block, source = pl.pallas_call(
        functools.partial(rows_kernel, n_gy),
        out_shape=(
            rows, rows, whole(regional.shape, F32), whole(zone_table.shape, F32),
            whole(building.shape, jnp.int32), whole(block.shape, jnp.int32), whole((CHUNK, CY), jnp.int32),
        ),
        in_specs=[hbm] * 8,
        out_specs=(vmem,) * 7,
        scratch_shapes=[
            pltpu.VMEM((2, 9, NZ, 8, CY), F32),
            pltpu.VMEM((2, NZ, 8, CY), jnp.int32),
            pltpu.SMEM(owner.shape, jnp.int32),
            pltpu.SemaphoreType.DMA((11,)),
        ],
        compiler_params=params,
        name="pack_rows",
    )(*from_hbm)
    rb = lax.ppermute(gxb, "gx", pairs_far(n_gx))
    ra = lax.ppermute(gxa, "gx", pairs_near(n_gx))
    own = shaped(FIELDS, RING, CY)
    S, V, gya, gyb, own = pl.pallas_call(
        cols_kernel,
        out_shape=(s_ring, v_ring, cols, cols, own),
        in_specs=[vmem] * 3,
        out_specs=(vmem,) * 5,
        scratch_shapes=[pltpu.SemaphoreType.DMA((2,))],
        compiler_params=params,
        name="pack_columns",
    )(velocity, stress, zones)

    def across(x, width):
        return lax.ppermute(x, "gx", [(i, i ^ width) for i in range(n_gx)])

    half = shaped(n_gx // 2, CHUNK, CY)
    sent, kept = pl.pallas_call(
        functools.partial(slices_kernel, n_gx),
        out_shape=(half, half),
        in_specs=[vmem],
        out_specs=(vmem,) * 2,
        scratch_shapes=[pltpu.VMEM((n_gx * CHUNK, CY), F32)],
        compiler_params=params,
        name="slices",
    )(regional)
    width = 2
    while 4 * width < n_gx:
        count = sent.shape[0]
        part = shaped(count // 2, CHUNK, CY)
        sent, kept = pl.pallas_call(
            functools.partial(trade_kernel, width),
            out_shape=(part, part),
            in_specs=[vmem] * 3,
            out_specs=(vmem,) * 2,
            scratch_shapes=[pltpu.VMEM((count, CHUNK, CY), F32)],
            compiler_params=params,
            name="trade",
        )(across(sent, width), kept, source)
        width *= 2
    LAM, MU, BUOY, made = pl.pallas_call(
        material_kernel,
        out_shape=(m_ring,) * 3 + (shaped(8, CY),),
        in_specs=[vmem] * 2,
        out_specs=(vmem,) * 4,
        compiler_params=params,
        name="materials",
    )(zones, zone_table)
    message = shaped(COLS + 8, CY)
    quad, message_a, message_b = pl.pallas_call(
        functools.partial(ends_kernel, width),
        out_shape=(shaped(4, CHUNK, CY), message, message),
        in_specs=[vmem] * 5 + [anywhere],
        out_specs=(vmem,) * 3,
        compiler_params=params,
        name="ends",
    )(across(sent, width), kept, source, gya, gyb, made)
    cb = lax.ppermute(message_b, "gy", pairs_far(n_gy))
    ca = lax.ppermute(message_a, "gy", pairs_near(n_gy))
    ends = shaped(PACKS, 8, CY)
    S, V, LAM, MU, BUOY, own, ta, tb = pl.pallas_call(
        unpack_kernel,
        out_shape=(s_ring, v_ring, m_ring, m_ring, m_ring, shaped(FIELDS, RING, CY), ends, ends),
        in_specs=[vmem] * 9,
        out_specs=(vmem,) * 8,
        scratch_shapes=[pltpu.VMEM((NZ, 8, CY), F32)],
        input_output_aliases={k: k for k in range(6)},
        compiler_params=params,
        name="unpack",
    )(S, V, LAM, MU, BUOY, own, zone_table, rb, ra)
    tcb = lax.ppermute(tb, "gy", pairs_far(n_gy))
    tca = lax.ppermute(ta, "gy", pairs_near(n_gy))
    V, token = pl.pallas_call(
        inner_kernel,
        out_shape=(v_ring, shaped(8, CY)),
        in_specs=[vmem] * 4,
        out_specs=(vmem,) * 2,
        input_output_aliases={1: 0},
        compiler_params=params,
        name="inner",
    )(S, V, MU, BUOY)
    two = shaped(2, CHUNK, CY)
    band = shaped(3, RING, CY)
    width *= 2
    sent, kept, BF, BM = pl.pallas_call(
        functools.partial(edges_kernel, width),
        out_shape=(two, two, shaped(FIELDS, RING, CY), band),
        in_specs=[vmem] * 3 + [anywhere] + [vmem] * 2,
        out_specs=(vmem,) * 4,
        compiler_params=params,
        name="edges",
    )(quad, cb, ca, token, own, zone_table)
    S, V, BF, BM, BV, BW, shares = pl.pallas_call(
        cone_kernel,
        out_shape=(s_ring, v_ring, shaped(FIELDS, RING, CY), band, band, shaped(9, RING, CY), shaped(n, 2, CY)),
        in_specs=[vmem] * 13,
        out_specs=(vmem,) * 7,
        input_output_aliases={0: 0, 1: 1, 5: 2, 6: 3},
        compiler_params=params,
        name="cone",
    )(S, V, LAM, MU, BUOY, BF, BM, zone_table, own, tcb, tca, building, block)
    held = jnp.where(((source ^ gx) & width) == 0, kept, across(sent, width))
    odd = (gx & 1) != 0
    sent, kept = jnp.where(odd, held[0], held[1])[None], jnp.where(odd, held[1], held[0])[None]
    got = across(sent, 1)
    gathered = lax.all_to_all(shares, ("gx", "gy"), 0, 0)
    S, V, _ = pl.pallas_call(
        upper_kernel,
        out_shape=(s_ring, v_ring, shaped(9, RING, CY)),
        in_specs=[vmem] * 9,
        out_specs=(vmem,) * 3,
        input_output_aliases={0: 0, 1: 1, 8: 2},
        compiler_params=params,
        name="upper",
    )(S, V, LAM, MU, BUOY, BF, BM, BV, BW)
    shear = pl.pallas_call(
        functools.partial(sum_kernel, n),
        out_shape=shaped(2, BUILDINGS),
        in_specs=[vmem],
        out_specs=vmem,
        compiler_params=params,
        name="sum_by_building",
    )(gathered)
    _, _, _, vel_out, stress_out = pl.pallas_call(
        lower_kernel,
        out_shape=(s_ring, v_ring, shaped(FIELDS, RING, CY), shaped(*velocity.shape), shaped(*stress.shape)),
        in_specs=[vmem] * 10,
        out_specs=(vmem, vmem, vmem, hbm, hbm),
        scratch_shapes=[
            pltpu.VMEM((STEPS, 3, 2, RING, CY), F32),
            pltpu.VMEM((CHUNK, CY), F32),
            pltpu.SemaphoreType.DMA((NZ,)),
        ],
        input_output_aliases={0: 0, 1: 1, 5: 2},
        compiler_params=params,
        name="lower",
    )(S, V, LAM, MU, BUOY, BF, BM, source, got, kept)
    return vel_out, stress_out, shear


def solution(mesh):
    n_gx, n_gy = mesh.shape["gx"], mesh.shape["gy"]
    return jax.shard_map(
        functools.partial(body, n_gx, n_gy),
        mesh=mesh,
        in_specs=(
            P(None, None, "gx", "gy"),
            P(None, None, "gx", "gy"),
            P(None, "gx", "gy"),
            P(),
            P("gx", None, None, None, "gy"),
            P(),
            P("gx", "gy", None),
            P("gx", "gy", None),
        ),
        out_specs=(P(None, None, "gx", "gy"), P(None, None, "gx", "gy"), P()),
        check_vma=False,
    )
```
